32 devices in a mesh: gx: 8 (over z, y), gy: 4 (over x, core).
Axes of the slice: x: 2, y: 2, z: 4, core: 2. Of those that a mesh axis runs over, the one named last changes fastest.
Arguments:
- e_adj: float32 [3, 8, 512, 1024], P(None, None, 'gx', 'gy'), may hold values from -6 to 6
- h_adj: float32 [3, 8, 512, 1024], P(None, None, 'gx', 'gy'), may hold values from -6 to 6
- density: float32 [512, 1024], P('gx', 'gy'), may hold values from 0.05 to 0.95
- material: int32 [8, 512, 1024], P(None, 'gx', 'gy'), may hold values from 0 to 3
- eps_table: float32 [4], replicated, may hold values from 1 to 12
- dft_adj: float32 [4, 2, 3, 2, 512, 1024], P(None, None, None, None, 'gx', 'gy'), may hold values from -6 to 6
- dft_fwd: bfloat16 [4, 2, 3, 2, 512, 1024], P(None, None, None, None, 'gx', 'gy'), may hold values from -6 to 6
- tile_map: int32 [8, 16], P('gx', 'gy'), may hold values from 0 to 31, as said below
Outputs:
- e_out: float32 [3, 8, 512, 1024], P(None, None, 'gx', 'gy')
- h_out: float32 [3, 8, 512, 1024], P(None, None, 'gx', 'gy')
- param_grad: float32 [32, 4096], P(('gx', 'gy'))
The draws below stay inside these ranges and needn't reach their ends.
Inputs may be any that keep to these rules, and one draw needn't show every extreme that they name: `tile_map`: each of the 32 design parameters is named by exactly 4 tiles. Parameter p belongs to the device at position p // (32 / number of devices) in the gx-major order of devices.
All inputs are finite; a program needn't handle non-finite values.
Results may differ from the reference program's by a relative error of at most 0.0003.
Values sent between devices are 32-bit elements; how exact they have to be, the bound alone decides.
No kernel may reach another device: no remote copies, remote signals or barrier semaphores. Data moves between devices by JAX's collectives and lax.ppermute only.
A program may use at most 64 MiB of HBM per device.

```python
import math
import jax
import jax.numpy as jnp
from jax import lax

CX = 64
CY = 256
NZ = 8
PLANES = 2
ZLO = 3
STEPS = 2
FREQ = 4
PML = 12
MATS = 4
TILE = 64
REPEAT = 4
NX = 512
NY = 1024
PARAMS = 32


def draw_tile_map(key, part):
    count_gx = NX // CX
    count_gy = NY // CY
    tiles_x = CX // TILE
    tiles_y = CY // TILE
    per_device = tiles_x * tiles_y
    rows_each = per_device // REPEAT
    devices_all = count_gx * count_gy
    key_mag = jax.random.fold_in(key, 11)
    key_sign = jax.random.fold_in(key, 12)
    key_perm = jax.random.fold_in(key, 13)
    magnitude = jax.random.randint(key_mag, (), 2, devices_all // 2)
    signs = 2 * jax.random.randint(key_sign, (), 0, 2) - 1
    extra = (magnitude * signs).astype(jnp.int32)
    offsets = jnp.stack([jnp.zeros((), jnp.int32), jnp.ones((), jnp.int32), jnp.full((), devices_all // 2, jnp.int32), extra]).astype(jnp.int32)
    device_ids = jnp.arange(devices_all, dtype=jnp.int32)[:, None]
    slots = jnp.arange(per_device, dtype=jnp.int32)[None, :]
    chosen = jnp.take(offsets, slots % REPEAT)
    owner = (device_ids - chosen + 2 * devices_all) % devices_all
    params = (owner * rows_each + slots // REPEAT).astype(jnp.int32)
    perm_keys = jax.random.split(key_perm, devices_all)
    orders = jax.vmap(lambda one_key: jax.random.permutation(one_key, per_device))(perm_keys)
    mixed = jnp.take_along_axis(params, orders.astype(jnp.int32), axis=1)
    layout = mixed.reshape(count_gx, count_gy, tiles_x, tiles_y).transpose(0, 2, 1, 3)
    return layout.reshape(count_gx * tiles_x, count_gy * tiles_y).astype(jnp.int32)


def with_ends(array, own_key, low, high):
    longest = array.shape.index(max(array.shape))
    spots = []
    for shift in (0, 1):
        where = [jax.random.randint(jax.random.fold_in(own_key, axis), (), 0, length) for axis, length in enumerate(array.shape)]
        where[longest] = (where[longest] + shift) % array.shape[longest]
        spots.append(tuple(where))
    return array.at[spots[0]].set(low).at[spots[1]].set(high)


def shard_levels(stream_key, dims, pieces, least, largest):
    factor_of = 1.0
    for position, parts in pieces:
        draws = jax.random.uniform(jax.random.fold_in(jax.random.fold_in(stream_key, 6), position), (parts,), jnp.float32, least / len(pieces), largest / len(pieces))
        factor_of = factor_of * jnp.repeat(jnp.exp(draws), dims[position] // parts).reshape((-1,) + (1,) * (len(dims) - 1 - position))
    return factor_of


def noise(stream_key, extent, deviation, bound, pieces=(), kind=jnp.bfloat16):
    gain = shard_levels(stream_key, extent, pieces, -0.22, 0.18) if pieces else 1.0
    values = jax.random.normal(stream_key, extent, jnp.float32) * deviation * gain
    return jnp.minimum(jnp.maximum(values, -bound), bound).astype(kind)


def setup_inputs(seed: int = 0) -> dict:
    arg_keys = jax.random.split(jax.random.key(seed), 9)
    e_adj = noise(arg_keys[0], (3, NZ, NX, NY), 1.0, 6.0, ((2, 8), (3, 4)), jnp.float32)
    h_adj = noise(arg_keys[1], (3, NZ, NX, NY), 1.0, 6.0, ((2, 8), (3, 4)), jnp.float32)
    density = jnp.clip(0.05 + 0.9 * jax.random.uniform(arg_keys[2], (NX, NY), jnp.float32) ** shard_levels(arg_keys[2], (NX, NY), ((0, 8), (1, 4)), -0.2, 0.2), 0.05, 0.95)
    material = with_ends(jax.random.randint(arg_keys[3], (NZ, NX, NY), 0, MATS), jax.random.fold_in(arg_keys[3], 1), 0, MATS - 1).astype(jnp.int32)
    eps_table = jnp.clip(jnp.exp(jax.random.uniform(arg_keys[4], (MATS,), jnp.float32, math.log(1.0), math.log(12.0))), 1.0, 12.0)
    dft_adj = noise(arg_keys[5], (FREQ, 2, 3, PLANES, NX, NY), 1.0, 6.0, ((4, 8), (5, 4)), jnp.float32)
    dft_fwd = noise(arg_keys[6], (FREQ, 2, 3, PLANES, NX, NY), 1.0, 6.0, ((4, 8), (5, 4)))
    tile_map = draw_tile_map(jax.random.fold_in(arg_keys[8], 71), 0)
    return dict(e_adj=e_adj, h_adj=h_adj, density=density, material=material, eps_table=eps_table, dft_adj=dft_adj, dft_fwd=dft_fwd, tile_map=tile_map)


courant = 0.5
sigma_peak = 0.8
dft_weight = 0.5
sharpness = 4.0
threshold = 0.5
eps_low = 2.1
eps_high = 12.1
grad_scale = 0.01


def profile(places, total):
    depth = jnp.maximum(jnp.maximum(PML - places, places - (total - 1 - PML)), 0.0) / PML
    return depth * depth * depth


def smooth(grid_field):
    padded = jnp.pad(grid_field, 1)
    summed = padded[:-2] + 2.0 * padded[1:-1] + padded[2:]
    return (summed[:, :-2] + 2.0 * summed[:, 1:-1] + summed[:, 2:]) / 16.0


def step_next(values, border, dim_index):
    inner = lax.slice_in_dim(values, 1, values.shape[dim_index], axis=dim_index)
    return jnp.concatenate([inner, border], axis=dim_index) - values


def step_prev(values, border, dim_index):
    inner = lax.slice_in_dim(values, 0, values.shape[dim_index] - 1, axis=dim_index)
    return values - jnp.concatenate([border, inner], axis=dim_index)


def zero_rim(values, dim_index):
    return jnp.zeros_like(lax.slice_in_dim(values, 0, 1, axis=dim_index))


def curl_forward(elec_x, elec_y, elec_z, ahead_x, ahead_y):
    curl_x = step_next(elec_z, ahead_y[1], 2) - step_next(elec_y, zero_rim(elec_y, 0), 0)
    curl_y = step_next(elec_x, zero_rim(elec_x, 0), 0) - step_next(elec_z, ahead_x[1], 1)
    curl_z = step_next(elec_y, ahead_x[0], 1) - step_next(elec_x, ahead_y[0], 2)
    return curl_x, curl_y, curl_z


def curl_backward(mag_x, mag_y, mag_z, behind_x, behind_y):
    curl_x = step_prev(mag_z, behind_y[1], 2) - step_prev(mag_y, zero_rim(mag_y, 0), 0)
    curl_y = step_prev(mag_x, zero_rim(mag_x, 0), 0) - step_prev(mag_z, behind_x[1], 1)
    curl_z = step_prev(mag_y, behind_x[0], 1) - step_prev(mag_x, behind_y[0], 2)
    return curl_x, curl_y, curl_z


def accumulate(accum, elec_x, elec_y, elec_z, step_index):
    design = jnp.stack([elec_x, elec_y, elec_z])[:, ZLO:ZLO + PLANES]
    angular = 0.21 + 0.06 * jnp.arange(FREQ, dtype=jnp.float32)
    turned = angular * (step_index + 1)
    weights = jnp.stack([dft_weight * jnp.cos(turned), -dft_weight * jnp.sin(turned)], axis=1)
    return accum + weights[:, :, None, None, None, None] * design[None, None]


def reference(e_adj, h_adj, density, material, eps_table, dft_adj, dft_fwd, tile_map):
    sigma = sigma_peak * (profile(jnp.arange(NX, dtype=jnp.float32), NX)[:, None]
                          + profile(jnp.arange(NY, dtype=jnp.float32), NY)[None, :])
    half_sum = 1.0 + 0.5 * sigma
    damping = (1.0 - 0.5 * sigma) / half_sum
    coef_h = courant / half_sum
    filtered = smooth(density)
    bend_value = jnp.tanh(sharpness * (filtered - threshold))
    scale_sum = jnp.tanh(sharpness * threshold) + jnp.tanh(sharpness * (1.0 - threshold))
    projected = (jnp.tanh(sharpness * threshold) + bend_value) / scale_sum
    slope = sharpness * (1.0 - bend_value * bend_value) / scale_sum
    design_eps = eps_low + (eps_high - eps_low) * projected
    eps_grid = jnp.zeros(material.shape, jnp.float32)
    for material_id in range(MATS):
        eps_grid = jnp.where(material == material_id, eps_table[material_id], eps_grid)
    layer_ids = jnp.arange(NZ, dtype=jnp.int32)[:, None, None]
    inside = (layer_ids >= ZLO) & (layer_ids < ZLO + PLANES)
    eps_grid = jnp.where(inside, design_eps[None], eps_grid)
    coef_e = courant / (eps_grid * half_sum[None])
    elec_x, elec_y, elec_z = e_adj[0], e_adj[1], e_adj[2]
    mag_x, mag_y, mag_z = h_adj[0], h_adj[1], h_adj[2]
    border_x = jnp.zeros((2, NZ, 1, NY), jnp.float32)
    border_y = jnp.zeros((2, NZ, NX, 1), jnp.float32)
    accum = dft_adj
    for step_index in range(STEPS):
        curl_x, curl_y, curl_z = curl_forward(elec_x, elec_y, elec_z, border_x, border_y)
        mag_x = damping * mag_x - coef_h * curl_x
        mag_y = damping * mag_y - coef_h * curl_y
        mag_z = damping * mag_z - coef_h * curl_z
        curl_x, curl_y, curl_z = curl_backward(mag_x, mag_y, mag_z, border_x, border_y)
        elec_x = damping * elec_x + coef_e * curl_x
        elec_y = damping * elec_y + coef_e * curl_y
        elec_z = damping * elec_z + coef_e * curl_z
        accum = accumulate(accum, elec_x, elec_y, elec_z, step_index)
    forward = dft_fwd.astype(jnp.float32)
    intersection = jnp.sum(forward[:, 0] * accum[:, 0] - forward[:, 1] * accum[:, 1], axis=(0, 1, 2))
    local_grad = grad_scale * (eps_high - eps_low) * slope * intersection
    grad_cells = smooth(local_grad)
    tile_rows = grad_cells.reshape(NX // TILE, TILE, NY // TILE, TILE).transpose(0, 2, 1, 3).reshape(-1, TILE * TILE)
    param_grad = jax.ops.segment_sum(tile_rows, tile_map.reshape(-1), num_segments=PARAMS)
    return (jnp.stack([elec_x, elec_y, elec_z]), jnp.stack([mag_x, mag_y, mag_z]), param_grad)
```

```python
import math

import jax
import jax.numpy as jnp
from jax import lax
from jax.experimental import pallas as pl
from jax.experimental.pallas import tpu as pltpu
from jax.sharding import PartitionSpec as P

PLANES = 2
ZLO = 3
STEPS = 2
FREQ = 4
PML = 12
TILE = 64
REPEAT = 4

courant = 0.5
sigma_peak = 0.8
dft_weight = 0.5
sharpness = 4.0
threshold = 0.5
eps_low = 2.1
eps_high = 12.1
grad_scale = 0.01

F32 = jnp.float32
LANES = 128
SUB = 8
GROUP = 16
ANY = pl.BlockSpec(memory_space=pl.ANY)
VMEM = pl.BlockSpec(memory_space=pltpu.VMEM)
SMEM = pl.BlockSpec(memory_space=pltpu.SMEM)


def params(mib=40):
    return pltpu.CompilerParams(vmem_limit_bytes=mib * 2**20)


def struct(*shape, dtype=F32):
    return jax.ShapeDtypeStruct(shape, dtype)


def cost(flops, moved):
    return pl.CostEstimate(flops=int(flops), bytes_accessed=int(moved), transcendentals=0)


def iota(shape, dim):
    return lax.broadcasted_iota(jnp.int32, shape, dim)


def in_design(z):
    return ZLO <= z < ZLO + PLANES


def turn(values, shift, axis):
    size = values.shape[axis]
    shift %= size
    return values if shift == 0 else pltpu.roll(values, shift, axis)


def depth_cubed(places, total):
    depth = jnp.maximum(jnp.maximum(PML - places, places - (total - 1 - PML)), 0.0) / PML
    return depth * depth * depth


def edge_coefs(rows, cols, total_x, total_y, inside=None):
    sigma = sigma_peak * (depth_cubed(rows, total_x) + depth_cubed(cols, total_y))
    inverse = 1.0 / (1.0 + 0.5 * sigma)
    if inside is not None:
        inverse = jnp.where(inside, inverse, 0.0)
    return (1.0 - 0.5 * sigma) * inverse, courant * inverse, inverse


def within(rows, cols, total_x, total_y):
    return (rows >= 0) & (rows < total_x) & (cols >= 0) & (cols < total_y)


def table_inverse(table, shape):
    return [courant / jnp.full(shape, table[k], F32) for k in range(table.shape[0])]


def pick(index, choices):
    out = jnp.zeros_like(choices[0])
    for k, choice in enumerate(choices):
        out = jnp.where(index == k, choice, out)
    return out


def design_terms(filtered):
    high = math.tanh(sharpness * threshold)
    norm = high + math.tanh(sharpness * (1.0 - threshold))
    bend = jnp.tanh(sharpness * (filtered - threshold))
    eps = eps_low + (eps_high - eps_low) * ((high + bend) / norm)
    return courant / eps, sharpness * (1.0 - bend * bend) / norm


def blur(values):
    rows, cols = values.shape
    summed = turn(values, 1, 0) + 2.0 * values + turn(values, rows - 1, 0)
    return (turn(summed, 1, 1) + 2.0 * summed + turn(summed, cols - 1, 1)) / 16.0


def id_row(tile_map, tx, shape):
    lane = iota(shape, len(shape) - 1)
    out = jnp.zeros(shape, F32)
    for t in range(tile_map.shape[1]):
        out = jnp.where(lane // TILE == t, (tile_map[tx, t] + 1).astype(F32), out)
    return out


def faces(fields, planes_z):
    return len(fields) * planes_z


def edge_copies(e_ref, h_ref, m_ref, d_ref, eb, hb, mb, db, sems):
    size = d_ref.shape[0]
    copies = []
    for side, start in enumerate((0, size - SUB)):
        rows = pl.ds(start, SUB)
        copies += [
            pltpu.make_async_copy(e_ref.at[:, :, rows, :], eb.at[side], sems.at[4 * side]),
            pltpu.make_async_copy(h_ref.at[:, :, rows, :], hb.at[side], sems.at[4 * side + 1]),
            pltpu.make_async_copy(m_ref.at[:, rows, :], mb.at[side], sems.at[4 * side + 2]),
            pltpu.make_async_copy(d_ref.at[rows, :], db.at[side], sems.at[4 * side + 3]),
        ]
    for copy in copies:
        copy.start()
    for copy in copies:
        copy.wait()


def edge_scratch(planes_z, width_y):
    return [
        pltpu.VMEM((2, 3, planes_z, SUB, width_y), F32),
        pltpu.VMEM((2, 3, planes_z, SUB, width_y), F32),
        pltpu.VMEM((2, planes_z, SUB, width_y), jnp.int32),
        pltpu.VMEM((2, SUB, width_y), F32),
        pltpu.SemaphoreType.DMA((8,)),
    ]


def edge_tile(side, q, planes_z, eb, hb, mb, db, ids):
    field, z = divmod(q, planes_z)
    if field < 3:
        return eb[side, field, z]
    if field < 6:
        return hb[side, field - 3, z]
    if field == 6:
        return db[side] if in_design(z) else mb[side, z].astype(F32)
    return ids


def n_faces(planes_z):
    return 7 * planes_z + 1


def pack_x(e_ref, h_ref, m_ref, d_ref, map_ref, a_ref, b_ref, eb, hb, mb, db, sems):
    planes_z, _, width_y = m_ref.shape
    edge_copies(e_ref, h_ref, m_ref, d_ref, eb, hb, mb, db, sems)
    even = lax.axis_index("gx") % 2 == 0
    last = map_ref.shape[0] - 1
    sub = iota((SUB, width_y), 0)
    ids = [id_row(map_ref, 0, (SUB, width_y)), id_row(map_ref, last, (SUB, width_y))]
    for group in range(a_ref.shape[0]):
        low = jnp.zeros((SUB, width_y), F32)
        high = low
        for k in range(4):
            q = 4 * group + k
            if q >= n_faces(planes_z):
                break
            mask = sub // 2 == k
            tile = edge_tile(0, q, planes_z, eb, hb, mb, db, ids[0])
            low = jnp.where(mask, turn(tile, 2 * k, 0), low)
            tile = edge_tile(1, q, planes_z, eb, hb, mb, db, ids[1])
            high = jnp.where(mask, turn(tile, 2 * k - 6, 0), high)
        a_ref[group] = jnp.where(even, high, low)
        b_ref[group] = jnp.where(even, low, high)


def halo_rows(a_ref, b_ref, q, even):
    group, k = divmod(q, 4)
    a, b = a_ref[group], b_ref[group]
    below = jnp.where(even, b, a)
    above = jnp.where(even, a, b)
    return turn(below, -2 * k, 0), turn(above, -2 * k, 0)


def to_strip(values, z, acc):
    lane = iota((values.shape[0], LANES), 1) - z * GROUP
    half = GROUP // 2
    low = turn(values[:, :LANES], z * GROUP + 2, 1)
    high = turn(values[:, -LANES:], z * GROUP + half - (LANES - half + 2), 1)
    acc = jnp.where((lane >= 2) & (lane < half), low, acc)
    return jnp.where((lane >= half) & (lane < GROUP - 2), high, acc)


def build_strips(e_ref, h_ref, m_ref, d_ref, map_ref, s_ref):
    planes_z, width_x, width_y = m_ref.shape
    zero = jnp.zeros((width_x, LANES), F32)

    def body(c, _):
        for base, ref in ((0, e_ref), (3, h_ref)):
            acc = zero
            for z in range(planes_z):
                acc = to_strip(ref[c, z], z, acc)
            s_ref[base + c] = acc
        return 0

    lax.fori_loop(0, 3, body, 0)
    acc = zero
    for z in range(planes_z):
        acc = to_strip(d_ref[...] if in_design(z) else m_ref[z].astype(F32), z, acc)
    s_ref[6] = acc
    for tx in range(width_x // TILE):
        rows = pl.ds(tx * TILE, TILE)
        row = id_row(map_ref, tx, (TILE, width_y))
        s_ref[7, rows] = to_strip(row, 0, jnp.zeros((TILE, LANES), F32))


def pack_y(s_ref, xa_ref, xb_ref, t_ref, a_ref, b_ref):
    planes_z = LANES // GROUP
    width_x = s_ref.shape[1]
    width_y = xa_ref.shape[2]
    even_x = lax.axis_index("gx") % 2 == 0
    even_y = lax.axis_index("gy") % 2 == 0
    sub = iota((SUB, width_y), 0)
    tails = []
    for f in range(8):
        acc = jnp.zeros((SUB, LANES), F32)
        for z in range(planes_z if f < 7 else 1):
            below, above = halo_rows(xa_ref, xb_ref, f * planes_z + z, even_x)
            halo = jnp.where(sub < 2, above, jnp.where(sub >= 6, turn(below, 6, 0), 0.0))
            acc = to_strip(halo, z, acc)
        t_ref[f] = acc
        tails.append(acc)
    for start in range(0, width_x + SUB, SUB):
        lane = iota((SUB, LANES), 1) % GROUP
        low = jnp.zeros((SUB, LANES), F32)
        high = low
        for f in range(8):
            values = tails[f] if start == width_x else s_ref[f, pl.ds(start, SUB)]
            mask = lane // 2 == f
            low = jnp.where(mask, turn(values, 2 * f - 2, 1), low)
            high = jnp.where(mask, turn(values, 2 * f - (GROUP - 4), 1), high)
        a_ref[pl.ds(start, SUB)] = jnp.where(even_y, high, low)
        b_ref[pl.ds(start, SUB)] = jnp.where(even_y, low, high)


def transform(adj_ref, fwd_ref, s_ref, g_ref):
    rows, cols = s_ref.shape
    total = jnp.zeros((rows, cols), F32)
    for c in range(3):
        for p in range(PLANES):
            parts = [None] * STEPS
            for f in range(FREQ):
                real = fwd_ref[f, 0, c, p].astype(F32)
                imag = fwd_ref[f, 1, c, p].astype(F32)
                total = total + (real * adj_ref[f, 0, c, p] - imag * adj_ref[f, 1, c, p])
                for n in range(STEPS):
                    angle = (0.21 + 0.06 * f) * (n + 1)
                    term = (dft_weight * math.cos(angle)) * real + (
                        dft_weight * math.sin(angle)
                    ) * imag
                    parts[n] = term if parts[n] is None else parts[n] + term
            for n in range(STEPS):
                g_ref[n, c, p] = parts[n]
    s_ref[...] = total


def interior(e_ref, h_ref, m_ref, d_ref, table, e2_ref, h2_ref, e1_ref, sl_ref, damp, ch, ce):
    planes_z, width_x, width_y = m_ref.shape
    gx, gy = lax.axis_index("gx"), lax.axis_index("gy")
    total_x, total_y = width_x * lax.axis_size("gx"), width_y * lax.axis_size("gy")
    shape = (width_x, width_y)
    rows = (iota(shape, 0) + gx * width_x).astype(F32)
    cols = (iota(shape, 1) + gy * width_y).astype(F32)
    damping, coef_h, inverse = edge_coefs(rows, cols, total_x, total_y)
    damp[...] = damping
    ch[...] = coef_h
    design, slope = design_terms(blur(d_ref[...]))
    sl_ref[...] = slope
    choices = table_inverse(table, (SUB, LANES))
    choices = [jnp.tile(c, (1, width_y // LANES)) for c in choices]
    for z in range(planes_z):
        if in_design(z):
            ce[z] = design * inverse
    for start in range(0, width_x, SUB):
        inv = inverse[start : start + SUB]
        for z in range(planes_z):
            if not in_design(z):
                ce[z, pl.ds(start, SUB)] = pick(m_ref[z, pl.ds(start, SUB)], choices) * inv

    def mag(src_e, src_h, z, last):
        for start in range(0, width_x, SUB):
            here = pl.ds(start, SUB)

            def ahead(c, tile):
                if start + SUB < width_x:
                    return src_e[c, z, pl.ds(start + 1, SUB)]
                return turn(tile, SUB - 1, 0)

            ex, ey, ez = (src_e[c, z, here] for c in range(3))
            up_x = -ex if last else src_e[0, z + 1, here] - ex
            up_y = -ey if last else src_e[1, z + 1, here] - ey
            cx = (turn(ez, width_y - 1, 1) - ez) - up_y
            cy = up_x - (ahead(2, ez) - ez)
            cz = (ahead(1, ey) - ey) - (turn(ex, width_y - 1, 1) - ex)
            dm, cf = damp[here], ch[here]
            for c, curl in enumerate((cx, cy, cz)):
                h2_ref[c, z, here] = dm * src_h[c, z, here] - cf * curl

    def elec(src_e, z, first):
        for start in range(0, width_x, SUB):
            here = pl.ds(start, SUB)

            def behind(c, tile):
                if start:
                    return h2_ref[c, z, pl.ds(start - 1, SUB)]
                return turn(tile, 1, 0)

            hx, hy, hz = (h2_ref[c, z, here] for c in range(3))
            up_x = hx if first else hx - h2_ref[0, z - 1, here]
            up_y = hy if first else hy - h2_ref[1, z - 1, here]
            cx = (hz - turn(hz, 1, 1)) - up_y
            cy = up_x - (hz - behind(2, hz))
            cz = (hy - behind(1, hy)) - (hx - turn(hx, 1, 1))
            dm, cf = damp[here], ce[z, here]
            for c, curl in enumerate((cx, cy, cz)):
                e2_ref[c, z, here] = dm * src_e[c, z, here] + cf * curl

    def loop(lo, hi, f):
        lax.fori_loop(lo, hi, lambda z, _: (f(z), 0)[1], 0)

    for n in range(STEPS):
        src_e, src_h = (e_ref, h_ref) if n == 0 else (e2_ref, h2_ref)
        loop(0, planes_z - 1, lambda z: mag(src_e, src_h, z, False))
        mag(src_e, src_h, planes_z - 1, True)
        elec(src_e, 0, True)
        loop(1, planes_z, lambda z: elec(src_e, z, False))
        if n == 0:
            for c in range(3):
                for p in range(PLANES):
                    e1_ref[c, p] = e2_ref[c, ZLO + p]


def strips_x(
    e_ref, h_ref, m_ref, d_ref, table, xa_ref, xb_ref,
    e2_ref, h2_ref, e1_ref, sl_ref, eb, hb, mb, db, sems, xe, xh, ce,
):
    planes_z, width_x, width_y = m_ref.shape
    edge_copies(e_ref, h_ref, m_ref, d_ref, eb, hb, mb, db, sems)
    gx, gy = lax.axis_index("gx"), lax.axis_index("gy")
    total_x, total_y = width_x * lax.axis_size("gx"), width_y * lax.axis_size("gy")
    even = gx % 2 == 0
    shape = (SUB, width_y)
    sub = iota(shape, 0)
    cols = (iota(shape, 1) + gy * width_y).astype(F32)
    choices = [jnp.tile(c, (1, width_y // LANES)) for c in table_inverse(table, (SUB, LANES))]
    zero = jnp.zeros(shape, F32)
    damps, chs = [], []

    def strip(side, q):
        below, above = halo_rows(xa_ref, xb_ref, q, even)
        own = edge_tile(side, q, planes_z, eb, hb, mb, db, None)
        if side == 0:
            return jnp.where(sub < 2, below, turn(own, 2, 0))
        return jnp.where(sub >= 6, turn(above, 6, 0), turn(own, 6, 0))

    for side in range(2):
        rows = (sub + gx * width_x + (-2 if side == 0 else width_x - 6)).astype(F32)
        inside = within(rows, cols, total_x, total_y)
        damping, coef_h, inverse = edge_coefs(rows, cols, total_x, total_y, inside)
        damps.append(damping)
        chs.append(coef_h)
        for z in range(planes_z):
            for c in range(3):
                xe[side, c, z] = strip(side, c * planes_z + z)
                xh[side, c, z + 1] = strip(side, (3 + c) * planes_z + z)
        for c in range(3):
            xe[side, c, planes_z] = zero
            xh[side, c, 0] = zero
        design, slope = design_terms(blur(strip(side, 6 * planes_z + ZLO)))
        sl_ref[side] = turn(slope, 6 if side == 0 else 2, 0)
        for z in range(planes_z):
            if in_design(z):
                ce[side, z] = design * inverse
            else:
                ce[side, z] = pick(strip(side, 6 * planes_z + z), choices) * inverse

    def mag(z):
        for side in range(2):
            ex, ey, ez = (xe[side, c, z] for c in range(3))
            cx = (turn(ez, width_y - 1, 1) - ez) - (xe[side, 1, z + 1] - ey)
            cy = (xe[side, 0, z + 1] - ex) - (turn(ez, SUB - 1, 0) - ez)
            cz = (turn(ey, SUB - 1, 0) - ey) - (turn(ex, width_y - 1, 1) - ex)
            for c, curl in enumerate((cx, cy, cz)):
                xh[side, c, z + 1] = damps[side] * xh[side, c, z + 1] - chs[side] * curl

    def elec(z):
        for side in range(2):
            hx, hy, hz = (xh[side, c, z + 1] for c in range(3))
            cx = (hz - turn(hz, 1, 1)) - (hy - xh[side, 1, z])
            cy = (hx - xh[side, 0, z]) - (hz - turn(hz, 1, 0))
            cz = (hy - turn(hy, 1, 0)) - (hx - turn(hx, 1, 1))
            for c, curl in enumerate((cx, cy, cz)):
                xe[side, c, z] = damps[side] * xe[side, c, z] + ce[side, z] * curl

    def loop(f):
        lax.fori_loop(0, planes_z, lambda z, _: (f(z), 0)[1], 0)

    back = (6, 2)
    for n in range(STEPS):
        loop(mag)
        loop(elec)
        if n == 0:
            for side in range(2):
                for c in range(3):
                    for p in range(PLANES):
                        e1_ref[c, p, side] = turn(xe[side, c, ZLO + p], back[side], 0)

    def finish(z):
        for side in range(2):
            for c in range(3):
                e2_ref[c, z, side] = turn(xe[side, c, z], back[side], 0)
                h2_ref[c, z, side] = turn(xh[side, c, z + 1], back[side], 0)

    loop(finish)


def patch_rows(values, strip, start, width_x):
    sub = iota(values.shape, 0)
    if start == 0:
        values = jnp.where(sub < 2, strip[0], values)
    if start == width_x - SUB:
        values = jnp.where(sub >= 6, strip[1], values)
    return values


def patch_cols(values, strip, z):
    lane = iota((values.shape[0], LANES), 1)
    low = turn(strip, -(z * GROUP + 2), 1)
    high = turn(strip, LANES - 2 - (z * GROUP + GROUP - 4), 1)
    tiles = [values[:, k : k + LANES] for k in range(0, values.shape[1], LANES)]
    tiles[0] = jnp.where(lane < 2, low, tiles[0])
    tiles[-1] = jnp.where(lane >= LANES - 2, high, tiles[-1])
    return jnp.concatenate(tiles, axis=1)


def strips_y(width_x, width_y, s_ref, t_ref, ya_ref, yb_ref, table):
    gx, gy = lax.axis_index("gx"), lax.axis_index("gy")
    total_x, total_y = width_x * lax.axis_size("gx"), width_y * lax.axis_size("gy")
    planes_z = LANES // GROUP
    even = gy % 2 == 0
    size = width_x + SUB
    shape = (size, LANES)
    lane = iota(shape, 1)
    col = lane % GROUP
    plane = lane // GROUP
    from_low = jnp.where(even, yb_ref[...], ya_ref[...])
    from_high = jnp.where(even, ya_ref[...], yb_ref[...])

    def field(f):
        own = jnp.concatenate([s_ref[f], t_ref[f]], axis=0)
        own = jnp.where(col < 2, turn(from_low, -2 * f, 1), own)
        return jnp.where(col >= GROUP - 2, turn(from_high, GROUP - 2 - 2 * f, 1), own)

    row = iota(shape, 0)
    row = jnp.where(row >= width_x + 4, row - size, row)
    place = jnp.where(col < GROUP // 2, col - 2, col + (width_y - GROUP + 2))
    rows = (row + gx * width_x).astype(F32)
    cols = (place + gy * width_y).astype(F32)
    inside = within(rows, cols, total_x, total_y)
    damping, coef_h, inverse = edge_coefs(rows, cols, total_x, total_y, inside)
    source = field(6)
    design, slope = design_terms(blur(source))
    choices = [jnp.tile(c, (size // SUB, 1)) for c in table_inverse(table, (SUB, LANES))]
    layer = (plane >= ZLO) & (plane < ZLO + PLANES)
    coef_e = jnp.where(layer, design, pick(source, choices)) * inverse
    e = [field(c) for c in range(3)]
    h = [field(3 + c) for c in range(3)]
    top = plane == planes_z - 1
    bottom = plane == 0

    def dxf(v):
        return turn(v, size - 1, 0) - v

    def dyf(v):
        return turn(v, LANES - 1, 1) - v

    def dzf(v):
        return jnp.where(top, 0.0, turn(v, LANES - GROUP, 1)) - v

    def dxb(v):
        return v - turn(v, 1, 0)

    def dyb(v):
        return v - turn(v, 1, 1)

    def dzb(v):
        return v - jnp.where(bottom, 0.0, turn(v, GROUP, 1))

    steps = []
    for _ in range(STEPS):
        curl = (dyf(e[2]) - dzf(e[1]), dzf(e[0]) - dxf(e[2]), dxf(e[1]) - dyf(e[0]))
        h = [damping * v - coef_h * c for v, c in zip(h, curl)]
        curl = (dyb(h[2]) - dzb(h[1]), dzb(h[0]) - dxb(h[2]), dxb(h[1]) - dyb(h[0]))
        e = [damping * v + coef_e * c for v, c in zip(e, curl)]
        steps.append(e)
    return steps, h, slope, field(7)


def scalar_of(values, sub, lane):
    here = (iota(values.shape, 0) == sub) & (iota(values.shape, 1) == lane)
    return jnp.max(jnp.where(here, values, 0.0)).astype(jnp.int32)


def slot_of(param, rows_mine):
    gx, gy = lax.axis_index("gx"), lax.axis_index("gy")
    count_gx, count_gy = lax.axis_size("gx"), lax.axis_size("gy")
    owner = lax.div(param, jnp.int32(rows_mine))
    row = param - owner * rows_mine
    ox = lax.div(owner, jnp.int32(count_gy))
    oy = owner - ox * count_gy
    core = (oy ^ gy) & 1
    near = ((ox & 1) + 2 * (oy >> 1)) ^ ((gx & 1) + 2 * (gy >> 1))
    far = (ox >> 1) ^ (gx >> 1)
    return ((core * count_gy + near) * (count_gx // 2) + far) * rows_mine + row


def gradient(
    s_ref, t_ref, ya_ref, yb_ref, xa_ref, xb_ref, table, map_ref, e1_ref, e2_ref, xe1_ref, xe2_ref,
    sl_ref, xsl_ref, sum_ref, g_ref, buf_ref, ye_ref, yh_ref, ye1, lpad, vpad, gpad,
):
    width_x, width_y = sl_ref.shape
    planes_z = LANES // GROUP
    steps, h, slope_y, ids_y = strips_y(width_x, width_y, s_ref, t_ref, ya_ref, yb_ref, table)
    for c in range(3):
        ye_ref[c] = steps[-1][c]
        yh_ref[c] = h[c]
        ye1[c] = steps[0][c]
    ye1[3] = slope_y
    pad = 2 * SUB
    lpad[pl.ds(0, pad)] = jnp.zeros((pad, width_y), F32)
    lpad[pl.ds(pad + width_x, pad)] = jnp.zeros((pad, width_y), F32)
    buf_ref[...] = jnp.zeros(buf_ref.shape, F32)
    for start in range(0, width_x, SUB):
        here = pl.ds(start, SUB)
        total = sum_ref[here]
        for c in range(3):
            for p in range(PLANES):
                first = patch_rows(e1_ref[c, p, here], xe1_ref.at[c, p], start, width_x)
                first = patch_cols(first, ye1[c, here], ZLO + p)
                second = patch_rows(e2_ref[c, ZLO + p, here], xe2_ref.at[c, ZLO + p], start, width_x)
                second = patch_cols(second, ye_ref[c, here], ZLO + p)
                total = total + g_ref[0, c, p, here] * first + g_ref[1, c, p, here] * second
        slope = patch_rows(sl_ref[here], xsl_ref, start, width_x)
        slope = patch_cols(slope, ye1[3, here], ZLO)
        lpad[pl.ds(pad + start, SUB)] = (grad_scale * (eps_high - eps_low)) * slope * total
    lane = iota((SUB, width_y), 1)
    for start in range(SUB, pad + width_x + SUB, SUB):
        v = lpad[pl.ds(start - 1, SUB)] + 2.0 * lpad[pl.ds(start, SUB)] + lpad[pl.ds(start + 1, SUB)]
        v = v / 16.0
        left = jnp.where(lane == 0, 0.0, turn(v, 1, 1))
        right = jnp.where(lane == width_y - 1, 0.0, turn(v, width_y - 1, 1))
        g = left + 2.0 * v + right
        for u in range(width_y // LANES):
            vpad[u, pl.ds(start, SUB)] = v[:, u * LANES : (u + 1) * LANES]
            gpad[u, pl.ds(start, SUB)] = g[:, u * LANES : (u + 1) * LANES]

    half = LANES // 2
    lines = TILE // 2
    tiles_x, tiles_y = width_x // TILE, width_y // TILE
    devices = lax.axis_size("gx") * lax.axis_size("gy")
    rows_mine = buf_ref.shape[0] // devices
    lane = iota((lines, LANES), 1)
    lane8 = iota((SUB, LANES), 1)
    sub8 = iota((SUB, LANES), 0)

    def add_tile(param, values):
        slot = slot_of(param, rows_mine)
        buf_ref[slot] = buf_ref[slot] + values

    def add_rows(ident, start, values):
        slot = slot_of(jnp.maximum(ident - 1, 0), rows_mine)
        rows = pl.ds(start, SUB)
        buf_ref[slot, rows] = buf_ref[slot, rows] + jnp.where(ident > 0, values, 0.0)

    for tx in range(tiles_x):
        for u in range(width_y // LANES):
            even = gpad[u, pl.ds(pad + tx * TILE, lines, stride=2)]
            odd = gpad[u, pl.ds(pad + tx * TILE + 1, lines, stride=2)]
            add_tile(map_ref[tx, 2 * u], jnp.where(lane < half, even, turn(odd, half, 1)))
            add_tile(map_ref[tx, 2 * u + 1], jnp.where(lane < half, turn(even, half, 1), odd))
    even_x = lax.axis_index("gx") % 2 == 0
    below, above = halo_rows(xa_ref, xb_ref, 7 * planes_z, even_x)
    before, after = pl.ds(pad - SUB, SUB), pl.ds(pad + width_x, SUB)
    for t in range(tiles_y):
        u, odd = divmod(t, 2)
        top, low = gpad[u, before], gpad[u, after]
        top = top if odd else turn(top, half, 1)
        low = turn(low, half, 1) if odd else low
        keep = (sub8 == SUB - 1) & (lane8 >= half)
        add_rows(scalar_of(below, 0, t * TILE), lines - SUB, jnp.where(keep, top, 0.0))
        keep = (sub8 == 0) & (lane8 < half)
        add_rows(scalar_of(above, 0, t * TILE), 0, jnp.where(keep, low, 0.0))
    end = width_y // LANES - 1
    for tx in range(tiles_x):
        ids = ids_y[tx * TILE : tx * TILE + SUB]
        even, odd = (pl.ds(pad + tx * TILE + k, lines, stride=2) for k in (0, 1))
        left = jnp.where(lane == half - 1, turn(vpad[0, even], half - 1, 1), 0.0)
        left = jnp.where(lane == LANES - 1, turn(vpad[0, odd], LANES - 1, 1), left)
        right = jnp.where(lane == 0, turn(vpad[end, even], 1, 1), 0.0)
        right = jnp.where(lane == half, turn(vpad[end, odd], half + 1, 1), right)
        for column, values in ((0, left), (GROUP - 1, right)):
            ident = scalar_of(ids, 0, column)
            add_tile(jnp.maximum(ident - 1, 0), jnp.where(ident > 0, values, 0.0))
    tail = ids_y[width_x : width_x + SUB]
    corners = (
        (SUB - 1, 0, before, 0, lines - SUB, LANES - 1),
        (SUB - 1, GROUP - 1, before, end, lines - SUB, half),
        (0, 0, after, 0, 0, half - 1),
        (0, GROUP - 1, after, end, 0, 0),
    )
    for sub, column, rows, u, start, target in corners:
        source = LANES - 1 if u == end and column else 0
        keep = (sub8 == sub) & (lane8 == target)
        values = jnp.where(keep, turn(vpad[u, rows], target - source, 1), 0.0)
        add_rows(scalar_of(tail, sub, column), start, values)


def merge(e_ref, h_ref, xe_ref, xh_ref, ye_ref, yh_ref, eo_ref, ho_ref):
    _, planes_z, width_x, _ = e_ref.shape
    for src, xs, ys, out in ((e_ref, xe_ref, ye_ref, eo_ref), (h_ref, xh_ref, yh_ref, ho_ref)):
        for z in range(planes_z):
            for start in range(0, width_x, SUB):
                here = pl.ds(start, SUB)
                values = patch_rows(src[0, z, here], xs.at[0, z], start, width_x)
                out[0, z, here] = patch_cols(values, ys[0, here], z)


def first_sum(parts, buf_ref, got_ref, *outs):
    size = outs[0].shape[0]
    for k in range(parts):
        rows = pl.ds(k * size, size)
        outs[k][...] = buf_ref[rows] + got_ref[rows]


def second_sum(parts, rows_mine, *refs):
    ins, outs = refs[:parts], refs[parts:]
    for k, out in enumerate(outs):
        rows = pl.ds(k * rows_mine, rows_mine)
        out[...] = sum(ref[rows] for ref in ins[1:]) + ins[0][rows]


def pair(block, partner):
    count_gx, count_gy = lax.axis_size("gx"), lax.axis_size("gy")
    route = []
    for i in range(count_gx):
        for j in range(count_gy):
            a, b = partner(i, j)
            if 0 <= a < count_gx and 0 <= b < count_gy:
                route.append((i * count_gy + j, a * count_gy + b))
    return lax.ppermute(block, ("gx", "gy"), route)


def on_device(e_adj, h_adj, density, material, eps_table, dft_adj, dft_fwd, tile_map):
    planes_z, width_x, width_y = material.shape
    count_gx, count_gy = lax.axis_size("gx"), lax.axis_size("gy")
    block = 4 * width_x * width_y
    groups = -(-n_faces(planes_z) // 4)
    face = struct(groups, SUB, width_y)
    xa, xb = pl.pallas_call(
        pack_x,
        out_shape=(face, face),
        in_specs=[ANY, ANY, ANY, ANY, SMEM],
        out_specs=(VMEM, VMEM),
        scratch_shapes=edge_scratch(planes_z, width_y),
        compiler_params=params(),
        name="pack_x",
    )(e_adj, h_adj, material, density, tile_map)
    xa = pair(xa, lambda i, j: (i ^ 1, j))
    xb = pair(xb, lambda i, j: (((i + 1) ^ 1) - 1, j))

    rows = 2 * SUB
    moved = struct(width_x, width_y), struct(STEPS, 3, PLANES, width_x, width_y)
    base, weight = pl.pallas_call(
        transform,
        grid=(width_x // rows,),
        out_shape=moved,
        in_specs=[pl.BlockSpec((FREQ, 2, 3, PLANES, rows, width_y), lambda i: (0, 0, 0, 0, i, 0))] * 2,
        out_specs=(
            pl.BlockSpec((rows, width_y), lambda i: (i, 0)),
            pl.BlockSpec((STEPS, 3, PLANES, rows, width_y), lambda i: (0, 0, 0, i, 0)),
        ),
        compiler_params=params(),
        cost_estimate=cost(48 * 8 * width_x * width_y, 85 * block),
        name="transform",
    )(dft_adj, dft_fwd)
    strip = pl.pallas_call(
        build_strips,
        out_shape=struct(8, width_x, LANES),
        in_specs=[VMEM] * 4 + [SMEM],
        out_specs=VMEM,
        compiler_params=params(),
        cost_estimate=cost(48 * 4 * width_x * width_y, 60 * block),
        name="build_strips",
    )(e_adj, h_adj, material, density, tile_map)
    e2, h2, e1, slope = pl.pallas_call(
        interior,
        out_shape=(
            struct(3, planes_z, width_x, width_y),
            struct(3, planes_z, width_x, width_y),
            struct(3, PLANES, width_x, width_y),
            struct(width_x, width_y),
        ),
        in_specs=[VMEM] * 4 + [SMEM],
        out_specs=(VMEM,) * 4,
        scratch_shapes=[
            pltpu.VMEM((width_x, width_y), F32),
            pltpu.VMEM((width_x, width_y), F32),
            pltpu.VMEM((planes_z, width_x, width_y), F32),
        ],
        compiler_params=params(),
        cost_estimate=cost(100 * planes_z * width_x * width_y, 110 * block),
        name="interior",
    )(e_adj, h_adj, material, density, eps_table)

    tails, ya, yb = pl.pallas_call(
        pack_y,
        out_shape=(struct(8, SUB, LANES),) + (struct(width_x + SUB, LANES),) * 2,
        in_specs=[VMEM] * 3,
        out_specs=(VMEM,) * 3,
        compiler_params=params(),
        name="pack_y",
    )(strip, xa, xb)
    ya = pair(ya, lambda i, j: (i, j ^ 1))
    yb = pair(yb, lambda i, j: (i, ((j + 1) ^ 1) - 1))
    xe2, xh2, xe1, xslope = pl.pallas_call(
        strips_x,
        out_shape=(
            struct(3, planes_z, 2, SUB, width_y),
            struct(3, planes_z, 2, SUB, width_y),
            struct(3, PLANES, 2, SUB, width_y),
            struct(2, SUB, width_y),
        ),
        in_specs=[ANY, ANY, ANY, ANY, SMEM, VMEM, VMEM],
        out_specs=(VMEM,) * 4,
        scratch_shapes=edge_scratch(planes_z, width_y)
        + [
            pltpu.VMEM((2, 3, planes_z + 1, SUB, width_y), F32),
            pltpu.VMEM((2, 3, planes_z + 1, SUB, width_y), F32),
            pltpu.VMEM((2, planes_z, SUB, width_y), F32),
        ],
        compiler_params=params(),
        cost_estimate=cost(30 * planes_z * width_x * width_y, 30 * block),
        name="strips_x",
    )(e_adj, h_adj, material, density, eps_table, xa, xb)

    devices = count_gx * count_gy
    rows_mine = (width_x // TILE) * (width_y // TILE) // REPEAT
    lines = TILE // 2
    padded = width_x + 4 * SUB
    buf, ye2, yh2 = pl.pallas_call(
        gradient,
        out_shape=(struct(devices * rows_mine, lines, LANES),)
        + (struct(3, width_x + SUB, LANES),) * 2,
        in_specs=[VMEM] * 6 + [SMEM] * 2 + [VMEM] * 8,
        out_specs=(VMEM,) * 3,
        scratch_shapes=[
            pltpu.VMEM((4, width_x + SUB, LANES), F32),
            pltpu.VMEM((padded, width_y), F32),
            pltpu.VMEM((width_y // LANES, padded, LANES), F32),
            pltpu.VMEM((width_y // LANES, padded, LANES), F32),
        ],
        compiler_params=params(),
        cost_estimate=cost(60 * width_x * width_y, 30 * block),
        name="gradient",
    )(strip, tails, ya, yb, xa, xb, eps_table, tile_map, e1, e2, xe1, xe2, slope, xslope, base, weight)

    half = devices * rows_mine // 2
    far = count_gx // 2
    got = pair(buf[half:], lambda i, j: (i, j ^ 1))
    parts = pl.pallas_call(
        lambda *refs: first_sum(count_gy, *refs),
        out_shape=(struct(far * rows_mine, lines, LANES),) * count_gy,
        in_specs=[VMEM] * 2,
        out_specs=(VMEM,) * count_gy,
        compiler_params=params(),
        name="first_sum",
    )(buf, got)
    parts = [parts[0]] + [
        pair(parts[k], lambda i, j: (i ^ (k & 1), j ^ (k >> 1 << 1))) for k in range(1, count_gy)
    ]
    parts = pl.pallas_call(
        lambda *refs: second_sum(count_gy, rows_mine, *refs),
        out_shape=(struct(rows_mine, lines, LANES),) * far,
        in_specs=[VMEM] * count_gy,
        out_specs=(VMEM,) * far,
        compiler_params=params(),
        name="second_sum",
    )(*parts)
    parts = [parts[0]] + [pair(parts[k], lambda i, j: (i ^ (k << 1), j)) for k in range(1, far)]
    param_grad = sum(parts[1:], parts[0]).reshape(rows_mine, TILE * TILE)

    whole = pl.BlockSpec((1, planes_z, width_x, width_y), lambda c: (c, 0, 0, 0))
    edge = pl.BlockSpec((1, planes_z, 2, SUB, width_y), lambda c: (c, 0, 0, 0, 0))
    side = pl.BlockSpec((1, width_x + SUB, LANES), lambda c: (c, 0, 0))
    e_out, h_out = pl.pallas_call(
        merge,
        grid=(3,),
        out_shape=(struct(3, planes_z, width_x, width_y),) * 2,
        in_specs=[whole, whole, edge, edge, side, side],
        out_specs=(whole, whole),
        compiler_params=params(),
        cost_estimate=cost(48 * 4 * width_x * width_y, 110 * block),
        name="merge",
    )(e2, h2, xe2, xh2, ye2, yh2)
    return e_out, h_out, param_grad


def solution(mesh):
    in_specs = (
        P(None, None, "gx", "gy"),
        P(None, None, "gx", "gy"),
        P("gx", "gy"),
        P(None, "gx", "gy"),
        P(),
        P(None, None, None, None, "gx", "gy"),
        P(None, None, None, None, "gx", "gy"),
        P("gx", "gy"),
    )
    out_specs = (P(None, None, "gx", "gy"), P(None, None, "gx", "gy"), P(("gx", "gy"), None))
    return jax.shard_map(
        on_device, mesh=mesh, in_specs=in_specs, out_specs=out_specs, check_vma=False
    )
```

```python
import math

import jax
import jax.numpy as jnp
from jax import lax
from jax.experimental import pallas as pl
from jax.experimental.pallas import tpu as pltpu
from jax.sharding import PartitionSpec as P

PLANES = 2
ZLO = 3
STEPS = 2
FREQ = 4
PML = 12
TILE = 64
REPEAT = 4

courant = 0.5
sigma_peak = 0.8
dft_weight = 0.5
sharpness = 4.0
threshold = 0.5
eps_low = 2.1
eps_high = 12.1
grad_scale = 0.01

F32 = jnp.float32
LANES = 128
SUB = 8
GROUP = 16
ANY = pl.BlockSpec(memory_space=pl.ANY)
HBM = pl.BlockSpec(memory_space=pltpu.HBM)
VMEM = pl.BlockSpec(memory_space=pltpu.VMEM)
SMEM = pl.BlockSpec(memory_space=pltpu.SMEM)


def params(size=40 * 2**20):
    return pltpu.CompilerParams(vmem_limit_bytes=size)


def struct(*shape, dtype=F32):
    return jax.ShapeDtypeStruct(shape, dtype)


def cost(flops, moved):
    return pl.CostEstimate(flops=int(flops), bytes_accessed=int(moved), transcendentals=0)


def iota(shape, dim):
    return lax.broadcasted_iota(jnp.int32, shape, dim)


def in_design(z):
    return ZLO <= z < ZLO + PLANES


def turn(values, shift, axis):
    size = values.shape[axis]
    shift %= size
    return values if shift == 0 else pltpu.roll(values, shift, axis)


def depth_cubed(places, total):
    depth = jnp.maximum(jnp.maximum(PML - places, places - (total - 1 - PML)), 0.0) / PML
    return depth * depth * depth


def edge_coefs(rows, cols, total_x, total_y, inside=None):
    sigma = sigma_peak * (depth_cubed(rows, total_x) + depth_cubed(cols, total_y))
    inverse = 1.0 / (1.0 + 0.5 * sigma)
    if inside is not None:
        inverse = jnp.where(inside, inverse, 0.0)
    return (1.0 - 0.5 * sigma) * inverse, courant * inverse, inverse


def within(rows, cols, total_x, total_y):
    return (rows >= 0) & (rows < total_x) & (cols >= 0) & (cols < total_y)


def table_inverse(table, shape):
    return [courant / jnp.full(shape, table[k], F32) for k in range(table.shape[0])]


def pick(index, choices):
    out = jnp.zeros_like(choices[0])
    for k, choice in enumerate(choices):
        out = jnp.where(index == k, choice, out)
    return out


def design_terms(filtered):
    high = math.tanh(sharpness * threshold)
    norm = high + math.tanh(sharpness * (1.0 - threshold))
    bend = jnp.tanh(sharpness * (filtered - threshold))
    eps = eps_low + (eps_high - eps_low) * ((high + bend) / norm)
    return courant / eps, sharpness * (1.0 - bend * bend) / norm


def blur(values):
    rows, cols = values.shape
    summed = turn(values, 1, 0) + 2.0 * values + turn(values, rows - 1, 0)
    return (turn(summed, 1, 1) + 2.0 * summed + turn(summed, cols - 1, 1)) / 16.0


def id_row(tile_map, tx, shape):
    lane = iota(shape, len(shape) - 1)
    out = jnp.zeros(shape, F32)
    for t in range(tile_map.shape[1]):
        out = jnp.where(lane // TILE == t, (tile_map[tx, t] + 1).astype(F32), out)
    return out


def n_faces(planes_z):
    return 7 * planes_z + 1


def edge_tile(q, start, e_ref, h_ref, m_ref, d_ref, ids=None):
    planes_z = m_ref.shape[0]
    field, z = divmod(q, planes_z)
    rows = pl.ds(start, SUB)
    if field < 3:
        return e_ref[field, z, rows]
    if field < 6:
        return h_ref[field - 3, z, rows]
    if field > 6:
        return ids
    return d_ref[rows] if in_design(z) else m_ref[z, rows].astype(F32)


def pack_x(e_in, h_in, m_in, d_in, map_in, a_ref, b_ref, eb, hb, mb, db, map_ref, sems):
    planes_z, size, width_y = m_in.shape
    fields = ((e_in, eb), (h_in, hb), (m_in, mb))
    copies = []
    for k, start in enumerate((0, size - SUB)):
        here, there = pl.ds(start, SUB), pl.ds(k * SUB, SUB)
        for n, (src, dst) in enumerate(fields):
            source = src.at[:, here] if n == 2 else src.at[:, :, here]
            target = dst.at[:, there] if n == 2 else dst.at[:, :, there]
            copies.append(pltpu.make_async_copy(source, target, sems.at[4 * k + n]))
        copies.append(pltpu.make_async_copy(d_in.at[here], db.at[there], sems.at[4 * k + 3]))
    copies.append(pltpu.make_async_copy(map_in, map_ref, sems.at[8]))
    for copy in copies:
        copy.start()
    even = lax.axis_index("gx") % 2 == 0
    sub = iota((SUB, width_y), 0)
    for copy in copies:
        copy.wait()
    for group in range(a_ref.shape[0]):
        low = jnp.zeros((SUB, width_y), F32)
        high = low
        for k in range(4):
            q = 4 * group + k
            if q >= n_faces(planes_z):
                break
            ids = [None, None]
            if q == n_faces(planes_z) - 1:
                ids = [id_row(map_ref, tx, (SUB, width_y)) for tx in (0, map_ref.shape[0] - 1)]
            tiles = [edge_tile(q, n * SUB, eb, hb, mb, db, ids[n]) for n in range(2)]
            low = jnp.where(sub // 2 == k, turn(tiles[0], 2 * k, 0), low)
            high = jnp.where(sub // 2 == k, turn(tiles[1], 2 * k - 6, 0), high)
        a_ref[group] = jnp.where(even, high, low)
        b_ref[group] = jnp.where(even, low, high)


def halo_rows(a_ref, b_ref, q, even):
    group, k = divmod(q, 4)
    a, b = a_ref[group], b_ref[group]
    below = jnp.where(even, b, a)
    above = jnp.where(even, a, b)
    return turn(below, -2 * k, 0), turn(above, -2 * k, 0)


def to_strip(values, z, acc):
    lane = iota((values.shape[0], LANES), 1) - z * GROUP
    half = GROUP // 2
    low = turn(values[:, :LANES], z * GROUP + 2, 1)
    high = turn(values[:, -LANES:], z * GROUP + half - (LANES - half + 2), 1)
    acc = jnp.where((lane >= 2) & (lane < half), low, acc)
    return jnp.where((lane >= half) & (lane < GROUP - 2), high, acc)


def build_strips(e_ref, h_ref, m_ref, d_ref, map_ref, s_ref):
    planes_z, width_x, width_y = m_ref.shape
    zero = jnp.zeros((width_x, LANES), F32)

    def body(c, _):
        for base, ref in ((0, e_ref), (3, h_ref)):
            acc = zero
            for z in range(planes_z):
                acc = to_strip(ref[c, z], z, acc)
            s_ref[base + c] = acc
        return 0

    lax.fori_loop(0, 3, body, 0)
    acc = zero
    for z in range(planes_z):
        acc = to_strip(d_ref[...] if in_design(z) else m_ref[z].astype(F32), z, acc)
    s_ref[6] = acc
    for tx in range(width_x // TILE):
        rows = pl.ds(tx * TILE, TILE)
        row = id_row(map_ref, tx, (TILE, width_y))
        s_ref[7, rows] = to_strip(row, 0, jnp.zeros((TILE, LANES), F32))


def pack_y(s_ref, xa_ref, xb_ref, _after, t_ref, a_ref, b_ref):
    planes_z = LANES // GROUP
    width_x = s_ref.shape[1]
    width_y = xa_ref.shape[2]
    even_x = lax.axis_index("gx") % 2 == 0
    even_y = lax.axis_index("gy") % 2 == 0
    sub = iota((SUB, width_y), 0)
    tails = []
    for f in range(8):
        acc = jnp.zeros((SUB, LANES), F32)
        for z in range(planes_z if f < 7 else 1):
            below, above = halo_rows(xa_ref, xb_ref, f * planes_z + z, even_x)
            halo = jnp.where(sub < 2, above, jnp.where(sub >= 6, turn(below, 6, 0), 0.0))
            acc = to_strip(halo, z, acc)
        t_ref[f] = acc
        tails.append(acc)
    for start in range(0, width_x + SUB, SUB):
        lane = iota((SUB, LANES), 1) % GROUP
        low = jnp.zeros((SUB, LANES), F32)
        high = low
        for f in range(8):
            values = tails[f] if start == width_x else s_ref[f, pl.ds(start, SUB)]
            mask = lane // 2 == f
            low = jnp.where(mask, turn(values, 2 * f - 2, 1), low)
            high = jnp.where(mask, turn(values, 2 * f - (GROUP - 4), 1), high)
        a_ref[pl.ds(start, SUB)] = jnp.where(even_y, high, low)
        b_ref[pl.ds(start, SUB)] = jnp.where(even_y, low, high)


def transform(adj_ref, fwd_ref, s_ref, g_ref):
    rows, cols = s_ref.shape
    total = jnp.zeros((rows, cols), F32)
    for c in range(3):
        for p in range(PLANES):
            parts = [None] * STEPS
            for f in range(FREQ):
                real = fwd_ref[f, 0, c, p].astype(F32)
                imag = fwd_ref[f, 1, c, p].astype(F32)
                total = total + (real * adj_ref[f, 0, c, p] - imag * adj_ref[f, 1, c, p])
                for n in range(STEPS):
                    angle = (0.21 + 0.06 * f) * (n + 1)
                    term = (dft_weight * math.cos(angle)) * real + (
                        dft_weight * math.sin(angle)
                    ) * imag
                    parts[n] = term if parts[n] is None else parts[n] + term
            for n in range(STEPS):
                g_ref[n, c, p] = parts[n]
    s_ref[...] = total


LO = ZLO - STEPS
HI = ZLO + PLANES + STEPS - 1


def update_mag(e, e_up, h, out, damp, ch):
    width_x, width_y = damp.shape
    for start in range(0, width_x, SUB):
        here = pl.ds(start, SUB)

        def ahead(c, tile):
            if start + SUB < width_x:
                return e(c)[pl.ds(start + 1, SUB)]
            return turn(tile, SUB - 1, 0)

        ex, ey, ez = (e(c)[here] for c in range(3))
        up_x = e_up(0)[here] - ex if e_up else -ex
        up_y = e_up(1)[here] - ey if e_up else -ey
        cx = (turn(ez, width_y - 1, 1) - ez) - up_y
        cy = up_x - (ahead(2, ez) - ez)
        cz = (ahead(1, ey) - ey) - (turn(ex, width_y - 1, 1) - ex)
        dm, cf = damp[here], ch[here]
        for c, curl in enumerate((cx, cy, cz)):
            out(c)[here] = dm * h(c)[here] - cf * curl


def update_elec(h, h_down, e, out, damp, ce):
    width_x, width_y = damp.shape
    for start in range(0, width_x, SUB):
        here = pl.ds(start, SUB)

        def behind(c, tile):
            return h(c)[pl.ds(start - 1, SUB)] if start else turn(tile, 1, 0)

        hx, hy, hz = (h(c)[here] for c in range(3))
        up_x = hx - h_down(0)[here] if h_down else hx
        up_y = hy - h_down(1)[here] if h_down else hy
        cx = (hz - turn(hz, 1, 1)) - up_y
        cy = up_x - (hz - behind(2, hz))
        cz = (hy - behind(1, hy)) - (hx - turn(hx, 1, 1))
        dm, cf = damp[here], ce[here]
        for c, curl in enumerate((cx, cy, cz)):
            out(c)[here] = dm * e(c)[here] + cf * curl


def at(ref, z):
    return lambda c: ref.at[c, z]


def fill_ce(ce, k, z, m_ref, choices, ch):
    for start in range(0, ch.shape[0], SUB):
        here = pl.ds(start, SUB)
        ce[k, here] = pick(m_ref[z, here], choices) * (ch[here] * (1.0 / courant))


def interior_first(e_ref, h_ref, m_ref, d_ref, table, em, hm, e1_ref, sl_ref, damp, ch, ce):
    planes_z, width_x, width_y = m_ref.shape
    gx, gy = lax.axis_index("gx"), lax.axis_index("gy")
    total_x, total_y = width_x * lax.axis_size("gx"), width_y * lax.axis_size("gy")
    shape = (width_x, width_y)
    rows = (iota(shape, 0) + gx * width_x).astype(F32)
    cols = (iota(shape, 1) + gy * width_y).astype(F32)
    damping, coef_h, inverse = edge_coefs(rows, cols, total_x, total_y)
    damp[...] = damping
    ch[...] = coef_h
    design, slope = design_terms(blur(d_ref[...]))
    sl_ref[...] = slope
    choices = [jnp.tile(c, (1, width_y // LANES)) for c in table_inverse(table, (SUB, LANES))]
    for z in range(LO, HI):
        if in_design(z):
            ce[z - LO] = design * inverse
        elif z > LO:
            fill_ce(ce, z - LO, z, m_ref, choices, ch)

    def e(z):
        return at(em, z - LO)

    def h(z):
        return at(hm, z - LO)

    for z in range(LO, HI):
        update_mag(at(e_ref, z), at(e_ref, z + 1), at(h_ref, z), h(z), damp, ch)
    for z in range(LO + 1, HI):
        update_elec(h(z), h(z - 1), at(e_ref, z), e(z), damp, ce.at[z - LO])
    for c in range(3):
        for p in range(PLANES):
            e1_ref[c, p] = em[c, ZLO + p - LO]
    for z in range(LO + 1, HI - 1):
        update_mag(e(z), e(z + 1), h(z), h(z), damp, ch)
    for z in range(LO + 2, HI - 1):
        update_elec(h(z), h(z - 1), e(z), e(z), damp, ce.at[z - LO])


def interior_rest(e_ref, h_ref, m_ref, table, em, hm, damp, ch, ce, e2, h2, done, ce2):
    planes_z, width_x, width_y = m_ref.shape
    choices = [jnp.tile(c, (1, width_y // LANES)) for c in table_inverse(table, (SUB, LANES))]
    done[...] = jnp.zeros(done.shape, F32)
    rest = [z for z in range(planes_z) if not LO < z < HI]
    for z in rest:
        fill_ce(ce2, z, z, m_ref, choices, ch)

    def coef(z):
        return ce.at[z - LO] if LO < z < HI else ce2.at[z]

    def e1(z):
        return at(em, z - LO) if LO < z < HI else at(e2, z)

    def h1(z):
        return at(hm, z - LO) if LO <= z < HI else at(h2, z)

    def h_last(z):
        return at(hm, z - LO) if LO < z < HI - 1 else at(h2, z)

    for z in range(planes_z):
        if not LO <= z < HI:
            up = at(e_ref, z + 1) if z + 1 < planes_z else None
            update_mag(at(e_ref, z), up, at(h_ref, z), at(h2, z), damp, ch)
    for z in rest:
        update_elec(h1(z), h1(z - 1) if z else None, at(e_ref, z), at(e2, z), damp, coef(z))
    for z in range(planes_z):
        if not LO < z < HI - 1:
            up = e1(z + 1) if z + 1 < planes_z else None
            update_mag(e1(z), up, h1(z), at(h2, z), damp, ch)
    for z in range(planes_z):
        if not in_design(z):
            down = h_last(z - 1) if z else None
            update_elec(h_last(z), down, e1(z), at(e2, z), damp, coef(z))


def strips_x(
    e_ref, h_ref, m_ref, d_ref, table, xa_ref, xb_ref,
    e2_ref, h2_ref, e1_ref, sl_ref, xe, xh, ce,
):
    planes_z, width_x, width_y = m_ref.shape
    gx, gy = lax.axis_index("gx"), lax.axis_index("gy")
    total_x, total_y = width_x * lax.axis_size("gx"), width_y * lax.axis_size("gy")
    even = gx % 2 == 0
    shape = (SUB, width_y)
    sub = iota(shape, 0)
    cols = (iota(shape, 1) + gy * width_y).astype(F32)
    choices = [jnp.tile(c, (1, width_y // LANES)) for c in table_inverse(table, (SUB, LANES))]
    zero = jnp.zeros(shape, F32)
    damps, chs = [], []

    def strip(side, q):
        below, above = halo_rows(xa_ref, xb_ref, q, even)
        own = edge_tile(q, side * (width_x - SUB), e_ref, h_ref, m_ref, d_ref)
        if side == 0:
            return jnp.where(sub < 2, below, turn(own, 2, 0))
        return jnp.where(sub >= 6, turn(above, 6, 0), turn(own, 6, 0))

    for side in range(2):
        rows = (sub + gx * width_x + (-2 if side == 0 else width_x - 6)).astype(F32)
        inside = within(rows, cols, total_x, total_y)
        damping, coef_h, inverse = edge_coefs(rows, cols, total_x, total_y, inside)
        damps.append(damping)
        chs.append(coef_h)
        for z in range(planes_z):
            for c in range(3):
                xe[side, c, z] = strip(side, c * planes_z + z)
                xh[side, c, z + 1] = strip(side, (3 + c) * planes_z + z)
        for c in range(3):
            xe[side, c, planes_z] = zero
            xh[side, c, 0] = zero
        design, slope = design_terms(blur(strip(side, 6 * planes_z + ZLO)))
        sl_ref[side] = turn(slope, 6 if side == 0 else 2, 0)
        for z in range(planes_z):
            if in_design(z):
                ce[side, z] = design * inverse
            else:
                ce[side, z] = pick(strip(side, 6 * planes_z + z), choices) * inverse

    def mag(z):
        for side in range(2):
            ex, ey, ez = (xe[side, c, z] for c in range(3))
            cx = (turn(ez, width_y - 1, 1) - ez) - (xe[side, 1, z + 1] - ey)
            cy = (xe[side, 0, z + 1] - ex) - (turn(ez, SUB - 1, 0) - ez)
            cz = (turn(ey, SUB - 1, 0) - ey) - (turn(ex, width_y - 1, 1) - ex)
            for c, curl in enumerate((cx, cy, cz)):
                xh[side, c, z + 1] = damps[side] * xh[side, c, z + 1] - chs[side] * curl

    def elec(z):
        for side in range(2):
            hx, hy, hz = (xh[side, c, z + 1] for c in range(3))
            cx = (hz - turn(hz, 1, 1)) - (hy - xh[side, 1, z])
            cy = (hx - xh[side, 0, z]) - (hz - turn(hz, 1, 0))
            cz = (hy - turn(hy, 1, 0)) - (hx - turn(hx, 1, 1))
            for c, curl in enumerate((cx, cy, cz)):
                xe[side, c, z] = damps[side] * xe[side, c, z] + ce[side, z] * curl

    def loop(f):
        for z in range(planes_z):
            f(z)

    back = (6, 2)
    for n in range(STEPS):
        loop(mag)
        loop(elec)
        if n == 0:
            for side in range(2):
                for c in range(3):
                    for p in range(PLANES):
                        e1_ref[c, p, side] = turn(xe[side, c, ZLO + p], back[side], 0)

    def finish(z):
        for side in range(2):
            for c in range(3):
                e2_ref[c, z, side] = turn(xe[side, c, z], back[side], 0)
                h2_ref[c, z, side] = turn(xh[side, c, z + 1], back[side], 0)

    loop(finish)


def patch_rows(values, strip, start, width_x):
    sub = iota(values.shape, 0)
    if start == 0:
        values = jnp.where(sub < 2, strip[0], values)
    if start == width_x - SUB:
        values = jnp.where(sub >= 6, strip[1], values)
    return values


def patch_cols(values, strip, z):
    lane = iota((values.shape[0], LANES), 1)
    low = turn(strip, -(z * GROUP + 2), 1)
    high = turn(strip, LANES - 2 - (z * GROUP + GROUP - 4), 1)
    tiles = [values[:, k : k + LANES] for k in range(0, values.shape[1], LANES)]
    tiles[0] = jnp.where(lane < 2, low, tiles[0])
    tiles[-1] = jnp.where(lane >= LANES - 2, high, tiles[-1])
    return jnp.concatenate(tiles, axis=1)


def strips_y(width_x, width_y, s_ref, t_ref, ya_ref, yb_ref, table):
    gx, gy = lax.axis_index("gx"), lax.axis_index("gy")
    total_x, total_y = width_x * lax.axis_size("gx"), width_y * lax.axis_size("gy")
    planes_z = LANES // GROUP
    even = gy % 2 == 0
    size = width_x + SUB
    shape = (size, LANES)
    lane = iota(shape, 1)
    col = lane % GROUP
    plane = lane // GROUP
    from_low = jnp.where(even, yb_ref[...], ya_ref[...])
    from_high = jnp.where(even, ya_ref[...], yb_ref[...])

    def field(f):
        own = jnp.concatenate([s_ref[f], t_ref[f]], axis=0)
        own = jnp.where(col < 2, turn(from_low, -2 * f, 1), own)
        return jnp.where(col >= GROUP - 2, turn(from_high, GROUP - 2 - 2 * f, 1), own)

    row = iota(shape, 0)
    row = jnp.where(row >= width_x + 4, row - size, row)
    place = jnp.where(col < GROUP // 2, col - 2, col + (width_y - GROUP + 2))
    rows = (row + gx * width_x).astype(F32)
    cols = (place + gy * width_y).astype(F32)
    inside = within(rows, cols, total_x, total_y)
    damping, coef_h, inverse = edge_coefs(rows, cols, total_x, total_y, inside)
    source = field(6)
    design, slope = design_terms(blur(source))
    choices = [jnp.tile(c, (size // SUB, 1)) for c in table_inverse(table, (SUB, LANES))]
    layer = (plane >= ZLO) & (plane < ZLO + PLANES)
    coef_e = jnp.where(layer, design, pick(source, choices)) * inverse
    e = [field(c) for c in range(3)]
    h = [field(3 + c) for c in range(3)]
    top = plane == planes_z - 1
    bottom = plane == 0

    def dxf(v):
        return turn(v, size - 1, 0) - v

    def dyf(v):
        return turn(v, LANES - 1, 1) - v

    def dzf(v):
        return jnp.where(top, 0.0, turn(v, LANES - GROUP, 1)) - v

    def dxb(v):
        return v - turn(v, 1, 0)

    def dyb(v):
        return v - turn(v, 1, 1)

    def dzb(v):
        return v - jnp.where(bottom, 0.0, turn(v, GROUP, 1))

    steps = []
    for _ in range(STEPS):
        curl = (dyf(e[2]) - dzf(e[1]), dzf(e[0]) - dxf(e[2]), dxf(e[1]) - dyf(e[0]))
        h = [damping * v - coef_h * c for v, c in zip(h, curl)]
        curl = (dyb(h[2]) - dzb(h[1]), dzb(h[0]) - dxb(h[2]), dxb(h[1]) - dyb(h[0]))
        e = [damping * v + coef_e * c for v, c in zip(e, curl)]
        steps.append(e)
    return steps, h, slope, field(7)


def scalar_of(values, sub, lane):
    here = (iota(values.shape, 0) == sub) & (iota(values.shape, 1) == lane)
    return jnp.max(jnp.where(here, values, 0.0)).astype(jnp.int32)


def slot_of(param, rows_mine):
    gx, gy = lax.axis_index("gx"), lax.axis_index("gy")
    count_gx, count_gy = lax.axis_size("gx"), lax.axis_size("gy")
    owner = lax.div(param, jnp.int32(rows_mine))
    row = param - owner * rows_mine
    ox = lax.div(owner, jnp.int32(count_gy))
    oy = owner - ox * count_gy
    core = (oy ^ gy) & 1
    near = ((ox & 1) + 2 * (oy >> 1)) ^ ((gx & 1) + 2 * (gy >> 1))
    far = (ox >> 1) ^ (gx >> 1)
    return ((core * count_gy + near) * (count_gx // 2) + far) * rows_mine + row


def gradient(
    s_ref, t_ref, ya_ref, yb_ref, xa_ref, xb_ref, table, map_ref, e1_ref, e2_ref, xe1_ref, xe2_ref,
    sl_ref, xsl_ref, sum_ref, g_ref, buf_ref, ye_ref, yh_ref, ye1, lpad, vpad, gpad,
):
    width_x, width_y = sl_ref.shape
    planes_z = LANES // GROUP
    steps, h, slope_y, ids_y = strips_y(width_x, width_y, s_ref, t_ref, ya_ref, yb_ref, table)
    for c in range(3):
        ye_ref[c] = steps[-1][c]
        yh_ref[c] = h[c]
        ye1[c] = steps[0][c]
    ye1[3] = slope_y
    pad = 2 * SUB
    lpad[pl.ds(0, pad)] = jnp.zeros((pad, width_y), F32)
    lpad[pl.ds(pad + width_x, pad)] = jnp.zeros((pad, width_y), F32)
    buf_ref[...] = jnp.zeros(buf_ref.shape, F32)
    for start in range(0, width_x, SUB):
        here = pl.ds(start, SUB)
        total = sum_ref[here]
        for c in range(3):
            for p in range(PLANES):
                first = patch_rows(e1_ref[c, p, here], xe1_ref.at[c, p], start, width_x)
                first = patch_cols(first, ye1[c, here], ZLO + p)
                second = e2_ref[c, ZLO + p - LO, here]
                second = patch_rows(second, xe2_ref.at[c, ZLO + p], start, width_x)
                second = patch_cols(second, ye_ref[c, here], ZLO + p)
                total = total + g_ref[0, c, p, here] * first + g_ref[1, c, p, here] * second
        slope = patch_rows(sl_ref[here], xsl_ref, start, width_x)
        slope = patch_cols(slope, ye1[3, here], ZLO)
        lpad[pl.ds(pad + start, SUB)] = (grad_scale * (eps_high - eps_low)) * slope * total
    lane = iota((SUB, width_y), 1)
    for start in range(SUB, pad + width_x + SUB, SUB):
        v = lpad[pl.ds(start - 1, SUB)] + 2.0 * lpad[pl.ds(start, SUB)] + lpad[pl.ds(start + 1, SUB)]
        v = v / 16.0
        left = jnp.where(lane == 0, 0.0, turn(v, 1, 1))
        right = jnp.where(lane == width_y - 1, 0.0, turn(v, width_y - 1, 1))
        g = left + 2.0 * v + right
        for u in range(width_y // LANES):
            vpad[u, pl.ds(start, SUB)] = v[:, u * LANES : (u + 1) * LANES]
            gpad[u, pl.ds(start, SUB)] = g[:, u * LANES : (u + 1) * LANES]

    half = LANES // 2
    lines = TILE // 2
    tiles_x, tiles_y = width_x // TILE, width_y // TILE
    devices = lax.axis_size("gx") * lax.axis_size("gy")
    rows_mine = buf_ref.shape[0] // devices
    lane = iota((lines, LANES), 1)
    lane8 = iota((SUB, LANES), 1)
    sub8 = iota((SUB, LANES), 0)

    def add_tile(param, values):
        slot = slot_of(param, rows_mine)
        buf_ref[slot] = buf_ref[slot] + values

    def add_rows(ident, start, values):
        slot = slot_of(jnp.maximum(ident - 1, 0), rows_mine)
        rows = pl.ds(start, SUB)
        buf_ref[slot, rows] = buf_ref[slot, rows] + jnp.where(ident > 0, values, 0.0)

    for tx in range(tiles_x):
        for u in range(width_y // LANES):
            even = gpad[u, pl.ds(pad + tx * TILE, lines, stride=2)]
            odd = gpad[u, pl.ds(pad + tx * TILE + 1, lines, stride=2)]
            add_tile(map_ref[tx, 2 * u], jnp.where(lane < half, even, turn(odd, half, 1)))
            add_tile(map_ref[tx, 2 * u + 1], jnp.where(lane < half, turn(even, half, 1), odd))
    even_x = lax.axis_index("gx") % 2 == 0
    below, above = halo_rows(xa_ref, xb_ref, 7 * planes_z, even_x)
    before, after = pl.ds(pad - SUB, SUB), pl.ds(pad + width_x, SUB)
    for t in range(tiles_y):
        u, odd = divmod(t, 2)
        top, low = gpad[u, before], gpad[u, after]
        top = top if odd else turn(top, half, 1)
        low = turn(low, half, 1) if odd else low
        keep = (sub8 == SUB - 1) & (lane8 >= half)
        add_rows(scalar_of(below, 0, t * TILE), lines - SUB, jnp.where(keep, top, 0.0))
        keep = (sub8 == 0) & (lane8 < half)
        add_rows(scalar_of(above, 0, t * TILE), 0, jnp.where(keep, low, 0.0))
    end = width_y // LANES - 1
    for tx in range(tiles_x):
        ids = ids_y[tx * TILE : tx * TILE + SUB]
        even, odd = (pl.ds(pad + tx * TILE + k, lines, stride=2) for k in (0, 1))
        left = jnp.where(lane == half - 1, turn(vpad[0, even], half - 1, 1), 0.0)
        left = jnp.where(lane == LANES - 1, turn(vpad[0, odd], LANES - 1, 1), left)
        right = jnp.where(lane == 0, turn(vpad[end, even], 1, 1), 0.0)
        right = jnp.where(lane == half, turn(vpad[end, odd], half + 1, 1), right)
        for column, values in ((0, left), (GROUP - 1, right)):
            ident = scalar_of(ids, 0, column)
            add_tile(jnp.maximum(ident - 1, 0), jnp.where(ident > 0, values, 0.0))
    tail = ids_y[width_x : width_x + SUB]
    corners = (
        (SUB - 1, 0, before, 0, lines - SUB, LANES - 1),
        (SUB - 1, GROUP - 1, before, end, lines - SUB, half),
        (0, 0, after, 0, 0, half - 1),
        (0, GROUP - 1, after, end, 0, 0),
    )
    for sub, column, rows, u, start, target in corners:
        source = LANES - 1 if u == end and column else 0
        keep = (sub8 == sub) & (lane8 == target)
        values = jnp.where(keep, turn(vpad[u, rows], target - source, 1), 0.0)
        add_rows(scalar_of(tail, sub, column), start, values)


def merge(e_ref, h_ref, em, hm, xe_ref, xh_ref, ye_ref, yh_ref, eo_ref, ho_ref):
    _, planes_z, width_x, _ = e_ref.shape
    parts = (
        (e_ref, em, xe_ref, ye_ref, eo_ref, LO + 2, HI - 1),
        (h_ref, hm, xh_ref, yh_ref, ho_ref, LO + 1, HI - 1),
    )
    for rest, mid, xs, ys, out, low, high in parts:
        for z in range(planes_z):
            src = mid.at[0, z - LO] if low <= z < high else rest.at[0, z]
            for start in range(0, width_x, SUB):
                here = pl.ds(start, SUB)
                values = patch_rows(src[here], xs.at[0, z], start, width_x)
                out[0, z, here] = patch_cols(values, ys[0, here], z)


def first_sum(parts, buf_ref, got_ref, *outs):
    size = outs[0].shape[0]
    for k in range(parts):
        rows = pl.ds(k * size, size)
        outs[k][...] = buf_ref[rows] + got_ref[rows]


def second_sum(parts, rows_mine, *refs):
    ins, outs = refs[:parts], refs[parts + 1 :]
    for k, out in enumerate(outs):
        rows = pl.ds(k * rows_mine, rows_mine)
        out[...] = sum(ref[rows] for ref in ins[1:]) + ins[0][rows]


def pair(block, partner):
    count_gx, count_gy = lax.axis_size("gx"), lax.axis_size("gy")
    route = []
    for i in range(count_gx):
        for j in range(count_gy):
            a, b = partner(i, j)
            if 0 <= a < count_gx and 0 <= b < count_gy:
                route.append((i * count_gy + j, a * count_gy + b))
    return lax.ppermute(block, ("gx", "gy"), route)


def on_device(e_adj, h_adj, density, material, eps_table, dft_adj, dft_fwd, tile_map):
    planes_z, width_x, width_y = material.shape
    count_gx, count_gy = lax.axis_size("gx"), lax.axis_size("gy")
    block = 4 * width_x * width_y
    groups = -(-n_faces(planes_z) // 4)
    face = struct(groups, SUB, width_y)
    xa, xb = pl.pallas_call(
        pack_x,
        out_shape=(face, face),
        in_specs=[HBM] * 5,
        out_specs=(VMEM,) * 2,
        scratch_shapes=[
            pltpu.VMEM((3, planes_z, 2 * SUB, width_y), F32),
            pltpu.VMEM((3, planes_z, 2 * SUB, width_y), F32),
            pltpu.VMEM((planes_z, 2 * SUB, width_y), jnp.int32),
            pltpu.VMEM((2 * SUB, width_y), F32),
            pltpu.SMEM(tile_map.shape, jnp.int32),
            pltpu.SemaphoreType.DMA((9,)),
        ],
        compiler_params=params(62700000),
        name="pack_x",
    )(e_adj, h_adj, material, density, tile_map)
    xa = pair(xa, lambda i, j: (i ^ 1, j))
    xb = pair(xb, lambda i, j: (((i + 1) ^ 1) - 1, j))
    strip = pl.pallas_call(
        build_strips,
        out_shape=struct(8, width_x, LANES),
        in_specs=[VMEM] * 4 + [SMEM],
        out_specs=VMEM,
        compiler_params=params(),
        cost_estimate=cost(1, 1),
        name="build_strips",
    )(e_adj, h_adj, material, density, tile_map)

    rows = 2 * SUB
    moved = struct(width_x, width_y), struct(STEPS, 3, PLANES, width_x, width_y)
    base, weight = pl.pallas_call(
        transform,
        grid=(width_x // rows,),
        out_shape=moved,
        in_specs=[pl.BlockSpec((FREQ, 2, 3, PLANES, rows, width_y), lambda i: (0, 0, 0, 0, i, 0))] * 2,
        out_specs=(
            pl.BlockSpec((rows, width_y), lambda i: (i, 0)),
            pl.BlockSpec((STEPS, 3, PLANES, rows, width_y), lambda i: (0, 0, 0, i, 0)),
        ),
        compiler_params=params(),
        cost_estimate=cost(1, 1),
        name="transform",
    )(dft_adj, dft_fwd)
    plane = struct(width_x, width_y)
    middle = struct(3, HI - LO, width_x, width_y)
    full = struct(3, planes_z, width_x, width_y)
    em, hm, e1, slope, damp, ch, ce = pl.pallas_call(
        interior_first,
        out_shape=(middle, middle, struct(3, PLANES, width_x, width_y))
        + (plane,) * 3
        + (struct(HI - LO, width_x, width_y),),
        in_specs=[VMEM] * 4 + [SMEM],
        out_specs=(VMEM,) * 7,
        compiler_params=params(),
        cost_estimate=cost(1, 1),
        name="interior_first",
    )(e_adj, h_adj, material, density, eps_table)
    e2, h2, done = pl.pallas_call(
        interior_rest,
        out_shape=(full, full, struct(SUB, LANES)),
        in_specs=[VMEM] * 3 + [SMEM] + [VMEM] * 5,
        out_specs=(VMEM,) * 3,
        scratch_shapes=[pltpu.VMEM((planes_z, width_x, width_y), F32)],
        compiler_params=params(),
        cost_estimate=cost(1, 1),
        name="interior_rest",
    )(e_adj, h_adj, material, eps_table, em, hm, damp, ch, ce)

    tails, ya, yb = pl.pallas_call(
        pack_y,
        out_shape=(struct(8, SUB, LANES),) + (struct(width_x + SUB, LANES),) * 2,
        in_specs=[VMEM] * 3 + [ANY],
        out_specs=(VMEM,) * 3,
        compiler_params=params(),
        name="pack_y",
    )(strip, xa, xb, slope)
    ya = pair(ya, lambda i, j: (i, j ^ 1))
    yb = pair(yb, lambda i, j: (i, ((j + 1) ^ 1) - 1))
    xe2, xh2, xe1, xslope = pl.pallas_call(
        strips_x,
        out_shape=(
            struct(3, planes_z, 2, SUB, width_y),
            struct(3, planes_z, 2, SUB, width_y),
            struct(3, PLANES, 2, SUB, width_y),
            struct(2, SUB, width_y),
        ),
        in_specs=[VMEM] * 4 + [SMEM] + [VMEM] * 2,
        out_specs=(VMEM,) * 4,
        scratch_shapes=[
            pltpu.VMEM((2, 3, planes_z + 1, SUB, width_y), F32),
            pltpu.VMEM((2, 3, planes_z + 1, SUB, width_y), F32),
            pltpu.VMEM((2, planes_z, SUB, width_y), F32),
        ],
        compiler_params=params(),
        cost_estimate=cost(1, 1),
        name="strips_x",
    )(e_adj, h_adj, material, density, eps_table, xa, xb)

    devices = count_gx * count_gy
    rows_mine = (width_x // TILE) * (width_y // TILE) // REPEAT
    lines = TILE // 2
    padded = width_x + 4 * SUB
    buf, ye2, yh2 = pl.pallas_call(
        gradient,
        out_shape=(struct(devices * rows_mine, lines, LANES),)
        + (struct(3, width_x + SUB, LANES),) * 2,
        in_specs=[VMEM] * 6 + [SMEM] * 2 + [VMEM] * 8,
        out_specs=(VMEM,) * 3,
        scratch_shapes=[
            pltpu.VMEM((4, width_x + SUB, LANES), F32),
            pltpu.VMEM((padded, width_y), F32),
            pltpu.VMEM((width_y // LANES, padded, LANES), F32),
            pltpu.VMEM((width_y // LANES, padded, LANES), F32),
        ],
        compiler_params=params(),
        cost_estimate=cost(1, 1),
        name="gradient",
    )(strip, tails, ya, yb, xa, xb, eps_table, tile_map, e1, em, xe1, xe2, slope, xslope, base, weight)

    half = devices * rows_mine // 2
    far = count_gx // 2
    got = pair(buf[half:], lambda i, j: (i, j ^ 1))
    parts = pl.pallas_call(
        lambda *refs: first_sum(count_gy, *refs),
        out_shape=(struct(far * rows_mine, lines, LANES),) * count_gy,
        in_specs=[VMEM] * 2,
        out_specs=(VMEM,) * count_gy,
        compiler_params=params(),
        name="first_sum",
    )(buf, got)
    parts = [parts[0]] + [
        pair(parts[k], lambda i, j: (i ^ (k & 1), j ^ (k >> 1 << 1))) for k in range(1, count_gy)
    ]
    core = pl.BlockSpec((1, HI - LO, width_x, width_y), lambda c: (c, 0, 0, 0))
    whole = pl.BlockSpec((1, planes_z, width_x, width_y), lambda c: (c, 0, 0, 0))
    edge = pl.BlockSpec((1, planes_z, 2, SUB, width_y), lambda c: (c, 0, 0, 0, 0))
    side = pl.BlockSpec((1, width_x + SUB, LANES), lambda c: (c, 0, 0))
    e_out, h_out = pl.pallas_call(
        merge,
        grid=(3,),
        out_shape=(struct(3, planes_z, width_x, width_y),) * 2,
        in_specs=[whole, whole, core, core, edge, edge, side, side],
        out_specs=(whole, whole),
        compiler_params=params(),
        cost_estimate=cost(1, 1),
        name="merge",
    )(e2, h2, em, hm, xe2, xh2, ye2, yh2)
    parts = pl.pallas_call(
        lambda *refs: second_sum(count_gy, rows_mine, *refs),
        out_shape=(struct(rows_mine, lines, LANES),) * far,
        in_specs=[VMEM] * count_gy + [ANY],
        out_specs=(VMEM,) * far,
        compiler_params=params(),
        name="second_sum",
    )(*parts, done)
    parts = [parts[0]] + [pair(parts[k], lambda i, j: (i ^ (k << 1), j)) for k in range(1, far)]
    param_grad = sum(parts[1:], parts[0]).reshape(rows_mine, TILE * TILE)

    return e_out, h_out, param_grad


def solution(mesh):
    in_specs = (
        P(None, None, "gx", "gy"),
        P(None, None, "gx", "gy"),
        P("gx", "gy"),
        P(None, "gx", "gy"),
        P(),
        P(None, None, None, None, "gx", "gy"),
        P(None, None, None, None, "gx", "gy"),
        P("gx", "gy"),
    )
    out_specs = (P(None, None, "gx", "gy"), P(None, None, "gx", "gy"), P(("gx", "gy"), None))
    return jax.shard_map(
        on_device, mesh=mesh, in_specs=in_specs, out_specs=out_specs, check_vma=False
    )
```

```python
import math

import jax
import jax.numpy as jnp
from jax import lax
from jax.experimental import pallas as pl
from jax.experimental.pallas import tpu as pltpu
from jax.sharding import PartitionSpec as P

PLANES = 2
ZLO = 3
STEPS = 2
FREQ = 4
PML = 12
TILE = 64
REPEAT = 4

courant = 0.5
sigma_peak = 0.8
dft_weight = 0.5
sharpness = 4.0
threshold = 0.5
eps_low = 2.1
eps_high = 12.1
grad_scale = 0.01

F32 = jnp.float32
LANES = 128
SUB = 8
GROUP = 16
ANY = pl.BlockSpec(memory_space=pl.ANY)
HBM = pl.BlockSpec(memory_space=pltpu.HBM)
VMEM = pl.BlockSpec(memory_space=pltpu.VMEM)
SMEM = pl.BlockSpec(memory_space=pltpu.SMEM)


def params(size=40 * 2**20):
    return pltpu.CompilerParams(vmem_limit_bytes=size)


def struct(*shape, dtype=F32):
    return jax.ShapeDtypeStruct(shape, dtype)


def cost(flops, moved):
    return pl.CostEstimate(flops=int(flops), bytes_accessed=int(moved), transcendentals=0)


def iota(shape, dim):
    return lax.broadcasted_iota(jnp.int32, shape, dim)


def in_design(z):
    return ZLO <= z < ZLO + PLANES


def turn(values, shift, axis):
    size = values.shape[axis]
    shift %= size
    return values if shift == 0 else pltpu.roll(values, shift, axis)


def depth_cubed(places, total):
    depth = jnp.maximum(jnp.maximum(PML - places, places - (total - 1 - PML)), 0.0) / PML
    return depth * depth * depth


def edge_coefs(rows, cols, total_x, total_y, inside=None):
    sigma = sigma_peak * (depth_cubed(rows, total_x) + depth_cubed(cols, total_y))
    inverse = 1.0 / (1.0 + 0.5 * sigma)
    if inside is not None:
        inverse = jnp.where(inside, inverse, 0.0)
    return (1.0 - 0.5 * sigma) * inverse, courant * inverse, inverse


def within(rows, cols, total_x, total_y):
    return (rows >= 0) & (rows < total_x) & (cols >= 0) & (cols < total_y)


def table_inverse(table, shape):
    return [courant / jnp.full(shape, table[k], F32) for k in range(table.shape[0])]


def pick(index, choices):
    out = jnp.zeros_like(choices[0])
    for k, choice in enumerate(choices):
        out = jnp.where(index == k, choice, out)
    return out


def design_terms(filtered):
    high = math.tanh(sharpness * threshold)
    norm = high + math.tanh(sharpness * (1.0 - threshold))
    bend = jnp.tanh(sharpness * (filtered - threshold))
    eps = eps_low + (eps_high - eps_low) * ((high + bend) / norm)
    return courant / eps, sharpness * (1.0 - bend * bend) / norm


def blur(values):
    rows, cols = values.shape
    summed = turn(values, 1, 0) + 2.0 * values + turn(values, rows - 1, 0)
    return (turn(summed, 1, 1) + 2.0 * summed + turn(summed, cols - 1, 1)) / 16.0


def id_row(tile_map, tx, shape):
    lane = iota(shape, len(shape) - 1)
    out = jnp.zeros(shape, F32)
    for t in range(tile_map.shape[1]):
        out = jnp.where(lane // TILE == t, (tile_map[tx, t] + 1).astype(F32), out)
    return out


TILES = 10
BEHIND = (0, 1, 2, 4, 5)


def pack_x(e_in, h_in, m_in, d_in, map_in, a_ref, b_ref, eb, hb, mb, db, map_ref, sems):
    planes_z, size, width_y = m_in.shape
    span = 2 * SUB
    tiles = width_y // LANES
    views = [
        (e_in, eb.reshape(tiles, 3, planes_z, span, LANES)),
        (h_in, hb.reshape(tiles, 3, planes_z, span, LANES)),
        (m_in, mb.reshape(tiles, planes_z, span, LANES)),
    ]
    copies = []
    for k, start in enumerate((0, size - SUB)):
        here, there = pl.ds(start, SUB), pl.ds(k * SUB, SUB)
        for u in range(tiles):
            lanes = pl.ds(u * LANES, LANES)
            for n, (src, dst) in enumerate(views):
                source = src.at[:, here, lanes] if n == 2 else src.at[:, :, here, lanes]
                target = dst.at[u, :, there] if n == 2 else dst.at[u, :, :, there]
                copies.append(pltpu.make_async_copy(source, target, sems.at[len(copies)]))
        copies.append(pltpu.make_async_copy(d_in.at[here], db.at[there], sems.at[len(copies)]))
    copies.append(pltpu.make_async_copy(map_in, map_ref, sems.at[len(copies)]))
    for copy in copies:
        copy.start()
    gx, gy = lax.axis_index("gx"), lax.axis_index("gy")
    total_x, total_y = size * lax.axis_size("gx"), width_y * lax.axis_size("gy")
    shape = (SUB, width_y)
    sub = iota(shape, 0)
    rows = jnp.full(shape, (gx + 1) * size - 2, jnp.int32).astype(F32)
    cols = (iota(shape, 1) + gy * width_y).astype(F32)
    damping, coef_h, _ = edge_coefs(rows, cols, total_x, total_y)
    layer = (sub >= ZLO) & (sub < ZLO + PLANES)
    for copy in copies:
        copy.wait()

    def row(ref, c, r):
        rows = pl.ds(c * planes_z * span + r, planes_z, stride=span)
        return jnp.concatenate([ref[u, rows] for u in range(tiles)], axis=1)

    near, far = span - 1, span - 2
    ex, ey, ez = (row(eb, c, far) for c in range(3))
    up = jnp.where(sub == SUB - 1, 0.0, turn(ex, SUB - 1, 0))
    curl_y = (up - ex) - (row(eb, 2, near) - ez)
    curl_z = (row(eb, 1, near) - ey) - (turn(ex, width_y - 1, 1) - ex)
    mag = [row(hb, c, far) for c in (1, 2)]
    high = [row(eb, c, near) for c in range(3)] + [row(hb, c, near) for c in range(3)]
    high += [damping * h - coef_h * curl for h, curl in zip(mag, (curl_y, curl_z))]
    low = [row(eb, c, 0) for c in range(3)] + [row(hb, c, 0) for c in range(3)]
    low += [row(eb, 1, 1), row(eb, 2, 1)]
    for side, edge, further, tx in ((low, 0, 1, 0), (high, near, far, map_ref.shape[0] - 1)):
        density = jnp.broadcast_to(db[edge : edge + 1], shape)
        side.append(jnp.where(layer, density, row(mb, 0, edge).astype(F32)))
        misc = jnp.broadcast_to(db[further : further + 1], shape)
        side.append(jnp.where(sub == 1, id_row(map_ref, tx, shape), misc))
    strips = [row_to_strip(v) for v in [ex, ey, ez] + mag]
    strips.append(strips[-1])
    for k in range(3):
        pair_of = jnp.concatenate([strips[2 * k], strips[2 * k + 1]], axis=1)
        high[-1] = jnp.where(sub == 2 + k, jnp.broadcast_to(pair_of, shape), high[-1])
    even = gx % 2 == 0
    for k in range(TILES):
        a_ref[k] = jnp.where(even, high[k], low[k])
        b_ref[k] = jnp.where(even, low[k], high[k])


def neighbours(axis, from_a, from_b):
    here = lax.axis_index(axis)
    even = here % 2 == 0
    before = jnp.where(here > 0, jnp.where(even, from_b, from_a), 0.0)
    after = jnp.where(here < lax.axis_size(axis) - 1, jnp.where(even, from_a, from_b), 0.0)
    return before, after


def x_halos(xa_ref, xb_ref):
    both = [neighbours("gx", xa_ref[k], xb_ref[k]) for k in range(TILES)]
    return [t[0] for t in both], [t[1] for t in both]


def ends(values):
    lane = iota((values.shape[0], LANES), 1)
    return jnp.where(lane < LANES // 2, values[:, :LANES], values[:, -LANES:])


def row_to_strip(values):
    shape = (SUB, LANES)
    rolled = pltpu.roll(ends(values), GROUP // 2, 1, stride=GROUP, stride_axis=0)
    rolled = jnp.where(iota(shape, 1) // GROUP == iota(shape, 0), rolled, 0.0)
    return jnp.sum(rolled, axis=0, keepdims=True)


def build_strips(e_ref, h_ref, m_ref, d_ref, map_ref, s_ref):
    planes_z, width_x, width_y = m_ref.shape
    group = iota((SUB, LANES), 1) // GROUP

    def gather(get, here):
        acc = jnp.zeros((SUB, LANES), F32)
        for z in range(planes_z):
            acc = jnp.where(group == z, turn(ends(get(z, here)), z * GROUP + GROUP // 2, 1), acc)
        return acc

    def body(c, _):
        for base, ref in ((0, e_ref), (3, h_ref)):
            for start in range(0, width_x, SUB):
                here = pl.ds(start, SUB)
                s_ref[base + c, here] = gather(lambda z, here: ref[c, z, here], here)
        return 0

    lax.fori_loop(0, 3, body, 0)

    def source(z, here):
        return d_ref[here] if in_design(z) else m_ref[z, here].astype(F32)

    for start in range(0, width_x, SUB):
        here = pl.ds(start, SUB)
        s_ref[6, here] = gather(source, here)
        row = id_row(map_ref, start // TILE, (SUB, width_y))
        s_ref[7, here] = turn(ends(row), GROUP // 2, 1)


def pack_y(s_ref, xa_ref, xb_ref, _after, t_ref, a_ref, b_ref):
    width_x = s_ref.shape[1]
    even_y = lax.axis_index("gy") % 2 == 0
    below, above = x_halos(xa_ref, xb_ref)
    shape = (SUB, LANES)
    sub = iota(shape, 0)

    def row(tile, k):
        return jnp.broadcast_to(tile[k : k + 1], tile.shape)

    def wide(values):
        return jnp.broadcast_to(values, shape)

    zero = jnp.zeros(shape, F32)
    tails = []
    for f in range(8):
        if f < 7:
            k = 8 if f == 6 else f
            after_1, before_1 = (wide(row_to_strip(side[k])) for side in (above, below))
        else:
            after_1, before_1 = (wide(row_to_strip(row(side[9], 1))) for side in (above, below))
        after_2, before_2 = zero, zero
        if f in (1, 2):
            after_2 = wide(row_to_strip(above[5 + f]))
        if f in BEHIND:
            k = BEHIND.index(f)
            lanes = (k % 2) * LANES
            before_2 = wide(below[9][2 + k // 2 : 3 + k // 2, lanes : lanes + LANES])
        if f == 6:
            after_2, before_2 = (wide(row_to_strip(row(side[9], 0))) for side in (above, below))
        tail = jnp.where(sub == 0, after_1, jnp.where(sub == 1, after_2, 0.0))
        tail = jnp.where(sub == 6, before_2, jnp.where(sub == 7, before_1, tail))
        t_ref[f] = tail
        tails.append(tail)
    lane = iota(shape, 1) % GROUP
    for start in range(0, width_x + SUB, SUB):
        low = zero
        high = zero
        for f in range(8):
            values = tails[f] if start == width_x else s_ref[f, pl.ds(start, SUB)]
            mask = lane // 2 == f
            low = jnp.where(mask, turn(values, 2 * f - GROUP // 2, 1), low)
            high = jnp.where(mask, turn(values, 2 * f - (GROUP // 2 - 2), 1), high)
        a_ref[pl.ds(start, SUB)] = jnp.where(even_y, high, low)
        b_ref[pl.ds(start, SUB)] = jnp.where(even_y, low, high)


def transform(adj_ref, fwd_ref, s_ref, g_ref):
    rows, cols = s_ref.shape
    total = jnp.zeros((rows, cols), F32)
    for c in range(3):
        for p in range(PLANES):
            parts = [None] * STEPS
            for f in range(FREQ):
                real = fwd_ref[f, 0, c, p].astype(F32)
                imag = fwd_ref[f, 1, c, p].astype(F32)
                total = total + (real * adj_ref[f, 0, c, p] - imag * adj_ref[f, 1, c, p])
                for n in range(STEPS):
                    angle = (0.21 + 0.06 * f) * (n + 1)
                    term = (dft_weight * math.cos(angle)) * real + (
                        dft_weight * math.sin(angle)
                    ) * imag
                    parts[n] = term if parts[n] is None else parts[n] + term
            for n in range(STEPS):
                g_ref[n, c, p] = parts[n]
    s_ref[...] = total


LO = ZLO - STEPS
HI = ZLO + PLANES + STEPS - 1


def update_mag(e, e_up, h, out, damp, ch):
    width_x, width_y = damp.shape
    for start in range(0, width_x, SUB):
        here = pl.ds(start, SUB)

        def ahead(c, tile):
            if start + SUB < width_x:
                return e(c)[pl.ds(start + 1, SUB)]
            return turn(tile, SUB - 1, 0)

        ex, ey, ez = (e(c)[here] for c in range(3))
        up_x = e_up(0)[here] - ex if e_up else -ex
        up_y = e_up(1)[here] - ey if e_up else -ey
        cx = (turn(ez, width_y - 1, 1) - ez) - up_y
        cy = up_x - (ahead(2, ez) - ez)
        cz = (ahead(1, ey) - ey) - (turn(ex, width_y - 1, 1) - ex)
        dm, cf = damp[here], ch[here]
        for c, curl in enumerate((cx, cy, cz)):
            out(c)[here] = dm * h(c)[here] - cf * curl


def update_elec(h, h_down, e, out, damp, ce):
    width_x, width_y = damp.shape
    for start in range(0, width_x, SUB):
        here = pl.ds(start, SUB)

        def behind(c, tile):
            return h(c)[pl.ds(start - 1, SUB)] if start else turn(tile, 1, 0)

        hx, hy, hz = (h(c)[here] for c in range(3))
        up_x = hx - h_down(0)[here] if h_down else hx
        up_y = hy - h_down(1)[here] if h_down else hy
        cx = (hz - turn(hz, 1, 1)) - up_y
        cy = up_x - (hz - behind(2, hz))
        cz = (hy - behind(1, hy)) - (hx - turn(hx, 1, 1))
        dm, cf = damp[here], ce[here]
        for c, curl in enumerate((cx, cy, cz)):
            out(c)[here] = dm * e(c)[here] + cf * curl


def at(ref, z):
    return lambda c: ref.at[c, z]


def fill_ce(ce, k, z, m_ref, choices, ch):
    for start in range(0, ch.shape[0], SUB):
        here = pl.ds(start, SUB)
        ce[k, here] = pick(m_ref[z, here], choices) * (ch[here] * (1.0 / courant))


def interior_first(e_ref, h_ref, m_ref, d_ref, table, em, hm, e1_ref, sl_ref, damp, ch, ce):
    planes_z, width_x, width_y = m_ref.shape
    gx, gy = lax.axis_index("gx"), lax.axis_index("gy")
    total_x, total_y = width_x * lax.axis_size("gx"), width_y * lax.axis_size("gy")
    shape = (width_x, width_y)
    rows = (iota(shape, 0) + gx * width_x).astype(F32)
    cols = (iota(shape, 1) + gy * width_y).astype(F32)
    damping, coef_h, inverse = edge_coefs(rows, cols, total_x, total_y)
    damp[...] = damping
    ch[...] = coef_h
    design, slope = design_terms(blur(d_ref[...]))
    sl_ref[...] = slope
    choices = [jnp.tile(c, (1, width_y // LANES)) for c in table_inverse(table, (SUB, LANES))]
    for z in range(LO, HI):
        if in_design(z):
            ce[z - LO] = design * inverse
        elif z > LO:
            fill_ce(ce, z - LO, z, m_ref, choices, ch)

    def e(z):
        return at(em, z - LO)

    def h(z):
        return at(hm, z - LO)

    for z in range(LO, HI):
        update_mag(at(e_ref, z), at(e_ref, z + 1), at(h_ref, z), h(z), damp, ch)
    for z in range(LO + 1, HI):
        update_elec(h(z), h(z - 1), at(e_ref, z), e(z), damp, ce.at[z - LO])
    for c in range(3):
        for p in range(PLANES):
            e1_ref[c, p] = em[c, ZLO + p - LO]
    for z in range(LO + 1, HI - 1):
        update_mag(e(z), e(z + 1), h(z), h(z), damp, ch)
    for z in range(LO + 2, HI - 1):
        update_elec(h(z), h(z - 1), e(z), e(z), damp, ce.at[z - LO])


def interior_rest(e_ref, h_ref, m_ref, table, em, hm, damp, ch, ce, e2, h2, done, ce2):
    planes_z, width_x, width_y = m_ref.shape
    choices = [jnp.tile(c, (1, width_y // LANES)) for c in table_inverse(table, (SUB, LANES))]
    done[...] = jnp.zeros(done.shape, F32)
    rest = [z for z in range(planes_z) if not LO < z < HI]
    for z in rest:
        fill_ce(ce2, z, z, m_ref, choices, ch)

    def coef(z):
        return ce.at[z - LO] if LO < z < HI else ce2.at[z]

    def e1(z):
        return at(em, z - LO) if LO < z < HI else at(e2, z)

    def h1(z):
        return at(hm, z - LO) if LO <= z < HI else at(h2, z)

    def h_last(z):
        return at(hm, z - LO) if LO < z < HI - 1 else at(h2, z)

    for z in range(planes_z):
        if not LO <= z < HI:
            up = at(e_ref, z + 1) if z + 1 < planes_z else None
            update_mag(at(e_ref, z), up, at(h_ref, z), at(h2, z), damp, ch)
    for z in rest:
        update_elec(h1(z), h1(z - 1) if z else None, at(e_ref, z), at(e2, z), damp, coef(z))
    for z in range(planes_z):
        if not LO < z < HI - 1:
            up = e1(z + 1) if z + 1 < planes_z else None
            update_mag(e1(z), up, h1(z), at(h2, z), damp, ch)
    for z in range(planes_z):
        if not in_design(z):
            down = h_last(z - 1) if z else None
            update_elec(h_last(z), down, e1(z), at(e2, z), damp, coef(z))


def strips_x(
    e_ref, h_ref, m_ref, d_ref, table, xa_ref, xb_ref,
    e2_ref, h2_ref, e1_ref, sl_ref, xe, xh, ce,
):
    planes_z, width_x, width_y = m_ref.shape
    gx, gy = lax.axis_index("gx"), lax.axis_index("gy")
    total_x, total_y = width_x * lax.axis_size("gx"), width_y * lax.axis_size("gy")
    shape = (SUB, width_y)
    sub = iota(shape, 0)
    cols = (iota(shape, 1) + gy * width_y).astype(F32)
    choices = [jnp.tile(c, (1, width_y // LANES)) for c in table_inverse(table, (SUB, LANES))]
    zero = jnp.zeros(shape, F32)
    damps, chs = [], []

    below, above = x_halos(xa_ref, xb_ref)
    edges = pl.ds(0, SUB), pl.ds(width_x - SUB, SUB)

    def place(values, tile, z, at_sub):
        return jnp.where(sub == at_sub, turn(tile, at_sub - z, 0), values)

    def strip(side, own, near, far, z):
        out = turn(own, 2 if side == 0 else 6, 0)
        out = place(out, near, z, 1 if side == 0 else 6)
        if far is None:
            return jnp.where(sub == (0 if side == 0 else 7), 0.0, out)
        return place(out, far[0], far[1], 0 if side == 0 else 7)

    def source(side, z):
        own = d_ref[edges[side]] if in_design(z) else m_ref[z, edges[side]].astype(F32)
        halo = (below, above)[side]
        return strip(side, own, halo[8], (halo[9], 0), z)

    for side in range(2):
        rows = (sub + gx * width_x + (-2 if side == 0 else width_x - 6)).astype(F32)
        inside = within(rows, cols, total_x, total_y)
        damping, coef_h, inverse = edge_coefs(rows, cols, total_x, total_y, inside)
        damps.append(damping)
        chs.append(coef_h)
        for z in range(planes_z):
            for c in range(3):
                halo = (below, above)[side]
                far = (above[5 + c], z) if side and c else None
                xe[side, c, z] = strip(side, e_ref[c, z, edges[side]], halo[c], far, z)
                xh[side, c, z + 1] = strip(side, h_ref[c, z, edges[side]], halo[3 + c], None, z)
        for c in range(3):
            xe[side, c, planes_z] = zero
            xh[side, c, 0] = zero
        design, slope = design_terms(blur(source(side, ZLO)))
        sl_ref[side] = turn(slope, 6 if side == 0 else 2, 0)
        for z in range(planes_z):
            if in_design(z):
                ce[side, z] = design * inverse
            else:
                ce[side, z] = pick(source(side, z), choices) * inverse

    def mag(z):
        for side in range(2):
            ex, ey, ez = (xe[side, c, z] for c in range(3))
            cx = (turn(ez, width_y - 1, 1) - ez) - (xe[side, 1, z + 1] - ey)
            cy = (xe[side, 0, z + 1] - ex) - (turn(ez, SUB - 1, 0) - ez)
            cz = (turn(ey, SUB - 1, 0) - ey) - (turn(ex, width_y - 1, 1) - ex)
            for c, curl in enumerate((cx, cy, cz)):
                xh[side, c, z + 1] = damps[side] * xh[side, c, z + 1] - chs[side] * curl

    def elec(z):
        for side in range(2):
            hx, hy, hz = (xh[side, c, z + 1] for c in range(3))
            cx = (hz - turn(hz, 1, 1)) - (hy - xh[side, 1, z])
            cy = (hx - xh[side, 0, z]) - (hz - turn(hz, 1, 0))
            cz = (hy - turn(hy, 1, 0)) - (hx - turn(hx, 1, 1))
            for c, curl in enumerate((cx, cy, cz)):
                xe[side, c, z] = damps[side] * xe[side, c, z] + ce[side, z] * curl

    def loop(f):
        for z in range(planes_z):
            f(z)

    back = (6, 2)
    for n in range(STEPS):
        loop(mag)
        if n == 0:
            for z in range(planes_z):
                for c in (1, 2):
                    xh[0, c, z + 1] = place(xh[0, c, z + 1], below[5 + c], z, 0)
        loop(elec)
        if n == 0:
            for side in range(2):
                for c in range(3):
                    for p in range(PLANES):
                        e1_ref[c, p, side] = turn(xe[side, c, ZLO + p], back[side], 0)

    def finish(z):
        for side in range(2):
            for c in range(3):
                e2_ref[c, z, side] = turn(xe[side, c, z], back[side], 0)
                h2_ref[c, z, side] = turn(xh[side, c, z + 1], back[side], 0)

    loop(finish)


def patch_rows(values, strip, start, width_x):
    sub = iota(values.shape, 0)
    if start == 0:
        values = jnp.where(sub < 2, strip[0], values)
    if start == width_x - SUB:
        values = jnp.where(sub >= 6, strip[1], values)
    return values


def patch_cols(values, strip, z):
    lane = iota((values.shape[0], LANES), 1)
    rolled = turn(strip, -(z * GROUP + GROUP // 2), 1)
    tiles = [values[:, k : k + LANES] for k in range(0, values.shape[1], LANES)]
    tiles[0] = jnp.where(lane < 2, rolled, tiles[0])
    tiles[-1] = jnp.where(lane >= LANES - 2, rolled, tiles[-1])
    return jnp.concatenate(tiles, axis=1)


def strips_y(width_x, width_y, s_ref, t_ref, ya_ref, yb_ref, table):
    gx, gy = lax.axis_index("gx"), lax.axis_index("gy")
    total_x, total_y = width_x * lax.axis_size("gx"), width_y * lax.axis_size("gy")
    planes_z = LANES // GROUP
    size = width_x + SUB
    shape = (size, LANES)
    lane = iota(shape, 1)
    col = lane % GROUP
    plane = lane // GROUP
    from_low, from_high = neighbours("gy", ya_ref[...], yb_ref[...])

    def field(f):
        own = jnp.concatenate([s_ref[f], t_ref[f]], axis=0)
        own = jnp.where(col < 2, turn(from_low, -2 * f, 1), own)
        return jnp.where(col >= GROUP - 2, turn(from_high, GROUP - 2 - 2 * f, 1), own)

    row = iota(shape, 0)
    row = jnp.where(row >= width_x + 4, row - size, row)
    place = jnp.where(col < GROUP // 2, col + (width_y - GROUP // 2), col - GROUP // 2)
    place = jnp.where(col < 2, col - 2, place)
    place = jnp.where(col >= GROUP - 2, col + (width_y - GROUP + 2), place)
    rows = (row + gx * width_x).astype(F32)
    cols = (place + gy * width_y).astype(F32)
    inside = within(rows, cols, total_x, total_y)
    damping, coef_h, inverse = edge_coefs(rows, cols, total_x, total_y, inside)
    source = field(6)
    half = GROUP // 2

    def next_col(v):
        jump = (col == 1) | (col == half - 1)
        return jnp.where(jump, turn(v, 1 - half, 1), turn(v, -1, 1))

    def prev_col(v):
        jump = (col == half) | (col == GROUP - 2)
        return jnp.where(jump, turn(v, half - 1, 1), turn(v, 1, 1))

    filtered = turn(source, 1, 0) + 2.0 * source + turn(source, size - 1, 0)
    filtered = (prev_col(filtered) + 2.0 * filtered + next_col(filtered)) / 16.0
    design, slope = design_terms(filtered)
    choices = [jnp.tile(c, (size // SUB, 1)) for c in table_inverse(table, (SUB, LANES))]
    layer = (plane >= ZLO) & (plane < ZLO + PLANES)
    coef_e = jnp.where(layer, design, pick(source, choices)) * inverse
    e = [field(c) for c in range(3)]
    h = [field(3 + c) for c in range(3)]
    top = plane == planes_z - 1
    bottom = plane == 0

    def dxf(v):
        return turn(v, size - 1, 0) - v

    def dyf(v):
        return next_col(v) - v

    def dzf(v):
        return jnp.where(top, 0.0, turn(v, LANES - GROUP, 1)) - v

    def dxb(v):
        return v - turn(v, 1, 0)

    def dyb(v):
        return v - prev_col(v)

    def dzb(v):
        return v - jnp.where(bottom, 0.0, turn(v, GROUP, 1))

    steps = []
    for _ in range(STEPS):
        curl = (dyf(e[2]) - dzf(e[1]), dzf(e[0]) - dxf(e[2]), dxf(e[1]) - dyf(e[0]))
        h = [damping * v - coef_h * c for v, c in zip(h, curl)]
        curl = (dyb(h[2]) - dzb(h[1]), dzb(h[0]) - dxb(h[2]), dxb(h[1]) - dyb(h[0]))
        e = [damping * v + coef_e * c for v, c in zip(e, curl)]
        steps.append(e)
    return steps, h, slope


def slot_of(param, rows_mine):
    gx, gy = lax.axis_index("gx"), lax.axis_index("gy")
    count_gx, count_gy = lax.axis_size("gx"), lax.axis_size("gy")
    owner = lax.div(param, jnp.int32(rows_mine))
    row = param - owner * rows_mine
    ox = lax.div(owner, jnp.int32(count_gy))
    oy = owner - ox * count_gy
    core = (oy ^ gy) & 1
    near = ((ox & 1) + 2 * (oy >> 1)) ^ ((gx & 1) + 2 * (gy >> 1))
    far = (ox >> 1) ^ (gx >> 1)
    return ((core * count_gy + near) * (count_gx // 2) + far) * rows_mine + row


def gradient(
    s_ref, t_ref, ya_ref, yb_ref, xa_ref, xb_ref, table, map_ref, e1_ref, e2_ref, xe1_ref, xe2_ref,
    sl_ref, xsl_ref, sum_ref, g_ref, buf_ref, ye_ref, yh_ref, ye1, lpad, vpad, gpad,
):
    width_x, width_y = sl_ref.shape
    tiles_x, tiles_y = width_x // TILE, width_y // TILE

    def scalar(row, lane):
        here = iota(row.shape, 1) == lane
        return jnp.max(jnp.where(here, row, 0.0)).astype(jnp.int32)

    id_x, id_y = {}, {}
    for k, tile in enumerate(neighbours("gx", xa_ref[TILES - 1], xb_ref[TILES - 1])):
        for t in range(tiles_y):
            u = t * TILE // LANES * LANES
            id_x[k, t] = scalar(tile[1:2, u : u + LANES], t * TILE - u)
    for row in [tx * TILE for tx in range(tiles_x)] + [width_x, width_x + SUB - 1]:
        first = row // SUB * SUB
        here = pl.ds(first, SUB)
        for k, tile in enumerate(neighbours("gy", ya_ref[here], yb_ref[here])):
            id_y[k, row] = scalar(tile[row - first : row - first + 1], GROUP - 1 - k)
    steps, h, slope_y = strips_y(width_x, width_y, s_ref, t_ref, ya_ref, yb_ref, table)
    for c in range(3):
        ye_ref[c] = steps[-1][c]
        yh_ref[c] = h[c]
        ye1[c] = steps[0][c]
    ye1[3] = slope_y
    pad = 2 * SUB
    lpad[pl.ds(0, pad)] = jnp.zeros((pad, width_y), F32)
    lpad[pl.ds(pad + width_x, pad)] = jnp.zeros((pad, width_y), F32)
    buf_ref[...] = jnp.zeros(buf_ref.shape, F32)
    for start in range(0, width_x, SUB):
        here = pl.ds(start, SUB)
        total = sum_ref[here]
        for c in range(3):
            for p in range(PLANES):
                first = patch_rows(e1_ref[c, p, here], xe1_ref.at[c, p], start, width_x)
                first = patch_cols(first, ye1[c, here], ZLO + p)
                second = e2_ref[c, ZLO + p - LO, here]
                second = patch_rows(second, xe2_ref.at[c, ZLO + p], start, width_x)
                second = patch_cols(second, ye_ref[c, here], ZLO + p)
                total = total + g_ref[0, c, p, here] * first + g_ref[1, c, p, here] * second
        slope = patch_rows(sl_ref[here], xsl_ref, start, width_x)
        slope = patch_cols(slope, ye1[3, here], ZLO)
        lpad[pl.ds(pad + start, SUB)] = (grad_scale * (eps_high - eps_low)) * slope * total
    lane = iota((SUB, width_y), 1)
    for start in range(SUB, pad + width_x + SUB, SUB):
        v = lpad[pl.ds(start - 1, SUB)] + 2.0 * lpad[pl.ds(start, SUB)] + lpad[pl.ds(start + 1, SUB)]
        v = v / 16.0
        left = jnp.where(lane == 0, 0.0, turn(v, 1, 1))
        right = jnp.where(lane == width_y - 1, 0.0, turn(v, width_y - 1, 1))
        g = left + 2.0 * v + right
        for u in range(width_y // LANES):
            vpad[u, pl.ds(start, SUB)] = v[:, u * LANES : (u + 1) * LANES]
            gpad[u, pl.ds(start, SUB)] = g[:, u * LANES : (u + 1) * LANES]

    half = LANES // 2
    lines = TILE // 2
    devices = lax.axis_size("gx") * lax.axis_size("gy")
    rows_mine = buf_ref.shape[0] // devices
    lane = iota((lines, LANES), 1)
    lane8 = iota((SUB, LANES), 1)
    sub8 = iota((SUB, LANES), 0)

    def add_tile(param, values):
        slot = slot_of(param, rows_mine)
        buf_ref[slot] = buf_ref[slot] + values

    def add_rows(ident, start, values):
        slot = slot_of(jnp.maximum(ident - 1, 0), rows_mine)
        rows = pl.ds(start, SUB)
        buf_ref[slot, rows] = buf_ref[slot, rows] + jnp.where(ident > 0, values, 0.0)

    for tx in range(tiles_x):
        for u in range(width_y // LANES):
            even = gpad[u, pl.ds(pad + tx * TILE, lines, stride=2)]
            odd = gpad[u, pl.ds(pad + tx * TILE + 1, lines, stride=2)]
            add_tile(map_ref[tx, 2 * u], jnp.where(lane < half, even, turn(odd, half, 1)))
            add_tile(map_ref[tx, 2 * u + 1], jnp.where(lane < half, turn(even, half, 1), odd))
    before, after = pl.ds(pad - SUB, SUB), pl.ds(pad + width_x, SUB)
    for t in range(tiles_y):
        u, odd = divmod(t, 2)
        top, low = gpad[u, before], gpad[u, after]
        top = top if odd else turn(top, half, 1)
        low = turn(low, half, 1) if odd else low
        keep = (sub8 == SUB - 1) & (lane8 >= half)
        add_rows(id_x[0, t], lines - SUB, jnp.where(keep, top, 0.0))
        keep = (sub8 == 0) & (lane8 < half)
        add_rows(id_x[1, t], 0, jnp.where(keep, low, 0.0))
    end = width_y // LANES - 1
    for tx in range(tiles_x):
        even, odd = (pl.ds(pad + tx * TILE + k, lines, stride=2) for k in (0, 1))
        left = jnp.where(lane == half - 1, turn(vpad[0, even], half - 1, 1), 0.0)
        left = jnp.where(lane == LANES - 1, turn(vpad[0, odd], LANES - 1, 1), left)
        right = jnp.where(lane == 0, turn(vpad[end, even], 1, 1), 0.0)
        right = jnp.where(lane == half, turn(vpad[end, odd], half + 1, 1), right)
        for ahead, values in ((False, left), (True, right)):
            owner = id_y[ahead, tx * TILE]
            add_tile(jnp.maximum(owner - 1, 0), jnp.where(owner > 0, values, 0.0))
    tail = width_x + SUB - 1
    corners = (
        (SUB - 1, False, tail, before, lines - SUB, LANES - 1),
        (SUB - 1, True, tail, before, lines - SUB, half),
        (0, False, width_x, after, 0, half - 1),
        (0, True, width_x, after, 0, 0),
    )
    for sub, ahead, row, rows, start, target in corners:
        keep = (sub8 == sub) & (lane8 == target)
        values = vpad[end, rows] if ahead else vpad[0, rows]
        values = turn(values, target - (LANES - 1 if ahead else 0), 1)
        add_rows(id_y[ahead, row], start, jnp.where(keep, values, 0.0))


def merge(e_ref, h_ref, em, hm, xe_ref, xh_ref, ye_ref, yh_ref, eo_ref, ho_ref, out, sems):
    _, planes_z, width_x, _ = e_ref.shape
    parts = (
        (e_ref, em, xe_ref, ye_ref, eo_ref, LO + 2, HI - 1),
        (h_ref, hm, xh_ref, yh_ref, ho_ref, LO + 1, HI - 1),
    )
    half = planes_z // 2

    def send(n, c, k):
        rows = pl.ds(k * half, half)
        return pltpu.make_async_copy(out.at[n, c, rows], parts[n][4].at[c, rows], sems.at[n, c, k])

    def body(c, _):
        for n, (rest, mid, xs, ys, _, low, high) in enumerate(parts):
            for z in range(planes_z):
                src = mid.at[c, z - LO] if low <= z < high else rest.at[c, z]
                for start in range(0, width_x, SUB):
                    here = pl.ds(start, SUB)
                    values = patch_rows(src[here], xs.at[c, z], start, width_x)
                    out[n, c, z, here] = patch_cols(values, ys[c, here], z)
                if z % half == half - 1:
                    send(n, c, z // half).start()
        return 0

    lax.fori_loop(0, 3, body, 0)
    for n in range(2):
        for c in range(3):
            for k in range(2):
                send(n, c, k).wait()


def first_sum(parts, buf_ref, got_ref, *outs):
    size = outs[0].shape[0]
    for k in range(parts):
        rows = pl.ds(k * size, size)
        outs[k][...] = buf_ref[rows] + got_ref[rows]


def second_sum(parts, rows_mine, *refs):
    ins, outs = refs[:parts], refs[parts + 1 :]
    for k, out in enumerate(outs):
        rows = pl.ds(k * rows_mine, rows_mine)
        out[...] = sum(ref[rows] for ref in ins[1:]) + ins[0][rows]


def pair(block, partner, spare=None):
    count_gx, count_gy = lax.axis_size("gx"), lax.axis_size("gy")
    route = []
    for i in range(count_gx):
        for j in range(count_gy):
            a, b = partner(i, j)
            if not (0 <= a < count_gx and 0 <= b < count_gy):
                a, b = spare(i, j)
            route.append((i * count_gy + j, a * count_gy + b))
    return lax.ppermute(block, ("gx", "gy"), route)


def after(k):
    return ((k + 1) ^ 1) - 1


def on_device(e_adj, h_adj, density, material, eps_table, dft_adj, dft_fwd, tile_map):
    planes_z, width_x, width_y = material.shape
    count_gx, count_gy = lax.axis_size("gx"), lax.axis_size("gy")
    block = 4 * width_x * width_y
    assert planes_z == SUB
    face = struct(TILES, SUB, width_y)
    xa, xb = pl.pallas_call(
        pack_x,
        out_shape=(face, face),
        in_specs=[HBM] * 5,
        out_specs=(VMEM,) * 2,
        scratch_shapes=[
            pltpu.VMEM((width_y // LANES, 3 * planes_z * 2 * SUB, LANES), F32),
            pltpu.VMEM((width_y // LANES, 3 * planes_z * 2 * SUB, LANES), F32),
            pltpu.VMEM((width_y // LANES, planes_z * 2 * SUB, LANES), jnp.int32),
            pltpu.VMEM((2 * SUB, width_y), F32),
            pltpu.SMEM(tile_map.shape, jnp.int32),
            pltpu.SemaphoreType.DMA((6 * width_y // LANES + 3,)),
        ],
        compiler_params=params(62300000),
        name="pack_x",
    )(e_adj, h_adj, material, density, tile_map)
    xa = pair(xa, lambda i, j: (i ^ 1, j))
    xb = pair(xb, lambda i, j: (after(i), j), lambda i, j: (i, j ^ 1))
    strip = pl.pallas_call(
        build_strips,
        out_shape=struct(8, width_x, LANES),
        in_specs=[VMEM] * 4 + [SMEM],
        out_specs=VMEM,
        compiler_params=params(),
        cost_estimate=cost(1, 1),
        name="build_strips",
    )(e_adj, h_adj, material, density, tile_map)

    rows = 2 * SUB
    moved = struct(width_x, width_y), struct(STEPS, 3, PLANES, width_x, width_y)
    base, weight = pl.pallas_call(
        transform,
        grid=(width_x // rows,),
        out_shape=moved,
        in_specs=[pl.BlockSpec((FREQ, 2, 3, PLANES, rows, width_y), lambda i: (0, 0, 0, 0, i, 0))] * 2,
        out_specs=(
            pl.BlockSpec((rows, width_y), lambda i: (i, 0)),
            pl.BlockSpec((STEPS, 3, PLANES, rows, width_y), lambda i: (0, 0, 0, i, 0)),
        ),
        compiler_params=params(),
        cost_estimate=cost(1, 1),
        name="transform",
    )(dft_adj, dft_fwd)
    plane = struct(width_x, width_y)
    middle = struct(3, HI - LO, width_x, width_y)
    full = struct(3, planes_z, width_x, width_y)
    em, hm, e1, slope, damp, ch, ce = pl.pallas_call(
        interior_first,
        out_shape=(middle, middle, struct(3, PLANES, width_x, width_y))
        + (plane,) * 3
        + (struct(HI - LO, width_x, width_y),),
        in_specs=[VMEM] * 4 + [SMEM],
        out_specs=(VMEM,) * 7,
        compiler_params=params(),
        cost_estimate=cost(1, 1),
        name="interior_first",
    )(e_adj, h_adj, material, density, eps_table)
    e2, h2, done = pl.pallas_call(
        interior_rest,
        out_shape=(full, full, struct(SUB, LANES)),
        in_specs=[VMEM] * 3 + [SMEM] + [VMEM] * 5,
        out_specs=(VMEM,) * 3,
        scratch_shapes=[pltpu.VMEM((planes_z, width_x, width_y), F32)],
        compiler_params=params(),
        cost_estimate=cost(1, 1),
        name="interior_rest",
    )(e_adj, h_adj, material, eps_table, em, hm, damp, ch, ce)

    tails, ya, yb = pl.pallas_call(
        pack_y,
        out_shape=(struct(8, SUB, LANES),) + (struct(width_x + SUB, LANES),) * 2,
        in_specs=[VMEM] * 3 + [ANY],
        out_specs=(VMEM,) * 3,
        compiler_params=params(),
        name="pack_y",
    )(strip, xa, xb, slope)
    ya = pair(ya, lambda i, j: (i, j ^ 1))
    yb = pair(yb, lambda i, j: (i, after(j)), lambda i, j: (i ^ 1, j))
    xe2, xh2, xe1, xslope = pl.pallas_call(
        strips_x,
        out_shape=(
            struct(3, planes_z, 2, SUB, width_y),
            struct(3, planes_z, 2, SUB, width_y),
            struct(3, PLANES, 2, SUB, width_y),
            struct(2, SUB, width_y),
        ),
        in_specs=[VMEM] * 4 + [SMEM] + [VMEM] * 2,
        out_specs=(VMEM,) * 4,
        scratch_shapes=[
            pltpu.VMEM((2, 3, planes_z + 1, SUB, width_y), F32),
            pltpu.VMEM((2, 3, planes_z + 1, SUB, width_y), F32),
            pltpu.VMEM((2, planes_z, SUB, width_y), F32),
        ],
        compiler_params=params(),
        cost_estimate=cost(1, 1),
        name="strips_x",
    )(e_adj, h_adj, material, density, eps_table, xa, xb)

    devices = count_gx * count_gy
    rows_mine = (width_x // TILE) * (width_y // TILE) // REPEAT
    lines = TILE // 2
    padded = width_x + 4 * SUB
    buf, ye2, yh2 = pl.pallas_call(
        gradient,
        out_shape=(struct(devices * rows_mine, lines, LANES),)
        + (struct(3, width_x + SUB, LANES),) * 2,
        in_specs=[VMEM] * 6 + [SMEM] * 2 + [VMEM] * 8,
        out_specs=(VMEM,) * 3,
        scratch_shapes=[
            pltpu.VMEM((4, width_x + SUB, LANES), F32),
            pltpu.VMEM((padded, width_y), F32),
            pltpu.VMEM((width_y // LANES, padded, LANES), F32),
            pltpu.VMEM((width_y // LANES, padded, LANES), F32),
        ],
        compiler_params=params(),
        cost_estimate=cost(1, 1),
        name="gradient",
    )(strip, tails, ya, yb, xa, xb, eps_table, tile_map, e1, em, xe1, xe2, slope, xslope, base, weight)

    half = devices * rows_mine // 2
    far = count_gx // 2
    got = pair(buf[half:], lambda i, j: (i, j ^ 1))
    parts = pl.pallas_call(
        lambda *refs: first_sum(count_gy, *refs),
        out_shape=(struct(far * rows_mine, lines, LANES),) * count_gy,
        in_specs=[VMEM] * 2,
        out_specs=(VMEM,) * count_gy,
        compiler_params=params(),
        name="first_sum",
    )(buf, got)
    parts = [parts[0]] + [
        pair(parts[k], lambda i, j: (i ^ (k & 1), j ^ (k >> 1 << 1))) for k in range(1, count_gy)
    ]
    e_out, h_out = pl.pallas_call(
        merge,
        out_shape=(full,) * 2,
        in_specs=[VMEM] * 8,
        out_specs=(HBM,) * 2,
        scratch_shapes=[
            pltpu.VMEM((2, 3, planes_z, width_x, width_y), F32),
            pltpu.SemaphoreType.DMA((2, 3, 2)),
        ],
        compiler_params=params(),
        cost_estimate=cost(1, 1),
        name="merge",
    )(e2, h2, em, hm, xe2, xh2, ye2, yh2)
    parts = pl.pallas_call(
        lambda *refs: second_sum(count_gy, rows_mine, *refs),
        out_shape=(struct(rows_mine, lines, LANES),) * far,
        in_specs=[VMEM] * count_gy + [ANY],
        out_specs=(VMEM,) * far,
        compiler_params=params(),
        name="second_sum",
    )(*parts, done)
    parts = [parts[0]] + [pair(parts[k], lambda i, j: (i ^ (k << 1), j)) for k in range(1, far)]
    param_grad = sum(parts[1:], parts[0]).reshape(rows_mine, TILE * TILE)

    return e_out, h_out, param_grad


def solution(mesh):
    in_specs = (
        P(None, None, "gx", "gy"),
        P(None, None, "gx", "gy"),
        P("gx", "gy"),
        P(None, "gx", "gy"),
        P(),
        P(None, None, None, None, "gx", "gy"),
        P(None, None, None, None, "gx", "gy"),
        P("gx", "gy"),
    )
    out_specs = (P(None, None, "gx", "gy"), P(None, None, "gx", "gy"), P(("gx", "gy"), None))
    return jax.shard_map(
        on_device, mesh=mesh, in_specs=in_specs, out_specs=out_specs, check_vma=False
    )
```

```python
import math

import jax
import jax.numpy as jnp
from jax import lax
from jax.experimental import pallas as pl
from jax.experimental.pallas import tpu as pltpu
from jax.sharding import PartitionSpec as P

PLANES = 2
ZLO = 3
STEPS = 2
FREQ = 4
PML = 12
TILE = 64
REPEAT = 4

courant = 0.5
sigma_peak = 0.8
dft_weight = 0.5
sharpness = 4.0
threshold = 0.5
eps_low = 2.1
eps_high = 12.1
grad_scale = 0.01

F32 = jnp.float32
LANES = 128
SUB = 8
GROUP = 16
ANY = pl.BlockSpec(memory_space=pl.ANY)
HBM = pl.BlockSpec(memory_space=pltpu.HBM)
VMEM = pl.BlockSpec(memory_space=pltpu.VMEM)
SMEM = pl.BlockSpec(memory_space=pltpu.SMEM)


def params(size=40 * 2**20):
    return pltpu.CompilerParams(vmem_limit_bytes=size)


def struct(*shape, dtype=F32):
    return jax.ShapeDtypeStruct(shape, dtype)


def cost(flops, moved):
    return pl.CostEstimate(flops=int(flops), bytes_accessed=int(moved), transcendentals=0)


def iota(shape, dim):
    return lax.broadcasted_iota(jnp.int32, shape, dim)


def in_design(z):
    return ZLO <= z < ZLO + PLANES


def turn(values, shift, axis):
    size = values.shape[axis]
    shift %= size
    return values if shift == 0 else pltpu.roll(values, shift, axis)


def depth_cubed(places, total):
    depth = jnp.maximum(jnp.maximum(PML - places, places - (total - 1 - PML)), 0.0) / PML
    return depth * depth * depth


def edge_coefs(rows, cols, total_x, total_y, inside=None):
    sigma = sigma_peak * (depth_cubed(rows, total_x) + depth_cubed(cols, total_y))
    inverse = 1.0 / (1.0 + 0.5 * sigma)
    if inside is not None:
        inverse = jnp.where(inside, inverse, 0.0)
    return (1.0 - 0.5 * sigma) * inverse, courant * inverse, inverse


def within(rows, cols, total_x, total_y):
    return (rows >= 0) & (rows < total_x) & (cols >= 0) & (cols < total_y)


def table_inverse(table, rows, cols):
    tiles = [table[k * SUB : (k + 1) * SUB] for k in range(table.shape[0] // SUB)]
    return [jnp.tile(tile, (rows // SUB, cols // LANES)) for tile in tiles]


def pick(index, choices):
    out = jnp.zeros_like(choices[0])
    for k, choice in enumerate(choices):
        out = jnp.where(index == k, choice, out)
    return out


def design_terms(filtered):
    high = math.tanh(sharpness * threshold)
    norm = high + math.tanh(sharpness * (1.0 - threshold))
    bend = jnp.tanh(sharpness * (filtered - threshold))
    eps = eps_low + (eps_high - eps_low) * ((high + bend) / norm)
    return courant / eps, sharpness * (1.0 - bend * bend) / norm


def blur(values):
    rows, cols = values.shape
    summed = turn(values, 1, 0) + 2.0 * values + turn(values, rows - 1, 0)
    return (turn(summed, 1, 1) + 2.0 * summed + turn(summed, cols - 1, 1)) / 16.0


def id_row(tile_map, tx, shape):
    lane = iota(shape, len(shape) - 1)
    out = jnp.zeros(shape, F32)
    for t in range(tile_map.shape[1]):
        out = jnp.where(lane // TILE == t, (tile_map[tx, t] + 1).astype(F32), out)
    return out


TILES = 10
BEHIND = (0, 1, 2, 4, 5)


def pack_x(
    e_in, h_in, m_in, d_in, map_in, table_in,
    a_ref, b_ref, id_ref, inverse_ref, eb, hb, mb, db, map_ref, table_ref, sems,
):
    planes_z, size, width_y = m_in.shape
    span = 2 * SUB
    tiles = width_y // LANES
    views = [
        (e_in, eb.reshape(tiles, 3, planes_z, span, LANES)),
        (h_in, hb.reshape(tiles, 3, planes_z, span, LANES)),
        (m_in, mb.reshape(tiles, planes_z, span, LANES)),
    ]
    copies = []
    for k, start in enumerate((0, size - SUB)):
        here, there = pl.ds(start, SUB), pl.ds(k * SUB, SUB)
        for u in range(tiles):
            lanes = pl.ds(u * LANES, LANES)
            for n, (src, dst) in enumerate(views):
                source = src.at[:, here, lanes] if n == 2 else src.at[:, :, here, lanes]
                target = dst.at[u, :, there] if n == 2 else dst.at[u, :, :, there]
                copies.append(pltpu.make_async_copy(source, target, sems.at[len(copies)]))
        copies.append(pltpu.make_async_copy(d_in.at[here], db.at[there], sems.at[len(copies)]))
    copies.append(pltpu.make_async_copy(map_in, map_ref, sems.at[len(copies)]))
    copies.append(pltpu.make_async_copy(table_in, table_ref, sems.at[len(copies)]))
    for copy in copies:
        copy.start()
    gx, gy = lax.axis_index("gx"), lax.axis_index("gy")
    total_x, total_y = size * lax.axis_size("gx"), width_y * lax.axis_size("gy")
    shape = (SUB, width_y)
    sub = iota(shape, 0)
    rows = jnp.full(shape, (gx + 1) * size - 2, jnp.int32).astype(F32)
    cols = (iota(shape, 1) + gy * width_y).astype(F32)
    damping, coef_h, _ = edge_coefs(rows, cols, total_x, total_y)
    layer = (sub >= ZLO) & (sub < ZLO + PLANES)
    for copy in copies:
        copy.wait()

    def row(ref, c, r):
        rows = pl.ds(c * planes_z * span + r, planes_z, stride=span)
        return jnp.concatenate([ref[u, rows] for u in range(tiles)], axis=1)

    near, far = span - 1, span - 2
    ex, ey, ez = (row(eb, c, far) for c in range(3))
    up = jnp.where(sub == SUB - 1, 0.0, turn(ex, SUB - 1, 0))
    curl_y = (up - ex) - (row(eb, 2, near) - ez)
    curl_z = (row(eb, 1, near) - ey) - (turn(ex, width_y - 1, 1) - ex)
    mag = [row(hb, c, far) for c in (1, 2)]
    high = [row(eb, c, near) for c in range(3)] + [row(hb, c, near) for c in range(3)]
    high += [damping * h - coef_h * curl for h, curl in zip(mag, (curl_y, curl_z))]
    low = [row(eb, c, 0) for c in range(3)] + [row(hb, c, 0) for c in range(3)]
    low += [row(eb, 1, 1), row(eb, 2, 1)]
    for side, edge, further, tx in ((low, 0, 1, 0), (high, near, far, map_ref.shape[0] - 1)):
        density = jnp.broadcast_to(db[edge : edge + 1], shape)
        side.append(jnp.where(layer, density, row(mb, 0, edge).astype(F32)))
        misc = jnp.broadcast_to(db[further : further + 1], shape)
        side.append(jnp.where(sub == 1, id_row(map_ref, tx, shape), misc))
    strips = [row_to_strip(v) for v in [ex, ey, ez] + mag]
    strips.append(strips[-1])
    for k in range(3):
        pair_of = jnp.concatenate([strips[2 * k], strips[2 * k + 1]], axis=1)
        high[-1] = jnp.where(sub == 2 + k, jnp.broadcast_to(pair_of, shape), high[-1])
    even = gx % 2 == 0
    for k in range(TILES):
        a_ref[k] = jnp.where(even, high[k], low[k])
        b_ref[k] = jnp.where(even, low[k], high[k])
    for tx in range(map_ref.shape[0]):
        id_ref[pl.ds(tx * SUB, SUB)] = id_row(map_ref, tx, shape)
    for k in range(table_ref.shape[0]):
        inverse_ref[pl.ds(k * SUB, SUB)] = courant / jnp.full((SUB, LANES), table_ref[k], F32)


def neighbours(axis, from_a, from_b):
    here = lax.axis_index(axis)
    even = here % 2 == 0
    before = jnp.where(here > 0, jnp.where(even, from_b, from_a), 0.0)
    after = jnp.where(here < lax.axis_size(axis) - 1, jnp.where(even, from_a, from_b), 0.0)
    return before, after


def x_halos(xa_ref, xb_ref):
    both = [neighbours("gx", xa_ref[k], xb_ref[k]) for k in range(TILES)]
    return [t[0] for t in both], [t[1] for t in both]


def ends(values):
    lane = iota((values.shape[0], LANES), 1)
    return jnp.where(lane < LANES // 2, values[:, :LANES], values[:, -LANES:])


def row_to_strip(values):
    shape = (SUB, LANES)
    rolled = pltpu.roll(ends(values), GROUP // 2, 1, stride=GROUP, stride_axis=0)
    rolled = jnp.where(iota(shape, 1) // GROUP == iota(shape, 0), rolled, 0.0)
    return jnp.sum(rolled, axis=0, keepdims=True)


def build_strips(e_ref, h_ref, m_ref, d_ref, id_ref, s_ref):
    planes_z, width_x, width_y = m_ref.shape
    group = iota((SUB, LANES), 1) // GROUP

    def gather(get, here):
        acc = jnp.zeros((SUB, LANES), F32)
        for z in range(planes_z):
            acc = jnp.where(group == z, turn(ends(get(z, here)), z * GROUP + GROUP // 2, 1), acc)
        return acc

    def body(c, _):
        for base, ref in ((0, e_ref), (3, h_ref)):
            for start in range(0, width_x, SUB):
                here = pl.ds(start, SUB)
                s_ref[base + c, here] = gather(lambda z, here: ref[c, z, here], here)
        return 0

    lax.fori_loop(0, 3, body, 0)

    def source(z, here):
        return d_ref[here] if in_design(z) else m_ref[z, here].astype(F32)

    for start in range(0, width_x, SUB):
        here = pl.ds(start, SUB)
        s_ref[6, here] = gather(source, here)
        row = id_ref[pl.ds(start // TILE * SUB, SUB)]
        s_ref[7, here] = turn(ends(row), GROUP // 2, 1)


def pack_y(s_ref, xa_ref, xb_ref, _after, t_ref, a_ref, b_ref):
    width_x = s_ref.shape[1]
    even_y = lax.axis_index("gy") % 2 == 0
    below, above = x_halos(xa_ref, xb_ref)
    shape = (SUB, LANES)
    sub = iota(shape, 0)

    def row(tile, k):
        return jnp.broadcast_to(tile[k : k + 1], tile.shape)

    def wide(values):
        return jnp.broadcast_to(values, shape)

    zero = jnp.zeros(shape, F32)
    tails = []
    for f in range(8):
        if f < 7:
            k = 8 if f == 6 else f
            after_1, before_1 = (wide(row_to_strip(side[k])) for side in (above, below))
        else:
            after_1, before_1 = (wide(row_to_strip(row(side[9], 1))) for side in (above, below))
        after_2, before_2 = zero, zero
        if f in (1, 2):
            after_2 = wide(row_to_strip(above[5 + f]))
        if f in BEHIND:
            k = BEHIND.index(f)
            lanes = (k % 2) * LANES
            before_2 = wide(below[9][2 + k // 2 : 3 + k // 2, lanes : lanes + LANES])
        if f == 6:
            after_2, before_2 = (wide(row_to_strip(row(side[9], 0))) for side in (above, below))
        tail = jnp.where(sub == 0, after_1, jnp.where(sub == 1, after_2, 0.0))
        tail = jnp.where(sub == 6, before_2, jnp.where(sub == 7, before_1, tail))
        t_ref[f] = tail
        tails.append(tail)
    lane = iota(shape, 1) % GROUP
    for start in range(0, width_x + SUB, SUB):
        low = zero
        high = zero
        for f in range(8):
            values = tails[f] if start == width_x else s_ref[f, pl.ds(start, SUB)]
            mask = lane // 2 == f
            low = jnp.where(mask, turn(values, 2 * f - GROUP // 2, 1), low)
            high = jnp.where(mask, turn(values, 2 * f - (GROUP // 2 - 2), 1), high)
        a_ref[pl.ds(start, SUB)] = jnp.where(even_y, high, low)
        b_ref[pl.ds(start, SUB)] = jnp.where(even_y, low, high)


def transform(adj_ref, fwd_ref, s_ref, g_ref):
    rows = 2 * SUB

    def body(k, _):
        here = pl.ds(pl.multiple_of(k * rows, rows), rows)
        total = None
        for c in range(3):
            for p in range(PLANES):
                parts = [None] * STEPS
                for f in range(FREQ):
                    real = fwd_ref[f, 0, c, p, here].astype(F32)
                    imag = fwd_ref[f, 1, c, p, here].astype(F32)
                    term = real * adj_ref[f, 0, c, p, here] - imag * adj_ref[f, 1, c, p, here]
                    total = term if total is None else total + term
                    for n in range(STEPS):
                        angle = (0.21 + 0.06 * f) * (n + 1)
                        term = (dft_weight * math.cos(angle)) * real + (
                            dft_weight * math.sin(angle)
                        ) * imag
                        parts[n] = term if parts[n] is None else parts[n] + term
                for n in range(STEPS):
                    g_ref[n, c, p, here] = parts[n]
        s_ref[here] = total
        return 0

    lax.fori_loop(0, s_ref.shape[0] // rows, body, 0)


LO = ZLO - STEPS
HI = ZLO + PLANES + STEPS - 1


def update_mag(e, e_up, h, out, damp, ch):
    width_x, width_y = damp.shape
    for start in range(0, width_x, SUB):
        here = pl.ds(start, SUB)

        def ahead(c, tile):
            if start + SUB < width_x:
                return e(c)[pl.ds(start + 1, SUB)]
            return turn(tile, SUB - 1, 0)

        ex, ey, ez = (e(c)[here] for c in range(3))
        up_x = e_up(0)[here] - ex if e_up else -ex
        up_y = e_up(1)[here] - ey if e_up else -ey
        cx = (turn(ez, width_y - 1, 1) - ez) - up_y
        cy = up_x - (ahead(2, ez) - ez)
        cz = (ahead(1, ey) - ey) - (turn(ex, width_y - 1, 1) - ex)
        dm, cf = damp[here], ch[here]
        for c, curl in enumerate((cx, cy, cz)):
            out(c)[here] = dm * h(c)[here] - cf * curl


def update_elec(h, h_down, e, out, damp, ce):
    width_x, width_y = damp.shape
    for start in range(0, width_x, SUB):
        here = pl.ds(start, SUB)

        def behind(c, tile):
            return h(c)[pl.ds(start - 1, SUB)] if start else turn(tile, 1, 0)

        hx, hy, hz = (h(c)[here] for c in range(3))
        up_x = hx - h_down(0)[here] if h_down else hx
        up_y = hy - h_down(1)[here] if h_down else hy
        cx = (hz - turn(hz, 1, 1)) - up_y
        cy = up_x - (hz - behind(2, hz))
        cz = (hy - behind(1, hy)) - (hx - turn(hx, 1, 1))
        dm, cf = damp[here], ce[here]
        for c, curl in enumerate((cx, cy, cz)):
            out(c)[here] = dm * e(c)[here] + cf * curl


def at(ref, z):
    return lambda c: ref.at[c, z]


def fill_ce(ce, k, z, m_ref, choices, ch):
    for start in range(0, ch.shape[0], SUB):
        here = pl.ds(start, SUB)
        ce[k, here] = pick(m_ref[z, here], choices) * (ch[here] * (1.0 / courant))


def interior_first(e_ref, h_ref, m_ref, d_ref, table, em, hm, e1_ref, sl_ref, damp, ch, ce):
    planes_z, width_x, width_y = m_ref.shape
    gx, gy = lax.axis_index("gx"), lax.axis_index("gy")
    total_x, total_y = width_x * lax.axis_size("gx"), width_y * lax.axis_size("gy")
    shape = (width_x, width_y)
    rows = (iota(shape, 0) + gx * width_x).astype(F32)
    cols = (iota(shape, 1) + gy * width_y).astype(F32)
    damping, coef_h, inverse = edge_coefs(rows, cols, total_x, total_y)
    damp[...] = damping
    ch[...] = coef_h
    design, slope = design_terms(blur(d_ref[...]))
    sl_ref[...] = slope
    choices = table_inverse(table, SUB, width_y)
    for z in range(LO, HI):
        if in_design(z):
            ce[z - LO] = design * inverse
        elif z > LO:
            fill_ce(ce, z - LO, z, m_ref, choices, ch)

    def e(z):
        return at(em, z - LO)

    def h(z):
        return at(hm, z - LO)

    for z in range(LO, HI):
        update_mag(at(e_ref, z), at(e_ref, z + 1), at(h_ref, z), h(z), damp, ch)
    for z in range(LO + 1, HI):
        update_elec(h(z), h(z - 1), at(e_ref, z), e(z), damp, ce.at[z - LO])
    for c in range(3):
        for p in range(PLANES):
            e1_ref[c, p] = em[c, ZLO + p - LO]
    for z in range(LO + 1, HI - 1):
        update_mag(e(z), e(z + 1), h(z), h(z), damp, ch)
    for z in range(LO + 2, HI - 1):
        update_elec(h(z), h(z - 1), e(z), e(z), damp, ce.at[z - LO])


def interior_rest(e_ref, h_ref, m_ref, table, em, hm, damp, ch, ce, e2, h2, done, ce2):
    planes_z, width_x, width_y = m_ref.shape
    choices = table_inverse(table, SUB, width_y)
    done[...] = jnp.zeros(done.shape, F32)
    rest = [z for z in range(planes_z) if not LO < z < HI]
    for z in rest:
        fill_ce(ce2, z, z, m_ref, choices, ch)

    def coef(z):
        return ce.at[z - LO] if LO < z < HI else ce2.at[z]

    def e1(z):
        return at(em, z - LO) if LO < z < HI else at(e2, z)

    def h1(z):
        return at(hm, z - LO) if LO <= z < HI else at(h2, z)

    def h_last(z):
        return at(hm, z - LO) if LO < z < HI - 1 else at(h2, z)

    for z in range(planes_z):
        if not LO <= z < HI:
            up = at(e_ref, z + 1) if z + 1 < planes_z else None
            update_mag(at(e_ref, z), up, at(h_ref, z), at(h2, z), damp, ch)
    for z in rest:
        update_elec(h1(z), h1(z - 1) if z else None, at(e_ref, z), at(e2, z), damp, coef(z))
    for z in range(planes_z):
        if not LO < z < HI - 1:
            up = e1(z + 1) if z + 1 < planes_z else None
            update_mag(e1(z), up, h1(z), at(h2, z), damp, ch)
    for z in range(planes_z):
        if not in_design(z):
            down = h_last(z - 1) if z else None
            update_elec(h_last(z), down, e1(z), at(e2, z), damp, coef(z))


def strips_x(
    e_ref, h_ref, m_ref, d_ref, table, xa_ref, xb_ref,
    e2_ref, h2_ref, e1_ref, sl_ref, xe, xh, ce,
):
    planes_z, width_x, width_y = m_ref.shape
    gx, gy = lax.axis_index("gx"), lax.axis_index("gy")
    total_x, total_y = width_x * lax.axis_size("gx"), width_y * lax.axis_size("gy")
    shape = (SUB, width_y)
    sub = iota(shape, 0)
    cols = (iota(shape, 1) + gy * width_y).astype(F32)
    choices = table_inverse(table, SUB, width_y)
    zero = jnp.zeros(shape, F32)
    damps, chs = [], []

    below, above = x_halos(xa_ref, xb_ref)
    edges = pl.ds(0, SUB), pl.ds(width_x - SUB, SUB)

    def place(values, tile, z, at_sub):
        return jnp.where(sub == at_sub, turn(tile, at_sub - z, 0), values)

    def strip(side, own, near, far, z):
        out = turn(own, 2 if side == 0 else 6, 0)
        out = place(out, near, z, 1 if side == 0 else 6)
        if far is None:
            return jnp.where(sub == (0 if side == 0 else 7), 0.0, out)
        return place(out, far[0], far[1], 0 if side == 0 else 7)

    def source(side, z):
        own = d_ref[edges[side]] if in_design(z) else m_ref[z, edges[side]].astype(F32)
        halo = (below, above)[side]
        return strip(side, own, halo[8], (halo[9], 0), z)

    for side in range(2):
        rows = (sub + gx * width_x + (-2 if side == 0 else width_x - 6)).astype(F32)
        inside = within(rows, cols, total_x, total_y)
        damping, coef_h, inverse = edge_coefs(rows, cols, total_x, total_y, inside)
        damps.append(damping)
        chs.append(coef_h)
        for z in range(planes_z):
            for c in range(3):
                halo = (below, above)[side]
                far = (above[5 + c], z) if side and c else None
                xe[side, c, z] = strip(side, e_ref[c, z, edges[side]], halo[c], far, z)
                xh[side, c, z + 1] = strip(side, h_ref[c, z, edges[side]], halo[3 + c], None, z)
        for c in range(3):
            xe[side, c, planes_z] = zero
            xh[side, c, 0] = zero
        design, slope = design_terms(blur(source(side, ZLO)))
        sl_ref[side] = turn(slope, 6 if side == 0 else 2, 0)
        for z in range(planes_z):
            if in_design(z):
                ce[side, z] = design * inverse
            else:
                ce[side, z] = pick(source(side, z), choices) * inverse

    def mag(z):
        for side in range(2):
            ex, ey, ez = (xe[side, c, z] for c in range(3))
            cx = (turn(ez, width_y - 1, 1) - ez) - (xe[side, 1, z + 1] - ey)
            cy = (xe[side, 0, z + 1] - ex) - (turn(ez, SUB - 1, 0) - ez)
            cz = (turn(ey, SUB - 1, 0) - ey) - (turn(ex, width_y - 1, 1) - ex)
            for c, curl in enumerate((cx, cy, cz)):
                xh[side, c, z + 1] = damps[side] * xh[side, c, z + 1] - chs[side] * curl

    def elec(z):
        for side in range(2):
            hx, hy, hz = (xh[side, c, z + 1] for c in range(3))
            cx = (hz - turn(hz, 1, 1)) - (hy - xh[side, 1, z])
            cy = (hx - xh[side, 0, z]) - (hz - turn(hz, 1, 0))
            cz = (hy - turn(hy, 1, 0)) - (hx - turn(hx, 1, 1))
            for c, curl in enumerate((cx, cy, cz)):
                xe[side, c, z] = damps[side] * xe[side, c, z] + ce[side, z] * curl

    def loop(f):
        for z in range(planes_z):
            f(z)

    back = (6, 2)
    for n in range(STEPS):
        loop(mag)
        if n == 0:
            for z in range(planes_z):
                for c in (1, 2):
                    xh[0, c, z + 1] = place(xh[0, c, z + 1], below[5 + c], z, 0)
        loop(elec)
        if n == 0:
            for side in range(2):
                for c in range(3):
                    for p in range(PLANES):
                        e1_ref[c, p, side] = turn(xe[side, c, ZLO + p], back[side], 0)

    def finish(z):
        for side in range(2):
            for c in range(3):
                e2_ref[c, z, side] = turn(xe[side, c, z], back[side], 0)
                h2_ref[c, z, side] = turn(xh[side, c, z + 1], back[side], 0)

    loop(finish)


def patch_rows(values, strip, start, width_x):
    sub = iota(values.shape, 0)
    if start == 0:
        values = jnp.where(sub < 2, strip[0], values)
    if start == width_x - SUB:
        values = jnp.where(sub >= 6, strip[1], values)
    return values


def patch_cols(values, strip, z):
    lane = iota((values.shape[0], LANES), 1)
    rolled = turn(strip, -(z * GROUP + GROUP // 2), 1)
    tiles = [values[:, k : k + LANES] for k in range(0, values.shape[1], LANES)]
    tiles[0] = jnp.where(lane < 2, rolled, tiles[0])
    tiles[-1] = jnp.where(lane >= LANES - 2, rolled, tiles[-1])
    return jnp.concatenate(tiles, axis=1)


def strip_columns(shape):
    lane = iota(shape, 1)
    return lane % GROUP, lane // GROUP


def strip_coefs(width_x, width_y):
    gx, gy = lax.axis_index("gx"), lax.axis_index("gy")
    total_x, total_y = width_x * lax.axis_size("gx"), width_y * lax.axis_size("gy")
    shape = (width_x + SUB, LANES)
    col, _ = strip_columns(shape)
    row = iota(shape, 0)
    row = jnp.where(row >= width_x + 4, row - shape[0], row)
    place = jnp.where(col < GROUP // 2, col + (width_y - GROUP // 2), col - GROUP // 2)
    place = jnp.where(col < 2, col - 2, place)
    place = jnp.where(col >= GROUP - 2, col + (width_y - GROUP + 2), place)
    rows = (row + gx * width_x).astype(F32)
    cols = (place + gy * width_y).astype(F32)
    return edge_coefs(rows, cols, total_x, total_y, within(rows, cols, total_x, total_y))


def design(
    e1_ref, e2_ref, xe1_ref, xe2_ref, sl_ref, xsl_ref, sum_ref, g_ref,
    l_ref, gs_ref, ss_ref, coef_ref,
):
    width_x, width_y = sl_ref.shape
    for k, values in enumerate(strip_coefs(width_x, width_y)):
        coef_ref[k] = values
    group = iota((SUB, LANES), 1) // GROUP
    for start in range(0, width_x, SUB):
        here = pl.ds(start, SUB)
        total = sum_ref[here]
        ss_ref[here] = jnp.where(group == ZLO, turn(ends(total), ZLO * GROUP + GROUP // 2, 1), 0.0)
        for c in range(3):
            strips = [jnp.zeros((SUB, LANES), F32) for _ in range(STEPS)]
            for p in range(PLANES):
                z = ZLO + p
                first = patch_rows(e1_ref[c, p, here], xe1_ref.at[c, p], start, width_x)
                second = patch_rows(e2_ref[c, z - LO, here], xe2_ref.at[c, z], start, width_x)
                weights = [g_ref[n, c, p, here] for n in range(STEPS)]
                total = total + weights[0] * first + weights[1] * second
                for n in range(STEPS):
                    rolled = turn(ends(weights[n]), z * GROUP + GROUP // 2, 1)
                    strips[n] = jnp.where(group == z, rolled, strips[n])
            for n in range(STEPS):
                gs_ref[n, c, here] = strips[n]
        slope = patch_rows(sl_ref[here], xsl_ref, start, width_x)
        l_ref[here] = (grad_scale * (eps_high - eps_low)) * slope * total


def strips_y(s_ref, t_ref, ya_ref, yb_ref, table, coef_ref):
    planes_z = LANES // GROUP
    size = coef_ref.shape[1]
    col, plane = strip_columns((size, LANES))
    from_low, from_high = neighbours("gy", ya_ref[...], yb_ref[...])

    def field(f):
        own = jnp.concatenate([s_ref[f], t_ref[f]], axis=0)
        own = jnp.where(col < 2, turn(from_low, -2 * f, 1), own)
        return jnp.where(col >= GROUP - 2, turn(from_high, GROUP - 2 - 2 * f, 1), own)

    damping, coef_h, inverse = coef_ref[0], coef_ref[1], coef_ref[2]
    source = field(6)
    half = GROUP // 2

    def next_col(v):
        jump = (col == 1) | (col == half - 1)
        return jnp.where(jump, turn(v, 1 - half, 1), turn(v, -1, 1))

    def prev_col(v):
        jump = (col == half) | (col == GROUP - 2)
        return jnp.where(jump, turn(v, half - 1, 1), turn(v, 1, 1))

    filtered = turn(source, 1, 0) + 2.0 * source + turn(source, size - 1, 0)
    filtered = (prev_col(filtered) + 2.0 * filtered + next_col(filtered)) / 16.0
    design, slope = design_terms(filtered)
    choices = table_inverse(table, size, LANES)
    layer = (plane >= ZLO) & (plane < ZLO + PLANES)
    coef_e = jnp.where(layer, design, pick(source, choices)) * inverse
    e = [field(c) for c in range(3)]
    h = [field(3 + c) for c in range(3)]
    top = plane == planes_z - 1
    bottom = plane == 0

    def dxf(v):
        return turn(v, size - 1, 0) - v

    def dyf(v):
        return next_col(v) - v

    def dzf(v):
        return jnp.where(top, 0.0, turn(v, LANES - GROUP, 1)) - v

    def dxb(v):
        return v - turn(v, 1, 0)

    def dyb(v):
        return v - prev_col(v)

    def dzb(v):
        return v - jnp.where(bottom, 0.0, turn(v, GROUP, 1))

    steps = []
    for _ in range(STEPS):
        curl = (dyf(e[2]) - dzf(e[1]), dzf(e[0]) - dxf(e[2]), dxf(e[1]) - dyf(e[0]))
        h = [damping * v - coef_h * c for v, c in zip(h, curl)]
        curl = (dyb(h[2]) - dzb(h[1]), dzb(h[0]) - dxb(h[2]), dxb(h[1]) - dyb(h[0]))
        e = [damping * v + coef_e * c for v, c in zip(e, curl)]
        steps.append(e)
    return steps, h, slope


def slot_of(param, rows_mine):
    gx, gy = lax.axis_index("gx"), lax.axis_index("gy")
    count_gx, count_gy = lax.axis_size("gx"), lax.axis_size("gy")
    owner = lax.div(param, jnp.int32(rows_mine))
    row = param - owner * rows_mine
    ox = lax.div(owner, jnp.int32(count_gy))
    oy = owner - ox * count_gy
    core = (oy ^ gy) & 1
    near = ((ox & 1) + 2 * (oy >> 1)) ^ ((gx & 1) + 2 * (gy >> 1))
    far = (ox >> 1) ^ (gx >> 1)
    return ((core * count_gy + near) * (count_gx // 2) + far) * rows_mine + row


def gradient(
    s_ref, t_ref, ya_ref, yb_ref, xa_ref, xb_ref, table, own_ref, l_ref, gs_ref, ss_ref, coef_ref,
    buf_ref, ye_ref, yh_ref, lpad, vpad, gpad,
):
    width_x, width_y = l_ref.shape
    tiles_x, tiles_y = width_x // TILE, width_y // TILE

    def scalar(row, lane):
        here = iota(row.shape, 1) == lane
        return jnp.max(jnp.where(here, row, 0.0)).astype(jnp.int32)

    id_x, id_y, own = {}, {}, {}
    for tx in range(tiles_x):
        for t in range(tiles_y):
            u = t * TILE // LANES * LANES
            row = own_ref[pl.ds(tx * SUB, 1), pl.ds(u, LANES)]
            own[tx, t] = scalar(row, t * TILE - u) - 1
    for k, tile in enumerate(neighbours("gx", xa_ref[TILES - 1], xb_ref[TILES - 1])):
        for t in range(tiles_y):
            u = t * TILE // LANES * LANES
            id_x[k, t] = scalar(tile[1:2, u : u + LANES], t * TILE - u)
    for row in [tx * TILE for tx in range(tiles_x)] + [width_x, width_x + SUB - 1]:
        first = row // SUB * SUB
        here = pl.ds(first, SUB)
        for k, tile in enumerate(neighbours("gy", ya_ref[here], yb_ref[here])):
            id_y[k, row] = scalar(tile[row - first : row - first + 1], GROUP - 1 - k)
    steps, h, slope_y = strips_y(s_ref, t_ref, ya_ref, yb_ref, table, coef_ref)
    for c in range(3):
        ye_ref[c] = steps[-1][c]
        yh_ref[c] = h[c]
    pad = 2 * SUB
    lpad[pl.ds(0, pad)] = jnp.zeros((pad, width_y), F32)
    lpad[pl.ds(pad + width_x, pad)] = jnp.zeros((pad, width_y), F32)
    buf_ref[...] = jnp.zeros(buf_ref.shape, F32)
    for start in range(0, width_x, SUB):
        here, rows = pl.ds(start, SUB), slice(start, start + SUB)
        total = ss_ref[here]
        for c in range(3):
            for n in range(STEPS):
                total = total + gs_ref[n, c, here] * steps[n][c][rows]
        total = sum((turn(total, -p * GROUP, 1) for p in range(1, PLANES)), total)
        total = (grad_scale * (eps_high - eps_low)) * slope_y[rows] * total
        lpad[pl.ds(pad + start, SUB)] = patch_cols(l_ref[here], total, ZLO)
    lane = iota((SUB, width_y), 1)
    for start in range(SUB, pad + width_x + SUB, SUB):
        v = lpad[pl.ds(start - 1, SUB)] + 2.0 * lpad[pl.ds(start, SUB)] + lpad[pl.ds(start + 1, SUB)]
        v = v / 16.0
        left = jnp.where(lane == 0, 0.0, turn(v, 1, 1))
        right = jnp.where(lane == width_y - 1, 0.0, turn(v, width_y - 1, 1))
        g = left + 2.0 * v + right
        for u in range(width_y // LANES):
            vpad[u, pl.ds(start, SUB)] = v[:, u * LANES : (u + 1) * LANES]
            gpad[u, pl.ds(start, SUB)] = g[:, u * LANES : (u + 1) * LANES]

    half = LANES // 2
    lines = TILE // 2
    devices = lax.axis_size("gx") * lax.axis_size("gy")
    rows_mine = buf_ref.shape[0] // devices
    lane = iota((lines, LANES), 1)
    lane8 = iota((SUB, LANES), 1)
    sub8 = iota((SUB, LANES), 0)

    def add_tile(param, values):
        slot = slot_of(param, rows_mine)
        buf_ref[slot] = buf_ref[slot] + values

    def add_rows(ident, start, values):
        slot = slot_of(jnp.maximum(ident - 1, 0), rows_mine)
        rows = pl.ds(start, SUB)
        buf_ref[slot, rows] = buf_ref[slot, rows] + jnp.where(ident > 0, values, 0.0)

    for tx in range(tiles_x):
        for u in range(width_y // LANES):
            even = gpad[u, pl.ds(pad + tx * TILE, lines, stride=2)]
            odd = gpad[u, pl.ds(pad + tx * TILE + 1, lines, stride=2)]
            add_tile(own[tx, 2 * u], jnp.where(lane < half, even, turn(odd, half, 1)))
            add_tile(own[tx, 2 * u + 1], jnp.where(lane < half, turn(even, half, 1), odd))
    before, after = pl.ds(pad - SUB, SUB), pl.ds(pad + width_x, SUB)
    for t in range(tiles_y):
        u, odd = divmod(t, 2)
        top, low = gpad[u, before], gpad[u, after]
        top = top if odd else turn(top, half, 1)
        low = turn(low, half, 1) if odd else low
        keep = (sub8 == SUB - 1) & (lane8 >= half)
        add_rows(id_x[0, t], lines - SUB, jnp.where(keep, top, 0.0))
        keep = (sub8 == 0) & (lane8 < half)
        add_rows(id_x[1, t], 0, jnp.where(keep, low, 0.0))
    end = width_y // LANES - 1
    for tx in range(tiles_x):
        even, odd = (pl.ds(pad + tx * TILE + k, lines, stride=2) for k in (0, 1))
        left = jnp.where(lane == half - 1, turn(vpad[0, even], half - 1, 1), 0.0)
        left = jnp.where(lane == LANES - 1, turn(vpad[0, odd], LANES - 1, 1), left)
        right = jnp.where(lane == 0, turn(vpad[end, even], 1, 1), 0.0)
        right = jnp.where(lane == half, turn(vpad[end, odd], half + 1, 1), right)
        for ahead, values in ((False, left), (True, right)):
            owner = id_y[ahead, tx * TILE]
            add_tile(jnp.maximum(owner - 1, 0), jnp.where(owner > 0, values, 0.0))
    tail = width_x + SUB - 1
    corners = (
        (SUB - 1, False, tail, before, lines - SUB, LANES - 1),
        (SUB - 1, True, tail, before, lines - SUB, half),
        (0, False, width_x, after, 0, half - 1),
        (0, True, width_x, after, 0, 0),
    )
    for sub, ahead, row, rows, start, target in corners:
        keep = (sub8 == sub) & (lane8 == target)
        values = vpad[end, rows] if ahead else vpad[0, rows]
        values = turn(values, target - (LANES - 1 if ahead else 0), 1)
        add_rows(id_y[ahead, row], start, jnp.where(keep, values, 0.0))


def merge(e_ref, h_ref, em, hm, xe_ref, xh_ref, ye_ref, yh_ref, eo_ref, ho_ref, out, sems):
    _, planes_z, width_x, _ = e_ref.shape
    parts = (
        (e_ref, em, xe_ref, ye_ref, eo_ref, LO + 2, HI - 1),
        (h_ref, hm, xh_ref, yh_ref, ho_ref, LO + 1, HI - 1),
    )
    half = planes_z // 2

    def send(n, c, k):
        rows = pl.ds(k * half, half)
        return pltpu.make_async_copy(out.at[n, c, rows], parts[n][4].at[c, rows], sems.at[n, c, k])

    def body(c, _):
        for n, (rest, mid, xs, ys, _, low, high) in enumerate(parts):
            for z in range(planes_z):
                src = mid.at[c, z - LO] if low <= z < high else rest.at[c, z]
                for start in range(0, width_x, SUB):
                    here = pl.ds(start, SUB)
                    values = patch_rows(src[here], xs.at[c, z], start, width_x)
                    out[n, c, z, here] = patch_cols(values, ys[c, here], z)
                if z % half == half - 1:
                    send(n, c, z // half).start()
        return 0

    lax.fori_loop(0, 3, body, 0)
    for n in range(2):
        for c in range(3):
            for k in range(2):
                send(n, c, k).wait()


def first_sum(parts, buf_ref, got_ref, *outs):
    size = outs[0].shape[0]
    for k in range(parts):
        rows = pl.ds(k * size, size)
        outs[k][...] = buf_ref[rows] + got_ref[rows]


def second_sum(parts, rows_mine, *refs):
    ins, outs = refs[:parts], refs[parts + 1 :]
    for k, out in enumerate(outs):
        rows = pl.ds(k * rows_mine, rows_mine)
        out[...] = sum(ref[rows] for ref in ins[1:]) + ins[0][rows]


def pair(block, partner, spare=None):
    count_gx, count_gy = lax.axis_size("gx"), lax.axis_size("gy")
    route = []
    for i in range(count_gx):
        for j in range(count_gy):
            a, b = partner(i, j)
            if not (0 <= a < count_gx and 0 <= b < count_gy):
                a, b = spare(i, j)
            route.append((i * count_gy + j, a * count_gy + b))
    return lax.ppermute(block, ("gx", "gy"), route)


def after(k):
    return ((k + 1) ^ 1) - 1


def on_device(e_adj, h_adj, density, material, eps_table, dft_adj, dft_fwd, tile_map):
    planes_z, width_x, width_y = material.shape
    count_gx, count_gy = lax.axis_size("gx"), lax.axis_size("gy")
    assert planes_z == SUB
    face = struct(TILES, SUB, width_y)
    xa, xb, own_ids, table = pl.pallas_call(
        pack_x,
        out_shape=(
            pltpu.VMEM(face.shape, F32),
            pltpu.VMEM(face.shape, F32),
            pltpu.VMEM((width_x // TILE * SUB, width_y), F32),
            pltpu.VMEM((eps_table.shape[0] * SUB, LANES), F32),
        ),
        in_specs=[HBM] * 6,
        out_specs=(VMEM,) * 4,
        scratch_shapes=[
            pltpu.VMEM((width_y // LANES, 3 * planes_z * 2 * SUB, LANES), F32),
            pltpu.VMEM((width_y // LANES, 3 * planes_z * 2 * SUB, LANES), F32),
            pltpu.VMEM((width_y // LANES, planes_z * 2 * SUB, LANES), jnp.int32),
            pltpu.VMEM((2 * SUB, width_y), F32),
            pltpu.SMEM(tile_map.shape, jnp.int32),
            pltpu.SMEM(eps_table.shape, F32),
            pltpu.SemaphoreType.DMA((6 * width_y // LANES + 4,)),
        ],
        compiler_params=params(),
        name="pack_x",
    )(
        *(
            pltpu.with_memory_space_constraint(x, pltpu.HBM)
            for x in (e_adj, h_adj, material, density, tile_map, eps_table)
        )
    )
    xa = pair(xa, lambda i, j: (i ^ 1, j))
    xb = pair(xb, lambda i, j: (after(i), j), lambda i, j: (i, j ^ 1))
    strip = pl.pallas_call(
        build_strips,
        out_shape=struct(8, width_x, LANES),
        in_specs=[VMEM] * 5,
        out_specs=VMEM,
        compiler_params=params(),
        cost_estimate=cost(1, 1),
        name="build_strips",
    )(e_adj, h_adj, material, density, own_ids)

    base, weight = pl.pallas_call(
        transform,
        out_shape=(
            struct(width_x, width_y),
            struct(STEPS, 3, PLANES, width_x, width_y),
        ),
        in_specs=[VMEM] * 2,
        out_specs=(VMEM,) * 2,
        compiler_params=params(),
        cost_estimate=cost(1, 1),
        name="transform",
    )(dft_adj, dft_fwd)
    plane = struct(width_x, width_y)
    middle = struct(3, HI - LO, width_x, width_y)
    full = struct(3, planes_z, width_x, width_y)
    em, hm, e1, slope, damp, ch, ce = pl.pallas_call(
        interior_first,
        out_shape=(middle, middle, struct(3, PLANES, width_x, width_y))
        + (plane,) * 3
        + (struct(HI - LO, width_x, width_y),),
        in_specs=[VMEM] * 5,
        out_specs=(VMEM,) * 7,
        compiler_params=params(),
        cost_estimate=cost(1, 1),
        name="interior_first",
    )(e_adj, h_adj, material, density, table)
    e2, h2, done = pl.pallas_call(
        interior_rest,
        out_shape=(full, full, struct(SUB, LANES)),
        in_specs=[VMEM] * 9,
        out_specs=(VMEM,) * 3,
        scratch_shapes=[pltpu.VMEM((planes_z, width_x, width_y), F32)],
        compiler_params=params(),
        cost_estimate=cost(1, 1),
        name="interior_rest",
    )(e_adj, h_adj, material, table, em, hm, damp, ch, ce)

    tails, ya, yb = pl.pallas_call(
        pack_y,
        out_shape=(struct(8, SUB, LANES),) + (struct(width_x + SUB, LANES),) * 2,
        in_specs=[VMEM] * 3 + [ANY],
        out_specs=(VMEM,) * 3,
        compiler_params=params(),
        name="pack_y",
    )(strip, xa, xb, slope)
    yb = pair(yb, lambda i, j: (i, after(j)), lambda i, j: (i ^ 1, j))
    ya = pair(ya, lambda i, j: (i, j ^ 1))
    xe2, xh2, xe1, xslope = pl.pallas_call(
        strips_x,
        out_shape=(
            struct(3, planes_z, 2, SUB, width_y),
            struct(3, planes_z, 2, SUB, width_y),
            struct(3, PLANES, 2, SUB, width_y),
            struct(2, SUB, width_y),
        ),
        in_specs=[VMEM] * 7,
        out_specs=(VMEM,) * 4,
        scratch_shapes=[
            pltpu.VMEM((2, 3, planes_z + 1, SUB, width_y), F32),
            pltpu.VMEM((2, 3, planes_z + 1, SUB, width_y), F32),
            pltpu.VMEM((2, planes_z, SUB, width_y), F32),
        ],
        compiler_params=params(),
        cost_estimate=cost(1, 1),
        name="strips_x",
    )(e_adj, h_adj, material, density, table, xa, xb)

    devices = count_gx * count_gy
    rows_mine = (width_x // TILE) * (width_y // TILE) // REPEAT
    lines = TILE // 2
    padded = width_x + 4 * SUB
    local, weight_y, base_y, coef_y = pl.pallas_call(
        design,
        out_shape=(
            plane,
            struct(STEPS, 3, width_x, LANES),
            struct(width_x, LANES),
            struct(3, width_x + SUB, LANES),
        ),
        in_specs=[VMEM] * 8,
        out_specs=(VMEM,) * 4,
        compiler_params=params(),
        cost_estimate=cost(1, 1),
        name="design",
    )(e1, em, xe1, xe2, slope, xslope, base, weight)
    buf, ye2, yh2 = pl.pallas_call(
        gradient,
        out_shape=(struct(devices * rows_mine, lines, LANES),)
        + (struct(3, width_x + SUB, LANES),) * 2,
        in_specs=[VMEM] * 12,
        out_specs=(VMEM,) * 3,
        scratch_shapes=[
            pltpu.VMEM((padded, width_y), F32),
            pltpu.VMEM((width_y // LANES, padded, LANES), F32),
            pltpu.VMEM((width_y // LANES, padded, LANES), F32),
        ],
        compiler_params=params(),
        cost_estimate=cost(1, 1),
        name="gradient",
    )(strip, tails, ya, yb, xa, xb, table, own_ids, local, weight_y, base_y, coef_y)

    half = devices * rows_mine // 2
    far = count_gx // 2
    got = pair(buf[half:], lambda i, j: (i, j ^ 1))
    parts = pl.pallas_call(
        lambda *refs: first_sum(count_gy, *refs),
        out_shape=(struct(far * rows_mine, lines, LANES),) * count_gy,
        in_specs=[VMEM] * 2,
        out_specs=(VMEM,) * count_gy,
        compiler_params=params(),
        name="first_sum",
    )(buf, got)
    parts = [parts[0]] + [
        pair(parts[k], lambda i, j: (i ^ (k & 1), j ^ (k >> 1 << 1))) for k in range(1, count_gy)
    ]
    e_out, h_out = pl.pallas_call(
        merge,
        out_shape=(full,) * 2,
        in_specs=[VMEM] * 8,
        out_specs=(HBM,) * 2,
        scratch_shapes=[
            pltpu.VMEM((2, 3, planes_z, width_x, width_y), F32),
            pltpu.SemaphoreType.DMA((2, 3, 2)),
        ],
        compiler_params=params(),
        cost_estimate=cost(1, 1),
        name="merge",
    )(e2, h2, em, hm, xe2, xh2, ye2, yh2)
    parts = pl.pallas_call(
        lambda *refs: second_sum(count_gy, rows_mine, *refs),
        out_shape=(struct(rows_mine, lines, LANES),) * far,
        in_specs=[VMEM] * count_gy + [ANY],
        out_specs=(VMEM,) * far,
        compiler_params=params(),
        name="second_sum",
    )(*parts, done)
    parts = [parts[0]] + [pair(parts[k], lambda i, j: (i ^ (k << 1), j)) for k in range(1, far)]
    param_grad = sum(parts[1:], parts[0]).reshape(rows_mine, TILE * TILE)

    return e_out, h_out, param_grad


def solution(mesh):
    in_specs = (
        P(None, None, "gx", "gy"),
        P(None, None, "gx", "gy"),
        P("gx", "gy"),
        P(None, "gx", "gy"),
        P(),
        P(None, None, None, None, "gx", "gy"),
        P(None, None, None, None, "gx", "gy"),
        P("gx", "gy"),
    )
    out_specs = (P(None, None, "gx", "gy"), P(None, None, "gx", "gy"), P(("gx", "gy"), None))
    return jax.shard_map(
        on_device, mesh=mesh, in_specs=in_specs, out_specs=out_specs, check_vma=False
    )
```

```python
import math

import jax
import jax.numpy as jnp
from jax import lax
from jax.experimental import pallas as pl
from jax.experimental.pallas import tpu as pltpu
from jax.sharding import PartitionSpec as P

PLANES = 2
ZLO = 3
STEPS = 2
FREQ = 4
PML = 12
TILE = 64
REPEAT = 4

courant = 0.5
sigma_peak = 0.8
dft_weight = 0.5
sharpness = 4.0
threshold = 0.5
eps_low = 2.1
eps_high = 12.1
grad_scale = 0.01

F32 = jnp.float32
LANES = 128
SUB = 8
GROUP = 16
ANY = pl.BlockSpec(memory_space=pl.ANY)
HBM = pl.BlockSpec(memory_space=pltpu.HBM)
VMEM = pl.BlockSpec(memory_space=pltpu.VMEM)
SMEM = pl.BlockSpec(memory_space=pltpu.SMEM)


def params(size=40 * 2**20):
    return pltpu.CompilerParams(vmem_limit_bytes=size)


def struct(*shape, dtype=F32):
    return jax.ShapeDtypeStruct(shape, dtype)


def cost(flops, moved):
    return pl.CostEstimate(flops=int(flops), bytes_accessed=int(moved), transcendentals=0)


def iota(shape, dim):
    return lax.broadcasted_iota(jnp.int32, shape, dim)


def in_design(z):
    return ZLO <= z < ZLO + PLANES


def turn(values, shift, axis):
    size = values.shape[axis]
    shift %= size
    return values if shift == 0 else pltpu.roll(values, shift, axis)


def depth_cubed(places, total):
    depth = jnp.maximum(jnp.maximum(PML - places, places - (total - 1 - PML)), 0.0) / PML
    return depth * depth * depth


def edge_coefs(rows, cols, total_x, total_y, inside=None):
    sigma = sigma_peak * (depth_cubed(rows, total_x) + depth_cubed(cols, total_y))
    inverse = 1.0 / (1.0 + 0.5 * sigma)
    if inside is not None:
        inverse = jnp.where(inside, inverse, 0.0)
    return (1.0 - 0.5 * sigma) * inverse, courant * inverse, inverse


def within(rows, cols, total_x, total_y):
    return (rows >= 0) & (rows < total_x) & (cols >= 0) & (cols < total_y)


def table_inverse(table, rows, cols):
    tiles = [table[k * SUB : (k + 1) * SUB] for k in range(table.shape[0] // SUB)]
    return [jnp.tile(tile, (rows // SUB, cols // LANES)) for tile in tiles]


def pick(index, choices):
    out = jnp.zeros_like(choices[0])
    for k, choice in enumerate(choices):
        out = jnp.where(index == k, choice, out)
    return out


def design_terms(filtered):
    high = math.tanh(sharpness * threshold)
    norm = high + math.tanh(sharpness * (1.0 - threshold))
    bend = jnp.tanh(sharpness * (filtered - threshold))
    eps = eps_low + (eps_high - eps_low) * ((high + bend) / norm)
    return courant / eps, sharpness * (1.0 - bend * bend) / norm


def blur(values):
    rows, cols = values.shape
    summed = turn(values, 1, 0) + 2.0 * values + turn(values, rows - 1, 0)
    return (turn(summed, 1, 1) + 2.0 * summed + turn(summed, cols - 1, 1)) / 16.0


def id_row(tile_map, tx, shape):
    lane = iota(shape, len(shape) - 1)
    out = jnp.zeros(shape, F32)
    for t in range(tile_map.shape[1]):
        out = jnp.where(lane // TILE == t, (tile_map[tx, t] + 1).astype(F32), out)
    return out


TILES = 10
BEHIND = (0, 1, 2, 4, 5)


def pack_x(
    e_in, h_in, m_in, d_in, map_in, table_in,
    a_ref, b_ref, id_ref, inverse_ref, eb, hb, mb, db, map_ref, table_ref, sems,
):
    planes_z, size, width_y = m_in.shape
    span = 2 * SUB
    tiles = width_y // LANES
    views = [
        (e_in, eb.reshape(tiles, 3, planes_z, span, LANES)),
        (h_in, hb.reshape(tiles, 3, planes_z, span, LANES)),
        (m_in, mb.reshape(tiles, planes_z, span, LANES)),
    ]
    copies = []
    for k, start in enumerate((0, size - SUB)):
        here, there = pl.ds(start, SUB), pl.ds(k * SUB, SUB)
        for u in range(tiles):
            lanes = pl.ds(u * LANES, LANES)
            for n, (src, dst) in enumerate(views):
                source = src.at[:, here, lanes] if n == 2 else src.at[:, :, here, lanes]
                target = dst.at[u, :, there] if n == 2 else dst.at[u, :, :, there]
                copies.append(pltpu.make_async_copy(source, target, sems.at[len(copies)]))
        copies.append(pltpu.make_async_copy(d_in.at[here], db.at[there], sems.at[len(copies)]))
    copies.append(pltpu.make_async_copy(map_in, map_ref, sems.at[len(copies)]))
    copies.append(pltpu.make_async_copy(table_in, table_ref, sems.at[len(copies)]))
    for copy in copies:
        copy.start()
    gx, gy = lax.axis_index("gx"), lax.axis_index("gy")
    total_x, total_y = size * lax.axis_size("gx"), width_y * lax.axis_size("gy")
    shape = (SUB, width_y)
    sub = iota(shape, 0)
    rows = jnp.full(shape, (gx + 1) * size - 2, jnp.int32).astype(F32)
    cols = (iota(shape, 1) + gy * width_y).astype(F32)
    damping, coef_h, _ = edge_coefs(rows, cols, total_x, total_y)
    layer = (sub >= ZLO) & (sub < ZLO + PLANES)
    for copy in copies:
        copy.wait()

    def row(ref, c, r):
        rows = pl.ds(c * planes_z * span + r, planes_z, stride=span)
        return jnp.concatenate([ref[u, rows] for u in range(tiles)], axis=1)

    near, far = span - 1, span - 2
    ex, ey, ez = (row(eb, c, far) for c in range(3))
    up = jnp.where(sub == SUB - 1, 0.0, turn(ex, SUB - 1, 0))
    curl_y = (up - ex) - (row(eb, 2, near) - ez)
    curl_z = (row(eb, 1, near) - ey) - (turn(ex, width_y - 1, 1) - ex)
    mag = [row(hb, c, far) for c in (1, 2)]
    high = [row(eb, c, near) for c in range(3)] + [row(hb, c, near) for c in range(3)]
    high += [damping * h - coef_h * curl for h, curl in zip(mag, (curl_y, curl_z))]
    low = [row(eb, c, 0) for c in range(3)] + [row(hb, c, 0) for c in range(3)]
    low += [row(eb, 1, 1), row(eb, 2, 1)]
    for side, edge, further, tx in ((low, 0, 1, 0), (high, near, far, map_ref.shape[0] - 1)):
        density = jnp.broadcast_to(db[edge : edge + 1], shape)
        side.append(jnp.where(layer, density, row(mb, 0, edge).astype(F32)))
        misc = jnp.broadcast_to(db[further : further + 1], shape)
        side.append(jnp.where(sub == 1, id_row(map_ref, tx, shape), misc))
    strips = [row_to_strip(v) for v in [ex, ey, ez] + mag]
    strips.append(strips[-1])
    for k in range(3):
        pair_of = jnp.concatenate([strips[2 * k], strips[2 * k + 1]], axis=1)
        high[-1] = jnp.where(sub == 2 + k, jnp.broadcast_to(pair_of, shape), high[-1])
    even = gx % 2 == 0
    for k in range(TILES):
        a_ref[k] = jnp.where(even, high[k], low[k])
        b_ref[k] = jnp.where(even, low[k], high[k])
    for tx in range(map_ref.shape[0]):
        id_ref[pl.ds(tx * SUB, SUB)] = id_row(map_ref, tx, shape)
    for k in range(table_ref.shape[0]):
        inverse_ref[pl.ds(k * SUB, SUB)] = courant / jnp.full((SUB, LANES), table_ref[k], F32)


def neighbours(axis, from_a, from_b):
    here = lax.axis_index(axis)
    even = here % 2 == 0
    before = jnp.where(here > 0, jnp.where(even, from_b, from_a), 0.0)
    after = jnp.where(here < lax.axis_size(axis) - 1, jnp.where(even, from_a, from_b), 0.0)
    return before, after


def x_halos(xa_ref, xb_ref):
    both = [neighbours("gx", xa_ref[k], xb_ref[k]) for k in range(TILES)]
    return [t[0] for t in both], [t[1] for t in both]


def ends(values):
    lane = iota((values.shape[0], LANES), 1)
    return jnp.where(lane < LANES // 2, values[:, :LANES], values[:, -LANES:])


def row_to_strip(values):
    shape = (SUB, LANES)
    rolled = pltpu.roll(ends(values), GROUP // 2, 1, stride=GROUP, stride_axis=0)
    rolled = jnp.where(iota(shape, 1) // GROUP == iota(shape, 0), rolled, 0.0)
    return jnp.sum(rolled, axis=0, keepdims=True)


def build_strips(e_ref, h_ref, m_ref, d_ref, id_ref, s_ref):
    planes_z, width_x, width_y = m_ref.shape
    group = iota((SUB, LANES), 1) // GROUP

    def gather(get, here):
        acc = jnp.zeros((SUB, LANES), F32)
        for z in range(planes_z):
            acc = jnp.where(group == z, turn(ends(get(z, here)), z * GROUP + GROUP // 2, 1), acc)
        return acc

    def body(c, _):
        for base, ref in ((0, e_ref), (3, h_ref)):
            for start in range(0, width_x, SUB):
                here = pl.ds(start, SUB)
                s_ref[base + c, here] = gather(lambda z, here: ref[c, z, here], here)
        return 0

    lax.fori_loop(0, 3, body, 0)

    def source(z, here):
        return d_ref[here] if in_design(z) else m_ref[z, here].astype(F32)

    for start in range(0, width_x, SUB):
        here = pl.ds(start, SUB)
        s_ref[6, here] = gather(source, here)
        row = id_ref[pl.ds(start // TILE * SUB, SUB)]
        s_ref[7, here] = turn(ends(row), GROUP // 2, 1)


def pack_y(s_ref, xa_ref, xb_ref, _after, t_ref, a_ref, b_ref):
    width_x = s_ref.shape[1]
    even_y = lax.axis_index("gy") % 2 == 0
    below, above = x_halos(xa_ref, xb_ref)
    shape = (SUB, LANES)
    sub = iota(shape, 0)

    def row(tile, k):
        return jnp.broadcast_to(tile[k : k + 1], tile.shape)

    def wide(values):
        return jnp.broadcast_to(values, shape)

    zero = jnp.zeros(shape, F32)
    tails = []
    for f in range(8):
        if f < 7:
            k = 8 if f == 6 else f
            after_1, before_1 = (wide(row_to_strip(side[k])) for side in (above, below))
        else:
            after_1, before_1 = (wide(row_to_strip(row(side[9], 1))) for side in (above, below))
        after_2, before_2 = zero, zero
        if f in (1, 2):
            after_2 = wide(row_to_strip(above[5 + f]))
        if f in BEHIND:
            k = BEHIND.index(f)
            lanes = (k % 2) * LANES
            before_2 = wide(below[9][2 + k // 2 : 3 + k // 2, lanes : lanes + LANES])
        if f == 6:
            after_2, before_2 = (wide(row_to_strip(row(side[9], 0))) for side in (above, below))
        tail = jnp.where(sub == 0, after_1, jnp.where(sub == 1, after_2, 0.0))
        tail = jnp.where(sub == 6, before_2, jnp.where(sub == 7, before_1, tail))
        t_ref[f] = tail
        tails.append(tail)
    lane = iota(shape, 1) % GROUP
    for start in range(0, width_x + SUB, SUB):
        low = zero
        high = zero
        for f in range(8):
            values = tails[f] if start == width_x else s_ref[f, pl.ds(start, SUB)]
            mask = lane // 2 == f
            low = jnp.where(mask, turn(values, 2 * f - GROUP // 2, 1), low)
            high = jnp.where(mask, turn(values, 2 * f - (GROUP // 2 - 2), 1), high)
        a_ref[pl.ds(start, SUB)] = jnp.where(even_y, high, low)
        b_ref[pl.ds(start, SUB)] = jnp.where(even_y, low, high)


def transform(adj_ref, fwd_ref, s_ref, g_ref):
    rows = 2 * SUB

    def body(k, _):
        here = pl.ds(pl.multiple_of(k * rows, rows), rows)
        total = None
        for c in range(3):
            for p in range(PLANES):
                parts = [None] * STEPS
                for f in range(FREQ):
                    real = fwd_ref[f, 0, c, p, here].astype(F32)
                    imag = fwd_ref[f, 1, c, p, here].astype(F32)
                    term = real * adj_ref[f, 0, c, p, here] - imag * adj_ref[f, 1, c, p, here]
                    total = term if total is None else total + term
                    for n in range(STEPS):
                        angle = (0.21 + 0.06 * f) * (n + 1)
                        term = (dft_weight * math.cos(angle)) * real + (
                            dft_weight * math.sin(angle)
                        ) * imag
                        parts[n] = term if parts[n] is None else parts[n] + term
                for n in range(STEPS):
                    g_ref[n, c, p, here] = parts[n]
        s_ref[here] = total
        return 0

    lax.fori_loop(0, s_ref.shape[0] // rows, body, 0)


LO = ZLO - STEPS
HI = ZLO + PLANES + STEPS - 1


def update_mag(e, e_up, h, out, damp, ch):
    width_x, width_y = damp.shape
    for start in range(0, width_x, SUB):
        here = pl.ds(start, SUB)

        def ahead(c, tile):
            if start + SUB < width_x:
                return e(c)[pl.ds(start + 1, SUB)]
            return turn(tile, SUB - 1, 0)

        ex, ey, ez = (e(c)[here] for c in range(3))
        up_x = e_up(0)[here] - ex if e_up else -ex
        up_y = e_up(1)[here] - ey if e_up else -ey
        cx = (turn(ez, width_y - 1, 1) - ez) - up_y
        cy = up_x - (ahead(2, ez) - ez)
        cz = (ahead(1, ey) - ey) - (turn(ex, width_y - 1, 1) - ex)
        dm, cf = damp[here], ch[here]
        for c, curl in enumerate((cx, cy, cz)):
            out(c)[here] = dm * h(c)[here] - cf * curl


def update_elec(h, h_down, e, out, damp, ce):
    width_x, width_y = damp.shape
    for start in range(0, width_x, SUB):
        here = pl.ds(start, SUB)

        def behind(c, tile):
            return h(c)[pl.ds(start - 1, SUB)] if start else turn(tile, 1, 0)

        hx, hy, hz = (h(c)[here] for c in range(3))
        up_x = hx - h_down(0)[here] if h_down else hx
        up_y = hy - h_down(1)[here] if h_down else hy
        cx = (hz - turn(hz, 1, 1)) - up_y
        cy = up_x - (hz - behind(2, hz))
        cz = (hy - behind(1, hy)) - (hx - turn(hx, 1, 1))
        dm, cf = damp[here], ce[here]
        for c, curl in enumerate((cx, cy, cz)):
            out(c)[here] = dm * e(c)[here] + cf * curl


def at(ref, z):
    return lambda c: ref.at[c, z]


def fill_ce(ce, k, z, m_ref, choices, ch):
    for start in range(0, ch.shape[0], SUB):
        here = pl.ds(start, SUB)
        ce[k, here] = pick(m_ref[z, here], choices) * (ch[here] * (1.0 / courant))


def interior_first(e_ref, h_ref, m_ref, d_ref, table, em, hm, e1_ref, sl_ref, damp, ch, ce):
    planes_z, width_x, width_y = m_ref.shape
    gx, gy = lax.axis_index("gx"), lax.axis_index("gy")
    total_x, total_y = width_x * lax.axis_size("gx"), width_y * lax.axis_size("gy")
    shape = (width_x, width_y)
    rows = (iota(shape, 0) + gx * width_x).astype(F32)
    cols = (iota(shape, 1) + gy * width_y).astype(F32)
    damping, coef_h, inverse = edge_coefs(rows, cols, total_x, total_y)
    damp[...] = damping
    ch[...] = coef_h
    design, slope = design_terms(blur(d_ref[...]))
    sl_ref[...] = slope
    choices = table_inverse(table, SUB, width_y)
    for z in range(LO, HI):
        if in_design(z):
            ce[z - LO] = design * inverse
        elif z > LO:
            fill_ce(ce, z - LO, z, m_ref, choices, ch)

    def e(z):
        return at(em, z - LO)

    def h(z):
        return at(hm, z - LO)

    for z in range(LO, HI):
        update_mag(at(e_ref, z), at(e_ref, z + 1), at(h_ref, z), h(z), damp, ch)
    for z in range(LO + 1, HI):
        update_elec(h(z), h(z - 1), at(e_ref, z), e(z), damp, ce.at[z - LO])
    for c in range(3):
        for p in range(PLANES):
            e1_ref[c, p] = em[c, ZLO + p - LO]
    for z in range(LO + 1, HI - 1):
        update_mag(e(z), e(z + 1), h(z), h(z), damp, ch)
    for z in range(LO + 2, HI - 1):
        update_elec(h(z), h(z - 1), e(z), e(z), damp, ce.at[z - LO])


def interior_rest(e_ref, h_ref, m_ref, table, em, hm, damp, ch, ce, e2, h2, done, ce2):
    planes_z, width_x, width_y = m_ref.shape
    choices = table_inverse(table, SUB, width_y)
    done[...] = jnp.zeros(done.shape, F32)
    rest = [z for z in range(planes_z) if not LO < z < HI]
    for z in rest:
        fill_ce(ce2, z, z, m_ref, choices, ch)

    def coef(z):
        return ce.at[z - LO] if LO < z < HI else ce2.at[z]

    def e1(z):
        return at(em, z - LO) if LO < z < HI else at(e2, z)

    def h1(z):
        return at(hm, z - LO) if LO <= z < HI else at(h2, z)

    def h_last(z):
        return at(hm, z - LO) if LO < z < HI - 1 else at(h2, z)

    for z in range(planes_z):
        if not LO <= z < HI:
            up = at(e_ref, z + 1) if z + 1 < planes_z else None
            update_mag(at(e_ref, z), up, at(h_ref, z), at(h2, z), damp, ch)
    for z in rest:
        update_elec(h1(z), h1(z - 1) if z else None, at(e_ref, z), at(e2, z), damp, coef(z))
    for z in range(planes_z):
        if not LO < z < HI - 1:
            up = e1(z + 1) if z + 1 < planes_z else None
            update_mag(e1(z), up, h1(z), at(h2, z), damp, ch)
    for z in range(planes_z):
        if not in_design(z):
            down = h_last(z - 1) if z else None
            update_elec(h_last(z), down, e1(z), at(e2, z), damp, coef(z))


def strips_x(
    e_ref, h_ref, m_ref, d_ref, table, xa_ref, xb_ref,
    e2_ref, h2_ref, e1_ref, sl_ref, xe, xh, ce,
):
    planes_z, width_x, width_y = m_ref.shape
    gx, gy = lax.axis_index("gx"), lax.axis_index("gy")
    total_x, total_y = width_x * lax.axis_size("gx"), width_y * lax.axis_size("gy")
    shape = (SUB, width_y)
    sub = iota(shape, 0)
    cols = (iota(shape, 1) + gy * width_y).astype(F32)
    choices = table_inverse(table, SUB, width_y)
    zero = jnp.zeros(shape, F32)
    damps, chs = [], []

    below, above = x_halos(xa_ref, xb_ref)
    edges = pl.ds(0, SUB), pl.ds(width_x - SUB, SUB)

    def place(values, tile, z, at_sub):
        return jnp.where(sub == at_sub, turn(tile, at_sub - z, 0), values)

    def strip(side, own, near, far, z):
        out = turn(own, 2 if side == 0 else 6, 0)
        out = place(out, near, z, 1 if side == 0 else 6)
        if far is None:
            return jnp.where(sub == (0 if side == 0 else 7), 0.0, out)
        return place(out, far[0], far[1], 0 if side == 0 else 7)

    def source(side, z):
        own = d_ref[edges[side]] if in_design(z) else m_ref[z, edges[side]].astype(F32)
        halo = (below, above)[side]
        return strip(side, own, halo[8], (halo[9], 0), z)

    for side in range(2):
        rows = (sub + gx * width_x + (-2 if side == 0 else width_x - 6)).astype(F32)
        inside = within(rows, cols, total_x, total_y)
        damping, coef_h, inverse = edge_coefs(rows, cols, total_x, total_y, inside)
        damps.append(damping)
        chs.append(coef_h)
        for z in range(planes_z):
            for c in range(3):
                halo = (below, above)[side]
                far = (above[5 + c], z) if side and c else None
                xe[side, c, z] = strip(side, e_ref[c, z, edges[side]], halo[c], far, z)
                xh[side, c, z + 1] = strip(side, h_ref[c, z, edges[side]], halo[3 + c], None, z)
        for c in range(3):
            xe[side, c, planes_z] = zero
            xh[side, c, 0] = zero
        design, slope = design_terms(blur(source(side, ZLO)))
        sl_ref[side] = turn(slope, 6 if side == 0 else 2, 0)
        for z in range(planes_z):
            if in_design(z):
                ce[side, z] = design * inverse
            else:
                ce[side, z] = pick(source(side, z), choices) * inverse

    def mag(z):
        for side in range(2):
            ex, ey, ez = (xe[side, c, z] for c in range(3))
            cx = (turn(ez, width_y - 1, 1) - ez) - (xe[side, 1, z + 1] - ey)
            cy = (xe[side, 0, z + 1] - ex) - (turn(ez, SUB - 1, 0) - ez)
            cz = (turn(ey, SUB - 1, 0) - ey) - (turn(ex, width_y - 1, 1) - ex)
            for c, curl in enumerate((cx, cy, cz)):
                xh[side, c, z + 1] = damps[side] * xh[side, c, z + 1] - chs[side] * curl

    def elec(z):
        for side in range(2):
            hx, hy, hz = (xh[side, c, z + 1] for c in range(3))
            cx = (hz - turn(hz, 1, 1)) - (hy - xh[side, 1, z])
            cy = (hx - xh[side, 0, z]) - (hz - turn(hz, 1, 0))
            cz = (hy - turn(hy, 1, 0)) - (hx - turn(hx, 1, 1))
            for c, curl in enumerate((cx, cy, cz)):
                xe[side, c, z] = damps[side] * xe[side, c, z] + ce[side, z] * curl

    def loop(f):
        for z in range(planes_z):
            f(z)

    back = (6, 2)
    for n in range(STEPS):
        loop(mag)
        if n == 0:
            for z in range(planes_z):
                for c in (1, 2):
                    xh[0, c, z + 1] = place(xh[0, c, z + 1], below[5 + c], z, 0)
        loop(elec)
        if n == 0:
            for side in range(2):
                for c in range(3):
                    for p in range(PLANES):
                        e1_ref[c, p, side] = turn(xe[side, c, ZLO + p], back[side], 0)

    def finish(z):
        for side in range(2):
            for c in range(3):
                e2_ref[c, z, side] = turn(xe[side, c, z], back[side], 0)
                h2_ref[c, z, side] = turn(xh[side, c, z + 1], back[side], 0)

    loop(finish)


def patch_rows(values, strip, start, width_x):
    sub = iota(values.shape, 0)
    if start == 0:
        values = jnp.where(sub < 2, strip[0], values)
    if start == width_x - SUB:
        values = jnp.where(sub >= 6, strip[1], values)
    return values


def patch_cols(values, strip, z):
    lane = iota((values.shape[0], LANES), 1)
    rolled = turn(strip, -(z * GROUP + GROUP // 2), 1)
    tiles = [values[:, k : k + LANES] for k in range(0, values.shape[1], LANES)]
    tiles[0] = jnp.where(lane < 2, rolled, tiles[0])
    tiles[-1] = jnp.where(lane >= LANES - 2, rolled, tiles[-1])
    return jnp.concatenate(tiles, axis=1)


def strip_columns(shape):
    lane = iota(shape, 1)
    return lane % GROUP, lane // GROUP


def strip_coefs(width_x, width_y):
    gx, gy = lax.axis_index("gx"), lax.axis_index("gy")
    total_x, total_y = width_x * lax.axis_size("gx"), width_y * lax.axis_size("gy")
    shape = (width_x + SUB, LANES)
    col, _ = strip_columns(shape)
    row = iota(shape, 0)
    row = jnp.where(row >= width_x + 4, row - shape[0], row)
    place = jnp.where(col < GROUP // 2, col + (width_y - GROUP // 2), col - GROUP // 2)
    place = jnp.where(col < 2, col - 2, place)
    place = jnp.where(col >= GROUP - 2, col + (width_y - GROUP + 2), place)
    rows = (row + gx * width_x).astype(F32)
    cols = (place + gy * width_y).astype(F32)
    return edge_coefs(rows, cols, total_x, total_y, within(rows, cols, total_x, total_y))


def design(
    e1_ref, e2_ref, xe1_ref, xe2_ref, sl_ref, xsl_ref, sum_ref, g_ref,
    l_ref, gs_ref, ss_ref, coef_ref,
):
    width_x, width_y = sl_ref.shape
    for k, values in enumerate(strip_coefs(width_x, width_y)):
        coef_ref[k] = values
    group = iota((SUB, LANES), 1) // GROUP
    for start in range(0, width_x, SUB):
        here = pl.ds(start, SUB)
        total = sum_ref[here]
        ss_ref[here] = jnp.where(group == ZLO, turn(ends(total), ZLO * GROUP + GROUP // 2, 1), 0.0)
        for c in range(3):
            strips = [jnp.zeros((SUB, LANES), F32) for _ in range(STEPS)]
            for p in range(PLANES):
                z = ZLO + p
                first = patch_rows(e1_ref[c, p, here], xe1_ref.at[c, p], start, width_x)
                second = patch_rows(e2_ref[c, z - LO, here], xe2_ref.at[c, z], start, width_x)
                weights = [g_ref[n, c, p, here] for n in range(STEPS)]
                total = total + weights[0] * first + weights[1] * second
                for n in range(STEPS):
                    rolled = turn(ends(weights[n]), z * GROUP + GROUP // 2, 1)
                    strips[n] = jnp.where(group == z, rolled, strips[n])
            for n in range(STEPS):
                gs_ref[n, c, here] = strips[n]
        slope = patch_rows(sl_ref[here], xsl_ref, start, width_x)
        l_ref[here] = (grad_scale * (eps_high - eps_low)) * slope * total


def strips_y(s_ref, t_ref, ya_ref, yb_ref, table, coef_ref):
    planes_z = LANES // GROUP
    size = coef_ref.shape[1]
    col, plane = strip_columns((size, LANES))
    from_low, from_high = neighbours("gy", ya_ref[...], yb_ref[...])

    def field(f):
        own = jnp.concatenate([s_ref[f], t_ref[f]], axis=0)
        own = jnp.where(col < 2, turn(from_low, -2 * f, 1), own)
        return jnp.where(col >= GROUP - 2, turn(from_high, GROUP - 2 - 2 * f, 1), own)

    damping, coef_h, inverse = coef_ref[0], coef_ref[1], coef_ref[2]
    source = field(6)
    half = GROUP // 2

    def next_col(v):
        jump = (col == 1) | (col == half - 1)
        return jnp.where(jump, turn(v, 1 - half, 1), turn(v, -1, 1))

    def prev_col(v):
        jump = (col == half) | (col == GROUP - 2)
        return jnp.where(jump, turn(v, half - 1, 1), turn(v, 1, 1))

    filtered = turn(source, 1, 0) + 2.0 * source + turn(source, size - 1, 0)
    filtered = (prev_col(filtered) + 2.0 * filtered + next_col(filtered)) / 16.0
    design, slope = design_terms(filtered)
    choices = table_inverse(table, size, LANES)
    layer = (plane >= ZLO) & (plane < ZLO + PLANES)
    coef_e = jnp.where(layer, design, pick(source, choices)) * inverse
    e = [field(c) for c in range(3)]
    h = [field(3 + c) for c in range(3)]
    top = plane == planes_z - 1
    bottom = plane == 0

    def dxf(v):
        return turn(v, size - 1, 0) - v

    def dyf(v):
        return next_col(v) - v

    def dzf(v):
        return jnp.where(top, 0.0, turn(v, LANES - GROUP, 1)) - v

    def dxb(v):
        return v - turn(v, 1, 0)

    def dyb(v):
        return v - prev_col(v)

    def dzb(v):
        return v - jnp.where(bottom, 0.0, turn(v, GROUP, 1))

    steps = []
    for _ in range(STEPS):
        curl = (dyf(e[2]) - dzf(e[1]), dzf(e[0]) - dxf(e[2]), dxf(e[1]) - dyf(e[0]))
        h = [damping * v - coef_h * c for v, c in zip(h, curl)]
        curl = (dyb(h[2]) - dzb(h[1]), dzb(h[0]) - dxb(h[2]), dxb(h[1]) - dyb(h[0]))
        e = [damping * v + coef_e * c for v, c in zip(e, curl)]
        steps.append(e)
    return steps, h, slope


def slot_of(param, rows_mine):
    gx, gy = lax.axis_index("gx"), lax.axis_index("gy")
    count_gx, count_gy = lax.axis_size("gx"), lax.axis_size("gy")
    owner = lax.div(param, jnp.int32(rows_mine))
    row = param - owner * rows_mine
    ox = lax.div(owner, jnp.int32(count_gy))
    oy = owner - ox * count_gy
    core = (oy ^ gy) & 1
    near = ((ox & 1) + 2 * (oy >> 1)) ^ ((gx & 1) + 2 * (gy >> 1))
    far = (ox >> 1) ^ (gx >> 1)
    return ((core * count_gy + near) * (count_gx // 2) + far) * rows_mine + row


def gradient(
    s_ref, t_ref, yb_ref, ya_ref, xa_ref, xb_ref, table, own_ref, l_ref, gs_ref, ss_ref, coef_ref,
    buf_ref, ye_ref, yh_ref, lpad, vpad, gpad,
):
    width_x, width_y = l_ref.shape
    tiles_x, tiles_y = width_x // TILE, width_y // TILE

    def scalar(row, lane):
        here = iota(row.shape, 1) == lane
        return jnp.max(jnp.where(here, row, 0.0)).astype(jnp.int32)

    id_x, id_y, own = {}, {}, {}
    for tx in range(tiles_x):
        for t in range(tiles_y):
            u = t * TILE // LANES * LANES
            row = own_ref[pl.ds(tx * SUB, 1), pl.ds(u, LANES)]
            own[tx, t] = scalar(row, t * TILE - u) - 1
    for k, tile in enumerate(neighbours("gx", xa_ref[TILES - 1], xb_ref[TILES - 1])):
        for t in range(tiles_y):
            u = t * TILE // LANES * LANES
            id_x[k, t] = scalar(tile[1:2, u : u + LANES], t * TILE - u)
    for row in [tx * TILE for tx in range(tiles_x)] + [width_x, width_x + SUB - 1]:
        first = row // SUB * SUB
        here = pl.ds(first, SUB)
        for k, tile in enumerate(neighbours("gy", ya_ref[here], yb_ref[here])):
            id_y[k, row] = scalar(tile[row - first : row - first + 1], GROUP - 1 - k)
    steps, h, slope_y = strips_y(s_ref, t_ref, ya_ref, yb_ref, table, coef_ref)
    for c in range(3):
        ye_ref[c] = steps[-1][c]
        yh_ref[c] = h[c]
    pad = 2 * SUB
    lpad[pl.ds(0, pad)] = jnp.zeros((pad, width_y), F32)
    lpad[pl.ds(pad + width_x, pad)] = jnp.zeros((pad, width_y), F32)
    buf_ref[...] = jnp.zeros(buf_ref.shape, F32)
    for start in range(0, width_x, SUB):
        here, rows = pl.ds(start, SUB), slice(start, start + SUB)
        total = ss_ref[here]
        for c in range(3):
            for n in range(STEPS):
                total = total + gs_ref[n, c, here] * steps[n][c][rows]
        total = sum((turn(total, -p * GROUP, 1) for p in range(1, PLANES)), total)
        total = (grad_scale * (eps_high - eps_low)) * slope_y[rows] * total
        lpad[pl.ds(pad + start, SUB)] = patch_cols(l_ref[here], total, ZLO)
    lane = iota((SUB, width_y), 1)
    for start in range(SUB, pad + width_x + SUB, SUB):
        v = lpad[pl.ds(start - 1, SUB)] + 2.0 * lpad[pl.ds(start, SUB)] + lpad[pl.ds(start + 1, SUB)]
        v = v / 16.0
        left = jnp.where(lane == 0, 0.0, turn(v, 1, 1))
        right = jnp.where(lane == width_y - 1, 0.0, turn(v, width_y - 1, 1))
        g = left + 2.0 * v + right
        for u in range(width_y // LANES):
            vpad[u, pl.ds(start, SUB)] = v[:, u * LANES : (u + 1) * LANES]
            gpad[u, pl.ds(start, SUB)] = g[:, u * LANES : (u + 1) * LANES]

    half = LANES // 2
    lines = TILE // 2
    devices = lax.axis_size("gx") * lax.axis_size("gy")
    rows_mine = buf_ref.shape[0] // devices
    lane = iota((lines, LANES), 1)
    lane8 = iota((SUB, LANES), 1)
    sub8 = iota((SUB, LANES), 0)

    def add_tile(param, values):
        slot = slot_of(param, rows_mine)
        buf_ref[slot] = buf_ref[slot] + values

    def add_rows(ident, start, values):
        slot = slot_of(jnp.maximum(ident - 1, 0), rows_mine)
        rows = pl.ds(start, SUB)
        buf_ref[slot, rows] = buf_ref[slot, rows] + jnp.where(ident > 0, values, 0.0)

    for tx in range(tiles_x):
        for u in range(width_y // LANES):
            even = gpad[u, pl.ds(pad + tx * TILE, lines, stride=2)]
            odd = gpad[u, pl.ds(pad + tx * TILE + 1, lines, stride=2)]
            add_tile(own[tx, 2 * u], jnp.where(lane < half, even, turn(odd, half, 1)))
            add_tile(own[tx, 2 * u + 1], jnp.where(lane < half, turn(even, half, 1), odd))
    before, after = pl.ds(pad - SUB, SUB), pl.ds(pad + width_x, SUB)
    for t in range(tiles_y):
        u, odd = divmod(t, 2)
        top, low = gpad[u, before], gpad[u, after]
        top = top if odd else turn(top, half, 1)
        low = turn(low, half, 1) if odd else low
        keep = (sub8 == SUB - 1) & (lane8 >= half)
        add_rows(id_x[0, t], lines - SUB, jnp.where(keep, top, 0.0))
        keep = (sub8 == 0) & (lane8 < half)
        add_rows(id_x[1, t], 0, jnp.where(keep, low, 0.0))
    end = width_y // LANES - 1
    for tx in range(tiles_x):
        even, odd = (pl.ds(pad + tx * TILE + k, lines, stride=2) for k in (0, 1))
        left = jnp.where(lane == half - 1, turn(vpad[0, even], half - 1, 1), 0.0)
        left = jnp.where(lane == LANES - 1, turn(vpad[0, odd], LANES - 1, 1), left)
        right = jnp.where(lane == 0, turn(vpad[end, even], 1, 1), 0.0)
        right = jnp.where(lane == half, turn(vpad[end, odd], half + 1, 1), right)
        for ahead, values in ((False, left), (True, right)):
            owner = id_y[ahead, tx * TILE]
            add_tile(jnp.maximum(owner - 1, 0), jnp.where(owner > 0, values, 0.0))
    tail = width_x + SUB - 1
    corners = (
        (SUB - 1, False, tail, before, lines - SUB, LANES - 1),
        (SUB - 1, True, tail, before, lines - SUB, half),
        (0, False, width_x, after, 0, half - 1),
        (0, True, width_x, after, 0, 0),
    )
    for sub, ahead, row, rows, start, target in corners:
        keep = (sub8 == sub) & (lane8 == target)
        values = vpad[end, rows] if ahead else vpad[0, rows]
        values = turn(values, target - (LANES - 1 if ahead else 0), 1)
        add_rows(id_y[ahead, row], start, jnp.where(keep, values, 0.0))


def merge(e_ref, h_ref, em, hm, xe_ref, xh_ref, ye_ref, yh_ref, eo_ref, ho_ref, out, sems):
    _, planes_z, width_x, _ = e_ref.shape
    parts = (
        (e_ref, em, xe_ref, ye_ref, eo_ref, LO + 2, HI - 1),
        (h_ref, hm, xh_ref, yh_ref, ho_ref, LO + 1, HI - 1),
    )
    half = planes_z // 2

    def send(n, c, k):
        rows = pl.ds(k * half, half)
        return pltpu.make_async_copy(out.at[n, c, rows], parts[n][4].at[c, rows], sems.at[n, c, k])

    def body(c, _):
        for n, (rest, mid, xs, ys, _, low, high) in enumerate(parts):
            for z in range(planes_z):
                src = mid.at[c, z - LO] if low <= z < high else rest.at[c, z]
                for start in range(0, width_x, SUB):
                    here = pl.ds(start, SUB)
                    values = patch_rows(src[here], xs.at[c, z], start, width_x)
                    out[n, c, z, here] = patch_cols(values, ys[c, here], z)
                if z % half == half - 1:
                    send(n, c, z // half).start()
        return 0

    lax.fori_loop(0, 3, body, 0)
    for n in range(2):
        for c in range(3):
            for k in range(2):
                send(n, c, k).wait()


def first_sum(parts, buf_ref, got_ref, *outs):
    size = outs[0].shape[0]
    for k in range(parts):
        rows = pl.ds(k * size, size)
        outs[k][...] = buf_ref[rows] + got_ref[rows]


def second_sum(parts, rows_mine, *refs):
    ins, outs = refs[:parts], refs[parts + 1 :]
    for k, out in enumerate(outs):
        rows = pl.ds(k * rows_mine, rows_mine)
        out[...] = sum(ref[rows] for ref in ins[1:]) + ins[0][rows]


def pair(block, partner, spare=None):
    count_gx, count_gy = lax.axis_size("gx"), lax.axis_size("gy")
    route = []
    for i in range(count_gx):
        for j in range(count_gy):
            a, b = partner(i, j)
            if not (0 <= a < count_gx and 0 <= b < count_gy):
                a, b = spare(i, j)
            route.append((i * count_gy + j, a * count_gy + b))
    return lax.ppermute(block, ("gx", "gy"), route)


def after(k):
    return ((k + 1) ^ 1) - 1


def on_device(e_adj, h_adj, density, material, eps_table, dft_adj, dft_fwd, tile_map):
    planes_z, width_x, width_y = material.shape
    count_gx, count_gy = lax.axis_size("gx"), lax.axis_size("gy")
    assert planes_z == SUB
    face = struct(TILES, SUB, width_y)
    xa, xb, own_ids, table = pl.pallas_call(
        pack_x,
        out_shape=(
            pltpu.VMEM(face.shape, F32),
            pltpu.VMEM(face.shape, F32),
            pltpu.VMEM((width_x // TILE * SUB, width_y), F32),
            pltpu.VMEM((eps_table.shape[0] * SUB, LANES), F32),
        ),
        in_specs=[HBM] * 6,
        out_specs=(VMEM,) * 4,
        scratch_shapes=[
            pltpu.VMEM((width_y // LANES, 3 * planes_z * 2 * SUB, LANES), F32),
            pltpu.VMEM((width_y // LANES, 3 * planes_z * 2 * SUB, LANES), F32),
            pltpu.VMEM((width_y // LANES, planes_z * 2 * SUB, LANES), jnp.int32),
            pltpu.VMEM((2 * SUB, width_y), F32),
            pltpu.SMEM(tile_map.shape, jnp.int32),
            pltpu.SMEM(eps_table.shape, F32),
            pltpu.SemaphoreType.DMA((6 * width_y // LANES + 4,)),
        ],
        compiler_params=params(),
        name="pack_x",
    )(
        *(
            pltpu.with_memory_space_constraint(x, pltpu.HBM)
            for x in (e_adj, h_adj, material, density, tile_map, eps_table)
        )
    )
    xa = pair(xa, lambda i, j: (i ^ 1, j))
    xb = pair(xb, lambda i, j: (after(i), j), lambda i, j: (i, j ^ 1))
    strip = pl.pallas_call(
        build_strips,
        out_shape=struct(8, width_x, LANES),
        in_specs=[VMEM] * 5,
        out_specs=VMEM,
        compiler_params=params(),
        cost_estimate=cost(1, 1),
        name="build_strips",
    )(e_adj, h_adj, material, density, own_ids)

    base, weight = pl.pallas_call(
        transform,
        out_shape=(
            struct(width_x, width_y),
            struct(STEPS, 3, PLANES, width_x, width_y),
        ),
        in_specs=[VMEM] * 2,
        out_specs=(VMEM,) * 2,
        compiler_params=params(),
        cost_estimate=cost(1, 1),
        name="transform",
    )(dft_adj, dft_fwd)
    plane = struct(width_x, width_y)
    middle = struct(3, HI - LO, width_x, width_y)
    full = struct(3, planes_z, width_x, width_y)
    em, hm, e1, slope, damp, ch, ce = pl.pallas_call(
        interior_first,
        out_shape=(middle, middle, struct(3, PLANES, width_x, width_y))
        + (plane,) * 3
        + (struct(HI - LO, width_x, width_y),),
        in_specs=[VMEM] * 5,
        out_specs=(VMEM,) * 7,
        compiler_params=params(),
        cost_estimate=cost(1, 1),
        name="interior_first",
    )(e_adj, h_adj, material, density, table)
    e2, h2, done = pl.pallas_call(
        interior_rest,
        out_shape=(full, full, struct(SUB, LANES)),
        in_specs=[VMEM] * 9,
        out_specs=(VMEM,) * 3,
        scratch_shapes=[pltpu.VMEM((planes_z, width_x, width_y), F32)],
        compiler_params=params(),
        cost_estimate=cost(1, 1),
        name="interior_rest",
    )(e_adj, h_adj, material, table, em, hm, damp, ch, ce)

    tails, ya, yb = pl.pallas_call(
        pack_y,
        out_shape=(struct(8, SUB, LANES),) + (struct(width_x + SUB, LANES),) * 2,
        in_specs=[VMEM] * 3 + [ANY],
        out_specs=(VMEM,) * 3,
        compiler_params=params(),
        name="pack_y",
    )(strip, xa, xb, slope)
    yb = pair(yb, lambda i, j: (i, after(j)), lambda i, j: (i ^ 1, j))
    ya = pair(ya, lambda i, j: (i, j ^ 1))
    xe2, xh2, xe1, xslope = pl.pallas_call(
        strips_x,
        out_shape=(
            struct(3, planes_z, 2, SUB, width_y),
            struct(3, planes_z, 2, SUB, width_y),
            struct(3, PLANES, 2, SUB, width_y),
            struct(2, SUB, width_y),
        ),
        in_specs=[VMEM] * 7,
        out_specs=(VMEM,) * 4,
        scratch_shapes=[
            pltpu.VMEM((2, 3, planes_z + 1, SUB, width_y), F32),
            pltpu.VMEM((2, 3, planes_z + 1, SUB, width_y), F32),
            pltpu.VMEM((2, planes_z, SUB, width_y), F32),
        ],
        compiler_params=params(),
        cost_estimate=cost(1, 1),
        name="strips_x",
    )(e_adj, h_adj, material, density, table, xa, xb)

    devices = count_gx * count_gy
    rows_mine = (width_x // TILE) * (width_y // TILE) // REPEAT
    lines = TILE // 2
    padded = width_x + 4 * SUB
    local, weight_y, base_y, coef_y = pl.pallas_call(
        design,
        out_shape=(
            plane,
            struct(STEPS, 3, width_x, LANES),
            struct(width_x, LANES),
            struct(3, width_x + SUB, LANES),
        ),
        in_specs=[VMEM] * 8,
        out_specs=(VMEM,) * 4,
        compiler_params=params(),
        cost_estimate=cost(1, 1),
        name="design",
    )(e1, em, xe1, xe2, slope, xslope, base, weight)
    buf, ye2, yh2 = pl.pallas_call(
        gradient,
        out_shape=(struct(devices * rows_mine, lines, LANES),)
        + (struct(3, width_x + SUB, LANES),) * 2,
        in_specs=[VMEM] * 12,
        out_specs=(VMEM,) * 3,
        scratch_shapes=[
            pltpu.VMEM((padded, width_y), F32),
            pltpu.VMEM((width_y // LANES, padded, LANES), F32),
            pltpu.VMEM((width_y // LANES, padded, LANES), F32),
        ],
        compiler_params=params(),
        cost_estimate=cost(1, 1),
        name="gradient",
    )(strip, tails, yb, ya, xa, xb, table, own_ids, local, weight_y, base_y, coef_y)

    half = devices * rows_mine // 2
    far = count_gx // 2
    got = pair(buf[half:], lambda i, j: (i, j ^ 1))
    parts = pl.pallas_call(
        lambda *refs: first_sum(count_gy, *refs),
        out_shape=(struct(far * rows_mine, lines, LANES),) * count_gy,
        in_specs=[VMEM] * 2,
        out_specs=(VMEM,) * count_gy,
        compiler_params=params(),
        name="first_sum",
    )(buf, got)
    parts = [parts[0]] + [
        pair(parts[k], lambda i, j: (i ^ (k & 1), j ^ (k >> 1 << 1))) for k in range(count_gy - 1, 0, -1)
    ]
    e_out, h_out = pl.pallas_call(
        merge,
        out_shape=(full,) * 2,
        in_specs=[VMEM] * 8,
        out_specs=(HBM,) * 2,
        scratch_shapes=[
            pltpu.VMEM((2, 3, planes_z, width_x, width_y), F32),
            pltpu.SemaphoreType.DMA((2, 3, 2)),
        ],
        compiler_params=params(),
        cost_estimate=cost(1, 1),
        name="merge",
    )(e2, h2, em, hm, xe2, xh2, ye2, yh2)
    parts = pl.pallas_call(
        lambda *refs: second_sum(count_gy, rows_mine, *refs),
        out_shape=(struct(rows_mine, lines, LANES),) * far,
        in_specs=[VMEM] * count_gy + [ANY],
        out_specs=(VMEM,) * far,
        compiler_params=params(),
        name="second_sum",
    )(*parts, done)
    parts = [parts[0]] + [pair(parts[k], lambda i, j: (i ^ (k << 1), j)) for k in range(1, far)]
    param_grad = sum(parts[1:], parts[0]).reshape(rows_mine, TILE * TILE)

    return e_out, h_out, param_grad


def solution(mesh):
    in_specs = (
        P(None, None, "gx", "gy"),
        P(None, None, "gx", "gy"),
        P("gx", "gy"),
        P(None, "gx", "gy"),
        P(),
        P(None, None, None, None, "gx", "gy"),
        P(None, None, None, None, "gx", "gy"),
        P("gx", "gy"),
    )
    out_specs = (P(None, None, "gx", "gy"), P(None, None, "gx", "gy"), P(("gx", "gy"), None))
    return jax.shard_map(
        on_device, mesh=mesh, in_specs=in_specs, out_specs=out_specs, check_vma=False
    )
```

```python
import math

import jax
import jax.numpy as jnp
from jax import lax
from jax.experimental import pallas as pl
from jax.experimental.pallas import tpu as pltpu
from jax.sharding import PartitionSpec as P

PLANES = 2
ZLO = 3
STEPS = 2
FREQ = 4
PML = 12
TILE = 64
REPEAT = 4

courant = 0.5
sigma_peak = 0.8
dft_weight = 0.5
sharpness = 4.0
threshold = 0.5
eps_low = 2.1
eps_high = 12.1
grad_scale = 0.01

F32 = jnp.float32
LANES = 128
SUB = 8
GROUP = 16
ANY = pl.BlockSpec(memory_space=pl.ANY)
HBM = pl.BlockSpec(memory_space=pltpu.HBM)
VMEM = pl.BlockSpec(memory_space=pltpu.VMEM)
SMEM = pl.BlockSpec(memory_space=pltpu.SMEM)


def params(size=40 * 2**20):
    return pltpu.CompilerParams(vmem_limit_bytes=size)


def struct(*shape, dtype=F32):
    return jax.ShapeDtypeStruct(shape, dtype)


def cost(flops, moved):
    return pl.CostEstimate(flops=int(flops), bytes_accessed=int(moved), transcendentals=0)


def iota(shape, dim):
    return lax.broadcasted_iota(jnp.int32, shape, dim)


def in_design(z):
    return ZLO <= z < ZLO + PLANES


def turn(values, shift, axis):
    size = values.shape[axis]
    shift %= size
    return values if shift == 0 else pltpu.roll(values, shift, axis)


def depth_cubed(places, total):
    depth = jnp.maximum(jnp.maximum(PML - places, places - (total - 1 - PML)), 0.0) / PML
    return depth * depth * depth


def edge_coefs(rows, cols, total_x, total_y, inside=None):
    sigma = sigma_peak * (depth_cubed(rows, total_x) + depth_cubed(cols, total_y))
    inverse = 1.0 / (1.0 + 0.5 * sigma)
    if inside is not None:
        inverse = jnp.where(inside, inverse, 0.0)
    return (1.0 - 0.5 * sigma) * inverse, courant * inverse, inverse


def within(rows, cols, total_x, total_y):
    return (rows >= 0) & (rows < total_x) & (cols >= 0) & (cols < total_y)


def table_inverse(table, rows, cols):
    tiles = [table[k * SUB : (k + 1) * SUB] for k in range(table.shape[0] // SUB)]
    return [jnp.tile(tile, (rows // SUB, cols // LANES)) for tile in tiles]


def pick(index, choices):
    out = jnp.zeros_like(choices[0])
    for k, choice in enumerate(choices):
        out = jnp.where(index == k, choice, out)
    return out


def design_terms(filtered):
    high = math.tanh(sharpness * threshold)
    norm = high + math.tanh(sharpness * (1.0 - threshold))
    bend = jnp.tanh(sharpness * (filtered - threshold))
    eps = eps_low + (eps_high - eps_low) * ((high + bend) / norm)
    return courant / eps, sharpness * (1.0 - bend * bend) / norm


def blur(values):
    rows, cols = values.shape
    summed = turn(values, 1, 0) + 2.0 * values + turn(values, rows - 1, 0)
    return (turn(summed, 1, 1) + 2.0 * summed + turn(summed, cols - 1, 1)) / 16.0


def id_row(tile_map, tx, shape):
    lane = iota(shape, len(shape) - 1)
    out = jnp.zeros(shape, F32)
    for t in range(tile_map.shape[1]):
        out = jnp.where(lane // TILE == t, (tile_map[tx, t] + 1).astype(F32), out)
    return out


TILES = 10
BEHIND = (0, 1, 2, 4, 5)


def pack_x(
    e_in, h_in, m_in, d_in, map_in, table_in,
    a_ref, b_ref, id_ref, inverse_ref, eb, hb, mb, db, map_ref, table_ref, sems,
):
    planes_z, size, width_y = m_in.shape
    span = 2 * SUB
    tiles = width_y // LANES
    views = [
        (e_in, eb.reshape(tiles, 3, planes_z, span, LANES)),
        (h_in, hb.reshape(tiles, 3, planes_z, span, LANES)),
        (m_in, mb.reshape(tiles, planes_z, span, LANES)),
    ]
    copies = []
    for k, start in enumerate((0, size - SUB)):
        here, there = pl.ds(start, SUB), pl.ds(k * SUB, SUB)
        for u in range(tiles):
            lanes = pl.ds(u * LANES, LANES)
            for n, (src, dst) in enumerate(views):
                source = src.at[:, here, lanes] if n == 2 else src.at[:, :, here, lanes]
                target = dst.at[u, :, there] if n == 2 else dst.at[u, :, :, there]
                copies.append(pltpu.make_async_copy(source, target, sems.at[len(copies)]))
        copies.append(pltpu.make_async_copy(d_in.at[here], db.at[there], sems.at[len(copies)]))
    copies.append(pltpu.make_async_copy(map_in, map_ref, sems.at[len(copies)]))
    copies.append(pltpu.make_async_copy(table_in, table_ref, sems.at[len(copies)]))
    for copy in copies:
        copy.start()
    gx, gy = lax.axis_index("gx"), lax.axis_index("gy")
    total_x, total_y = size * lax.axis_size("gx"), width_y * lax.axis_size("gy")
    shape = (SUB, width_y)
    sub = iota(shape, 0)
    rows = jnp.full(shape, (gx + 1) * size - 2, jnp.int32).astype(F32)
    cols = (iota(shape, 1) + gy * width_y).astype(F32)
    damping, coef_h, _ = edge_coefs(rows, cols, total_x, total_y)
    layer = (sub >= ZLO) & (sub < ZLO + PLANES)
    for copy in copies:
        copy.wait()

    def row(ref, c, r):
        rows = pl.ds(c * planes_z * span + r, planes_z, stride=span)
        return jnp.concatenate([ref[u, rows] for u in range(tiles)], axis=1)

    near, far = span - 1, span - 2
    ex, ey, ez = (row(eb, c, far) for c in range(3))
    up = jnp.where(sub == SUB - 1, 0.0, turn(ex, SUB - 1, 0))
    curl_y = (up - ex) - (row(eb, 2, near) - ez)
    curl_z = (row(eb, 1, near) - ey) - (turn(ex, width_y - 1, 1) - ex)
    mag = [row(hb, c, far) for c in (1, 2)]
    high = [row(eb, c, near) for c in range(3)] + [row(hb, c, near) for c in range(3)]
    high += [damping * h - coef_h * curl for h, curl in zip(mag, (curl_y, curl_z))]
    low = [row(eb, c, 0) for c in range(3)] + [row(hb, c, 0) for c in range(3)]
    low += [row(eb, 1, 1), row(eb, 2, 1)]
    for side, edge, further, tx in ((low, 0, 1, 0), (high, near, far, map_ref.shape[0] - 1)):
        density = jnp.broadcast_to(db[edge : edge + 1], shape)
        side.append(jnp.where(layer, density, row(mb, 0, edge).astype(F32)))
        misc = jnp.broadcast_to(db[further : further + 1], shape)
        side.append(jnp.where(sub == 1, id_row(map_ref, tx, shape), misc))
    strips = [row_to_strip(v) for v in [ex, ey, ez] + mag]
    strips.append(strips[-1])
    for k in range(3):
        pair_of = jnp.concatenate([strips[2 * k], strips[2 * k + 1]], axis=1)
        high[-1] = jnp.where(sub == 2 + k, jnp.broadcast_to(pair_of, shape), high[-1])
    even = gx % 2 == 0
    for k in range(TILES):
        a_ref[k] = jnp.where(even, high[k], low[k])
        b_ref[k] = jnp.where(even, low[k], high[k])
    for tx in range(map_ref.shape[0]):
        id_ref[pl.ds(tx * SUB, SUB)] = id_row(map_ref, tx, shape)
    for k in range(table_ref.shape[0]):
        inverse_ref[pl.ds(k * SUB, SUB)] = courant / jnp.full((SUB, LANES), table_ref[k], F32)


def neighbours(axis, from_a, from_b):
    here = lax.axis_index(axis)
    even = here % 2 == 0
    before = jnp.where(here > 0, jnp.where(even, from_b, from_a), 0.0)
    after = jnp.where(here < lax.axis_size(axis) - 1, jnp.where(even, from_a, from_b), 0.0)
    return before, after


def x_halos(xa_ref, xb_ref):
    both = [neighbours("gx", xa_ref[k], xb_ref[k]) for k in range(TILES)]
    return [t[0] for t in both], [t[1] for t in both]


def ends(values):
    lane = iota((values.shape[0], LANES), 1)
    return jnp.where(lane < LANES // 2, values[:, :LANES], values[:, -LANES:])


def row_to_strip(values):
    shape = (SUB, LANES)
    rolled = pltpu.roll(ends(values), GROUP // 2, 1, stride=GROUP, stride_axis=0)
    rolled = jnp.where(iota(shape, 1) // GROUP == iota(shape, 0), rolled, 0.0)
    return jnp.sum(rolled, axis=0, keepdims=True)


def build_strips(e_ref, h_ref, m_ref, d_ref, id_ref, s_ref):
    planes_z, width_x, width_y = m_ref.shape
    group = iota((SUB, LANES), 1) // GROUP

    def gather(get, here):
        acc = jnp.zeros((SUB, LANES), F32)
        for z in range(planes_z):
            acc = jnp.where(group == z, turn(ends(get(z, here)), z * GROUP + GROUP // 2, 1), acc)
        return acc

    def body(c, _):
        for base, ref in ((0, e_ref), (3, h_ref)):
            for start in range(0, width_x, SUB):
                here = pl.ds(start, SUB)
                s_ref[base + c, here] = gather(lambda z, here: ref[c, z, here], here)
        return 0

    lax.fori_loop(0, 3, body, 0)

    def source(z, here):
        return d_ref[here] if in_design(z) else m_ref[z, here].astype(F32)

    for start in range(0, width_x, SUB):
        here = pl.ds(start, SUB)
        s_ref[6, here] = gather(source, here)
        row = id_ref[pl.ds(start // TILE * SUB, SUB)]
        s_ref[7, here] = turn(ends(row), GROUP // 2, 1)


def pack_y(s_ref, xa_ref, xb_ref, _after, t_ref, a_ref, b_ref):
    width_x = s_ref.shape[1]
    even_y = lax.axis_index("gy") % 2 == 0
    below, above = x_halos(xa_ref, xb_ref)
    shape = (SUB, LANES)
    sub = iota(shape, 0)

    def row(tile, k):
        return jnp.broadcast_to(tile[k : k + 1], tile.shape)

    def wide(values):
        return jnp.broadcast_to(values, shape)

    zero = jnp.zeros(shape, F32)
    tails = []
    for f in range(8):
        if f < 7:
            k = 8 if f == 6 else f
            after_1, before_1 = (wide(row_to_strip(side[k])) for side in (above, below))
        else:
            after_1, before_1 = (wide(row_to_strip(row(side[9], 1))) for side in (above, below))
        after_2, before_2 = zero, zero
        if f in (1, 2):
            after_2 = wide(row_to_strip(above[5 + f]))
        if f in BEHIND:
            k = BEHIND.index(f)
            lanes = (k % 2) * LANES
            before_2 = wide(below[9][2 + k // 2 : 3 + k // 2, lanes : lanes + LANES])
        if f == 6:
            after_2, before_2 = (wide(row_to_strip(row(side[9], 0))) for side in (above, below))
        tail = jnp.where(sub == 0, after_1, jnp.where(sub == 1, after_2, 0.0))
        tail = jnp.where(sub == 6, before_2, jnp.where(sub == 7, before_1, tail))
        t_ref[f] = tail
        tails.append(tail)
    lane = iota(shape, 1) % GROUP
    for start in range(0, width_x + SUB, SUB):
        low = zero
        high = zero
        for f in range(8):
            values = tails[f] if start == width_x else s_ref[f, pl.ds(start, SUB)]
            mask = lane // 2 == f
            low = jnp.where(mask, turn(values, 2 * f - GROUP // 2, 1), low)
            high = jnp.where(mask, turn(values, 2 * f - (GROUP // 2 - 2), 1), high)
        a_ref[pl.ds(start, SUB)] = jnp.where(even_y, high, low)
        b_ref[pl.ds(start, SUB)] = jnp.where(even_y, low, high)


def transform(adj_ref, fwd_ref, s_ref, g_ref):
    rows = 2 * SUB

    def body(k, _):
        here = pl.ds(pl.multiple_of(k * rows, rows), rows)
        total = None
        for c in range(3):
            for p in range(PLANES):
                parts = [None] * STEPS
                for f in range(FREQ):
                    real = fwd_ref[f, 0, c, p, here].astype(F32)
                    imag = fwd_ref[f, 1, c, p, here].astype(F32)
                    term = real * adj_ref[f, 0, c, p, here] - imag * adj_ref[f, 1, c, p, here]
                    total = term if total is None else total + term
                    for n in range(STEPS):
                        angle = (0.21 + 0.06 * f) * (n + 1)
                        term = (dft_weight * math.cos(angle)) * real + (
                            dft_weight * math.sin(angle)
                        ) * imag
                        parts[n] = term if parts[n] is None else parts[n] + term
                for n in range(STEPS):
                    g_ref[n, c, p, here] = parts[n]
        s_ref[here] = total
        return 0

    lax.fori_loop(0, s_ref.shape[0] // rows, body, 0)


LO = ZLO - STEPS
HI = ZLO + PLANES + STEPS - 1


def update_mag(e, e_up, h, out, damp, ch):
    width_x, width_y = damp.shape
    for start in range(0, width_x, SUB):
        here = pl.ds(start, SUB)

        def ahead(c, tile):
            if start + SUB < width_x:
                return e(c)[pl.ds(start + 1, SUB)]
            return turn(tile, SUB - 1, 0)

        ex, ey, ez = (e(c)[here] for c in range(3))
        up_x = e_up(0)[here] - ex if e_up else -ex
        up_y = e_up(1)[here] - ey if e_up else -ey
        cx = (turn(ez, width_y - 1, 1) - ez) - up_y
        cy = up_x - (ahead(2, ez) - ez)
        cz = (ahead(1, ey) - ey) - (turn(ex, width_y - 1, 1) - ex)
        dm, cf = damp[here], ch[here]
        for c, curl in enumerate((cx, cy, cz)):
            out(c)[here] = dm * h(c)[here] - cf * curl


def update_elec(h, h_down, e, out, damp, ce):
    width_x, width_y = damp.shape
    for start in range(0, width_x, SUB):
        here = pl.ds(start, SUB)

        def behind(c, tile):
            return h(c)[pl.ds(start - 1, SUB)] if start else turn(tile, 1, 0)

        hx, hy, hz = (h(c)[here] for c in range(3))
        up_x = hx - h_down(0)[here] if h_down else hx
        up_y = hy - h_down(1)[here] if h_down else hy
        cx = (hz - turn(hz, 1, 1)) - up_y
        cy = up_x - (hz - behind(2, hz))
        cz = (hy - behind(1, hy)) - (hx - turn(hx, 1, 1))
        dm, cf = damp[here], ce[here]
        for c, curl in enumerate((cx, cy, cz)):
            out(c)[here] = dm * e(c)[here] + cf * curl


def at(ref, z):
    return lambda c: ref.at[c, z]


def fill_ce(ce, k, z, m_ref, choices, ch):
    for start in range(0, ch.shape[0], SUB):
        here = pl.ds(start, SUB)
        ce[k, here] = pick(m_ref[z, here], choices) * (ch[here] * (1.0 / courant))


def interior_first(e_ref, h_ref, m_ref, d_ref, table, em, hm, e1_ref, sl_ref, damp, ch, ce):
    planes_z, width_x, width_y = m_ref.shape
    gx, gy = lax.axis_index("gx"), lax.axis_index("gy")
    total_x, total_y = width_x * lax.axis_size("gx"), width_y * lax.axis_size("gy")
    shape = (width_x, width_y)
    rows = (iota(shape, 0) + gx * width_x).astype(F32)
    cols = (iota(shape, 1) + gy * width_y).astype(F32)
    damping, coef_h, inverse = edge_coefs(rows, cols, total_x, total_y)
    damp[...] = damping
    ch[...] = coef_h
    design, slope = design_terms(blur(d_ref[...]))
    sl_ref[...] = slope
    choices = table_inverse(table, SUB, width_y)
    for z in range(LO, HI):
        if in_design(z):
            ce[z - LO] = design * inverse
        elif z > LO:
            fill_ce(ce, z - LO, z, m_ref, choices, ch)

    def e(z):
        return at(em, z - LO)

    def h(z):
        return at(hm, z - LO)

    for z in range(LO, HI):
        update_mag(at(e_ref, z), at(e_ref, z + 1), at(h_ref, z), h(z), damp, ch)
    for z in range(LO + 1, HI):
        update_elec(h(z), h(z - 1), at(e_ref, z), e(z), damp, ce.at[z - LO])
    for c in range(3):
        for p in range(PLANES):
            e1_ref[c, p] = em[c, ZLO + p - LO]
    for z in range(LO + 1, HI - 1):
        update_mag(e(z), e(z + 1), h(z), h(z), damp, ch)
    for z in range(LO + 2, HI - 1):
        update_elec(h(z), h(z - 1), e(z), e(z), damp, ce.at[z - LO])


def interior_rest(e_ref, h_ref, m_ref, table, em, hm, damp, ch, ce, e2, h2, done, ce2):
    planes_z, width_x, width_y = m_ref.shape
    choices = table_inverse(table, SUB, width_y)
    done[...] = jnp.zeros(done.shape, F32)
    rest = [z for z in range(planes_z) if not LO < z < HI]
    for z in rest:
        fill_ce(ce2, z, z, m_ref, choices, ch)

    def coef(z):
        return ce.at[z - LO] if LO < z < HI else ce2.at[z]

    def e1(z):
        return at(em, z - LO) if LO < z < HI else at(e2, z)

    def h1(z):
        return at(hm, z - LO) if LO <= z < HI else at(h2, z)

    def h_last(z):
        return at(hm, z - LO) if LO < z < HI - 1 else at(h2, z)

    for z in range(planes_z):
        if not LO <= z < HI:
            up = at(e_ref, z + 1) if z + 1 < planes_z else None
            update_mag(at(e_ref, z), up, at(h_ref, z), at(h2, z), damp, ch)
    for z in rest:
        update_elec(h1(z), h1(z - 1) if z else None, at(e_ref, z), at(e2, z), damp, coef(z))
    for z in range(planes_z):
        if not LO < z < HI - 1:
            up = e1(z + 1) if z + 1 < planes_z else None
            update_mag(e1(z), up, h1(z), at(h2, z), damp, ch)
    for z in range(planes_z):
        if not in_design(z):
            down = h_last(z - 1) if z else None
            update_elec(h_last(z), down, e1(z), at(e2, z), damp, coef(z))


def strips_x(
    e_ref, h_ref, m_ref, d_ref, table, xa_ref, xb_ref,
    e2_ref, h2_ref, e1_ref, sl_ref, xe, xh, ce,
):
    planes_z, width_x, width_y = m_ref.shape
    gx, gy = lax.axis_index("gx"), lax.axis_index("gy")
    total_x, total_y = width_x * lax.axis_size("gx"), width_y * lax.axis_size("gy")
    shape = (SUB, width_y)
    sub = iota(shape, 0)
    cols = (iota(shape, 1) + gy * width_y).astype(F32)
    choices = table_inverse(table, SUB, width_y)
    zero = jnp.zeros(shape, F32)
    damps, chs = [], []

    below, above = x_halos(xa_ref, xb_ref)
    edges = pl.ds(0, SUB), pl.ds(width_x - SUB, SUB)

    def place(values, tile, z, at_sub):
        return jnp.where(sub == at_sub, turn(tile, at_sub - z, 0), values)

    def strip(side, own, near, far, z):
        out = turn(own, 2 if side == 0 else 6, 0)
        out = place(out, near, z, 1 if side == 0 else 6)
        if far is None:
            return jnp.where(sub == (0 if side == 0 else 7), 0.0, out)
        return place(out, far[0], far[1], 0 if side == 0 else 7)

    def source(side, z):
        own = d_ref[edges[side]] if in_design(z) else m_ref[z, edges[side]].astype(F32)
        halo = (below, above)[side]
        return strip(side, own, halo[8], (halo[9], 0), z)

    for side in range(2):
        rows = (sub + gx * width_x + (-2 if side == 0 else width_x - 6)).astype(F32)
        inside = within(rows, cols, total_x, total_y)
        damping, coef_h, inverse = edge_coefs(rows, cols, total_x, total_y, inside)
        damps.append(damping)
        chs.append(coef_h)
        for z in range(planes_z):
            for c in range(3):
                halo = (below, above)[side]
                far = (above[5 + c], z) if side and c else None
                xe[side, c, z] = strip(side, e_ref[c, z, edges[side]], halo[c], far, z)
                xh[side, c, z + 1] = strip(side, h_ref[c, z, edges[side]], halo[3 + c], None, z)
        for c in range(3):
            xe[side, c, planes_z] = zero
            xh[side, c, 0] = zero
        design, slope = design_terms(blur(source(side, ZLO)))
        sl_ref[side] = turn(slope, 6 if side == 0 else 2, 0)
        for z in range(planes_z):
            if in_design(z):
                ce[side, z] = design * inverse
            else:
                ce[side, z] = pick(source(side, z), choices) * inverse

    def mag(z):
        for side in range(2):
            ex, ey, ez = (xe[side, c, z] for c in range(3))
            cx = (turn(ez, width_y - 1, 1) - ez) - (xe[side, 1, z + 1] - ey)
            cy = (xe[side, 0, z + 1] - ex) - (turn(ez, SUB - 1, 0) - ez)
            cz = (turn(ey, SUB - 1, 0) - ey) - (turn(ex, width_y - 1, 1) - ex)
            for c, curl in enumerate((cx, cy, cz)):
                xh[side, c, z + 1] = damps[side] * xh[side, c, z + 1] - chs[side] * curl

    def elec(z):
        for side in range(2):
            hx, hy, hz = (xh[side, c, z + 1] for c in range(3))
            cx = (hz - turn(hz, 1, 1)) - (hy - xh[side, 1, z])
            cy = (hx - xh[side, 0, z]) - (hz - turn(hz, 1, 0))
            cz = (hy - turn(hy, 1, 0)) - (hx - turn(hx, 1, 1))
            for c, curl in enumerate((cx, cy, cz)):
                xe[side, c, z] = damps[side] * xe[side, c, z] + ce[side, z] * curl

    def loop(f):
        for z in range(planes_z):
            f(z)

    back = (6, 2)
    for n in range(STEPS):
        loop(mag)
        if n == 0:
            for z in range(planes_z):
                for c in (1, 2):
                    xh[0, c, z + 1] = place(xh[0, c, z + 1], below[5 + c], z, 0)
        loop(elec)
        if n == 0:
            for side in range(2):
                for c in range(3):
                    for p in range(PLANES):
                        e1_ref[c, p, side] = turn(xe[side, c, ZLO + p], back[side], 0)

    def finish(z):
        for side in range(2):
            for c in range(3):
                e2_ref[c, z, side] = turn(xe[side, c, z], back[side], 0)
                h2_ref[c, z, side] = turn(xh[side, c, z + 1], back[side], 0)

    loop(finish)


def patch_rows(values, strip, start, width_x):
    sub = iota(values.shape, 0)
    if start == 0:
        values = jnp.where(sub < 2, strip[0], values)
    if start == width_x - SUB:
        values = jnp.where(sub >= 6, strip[1], values)
    return values


def patch_cols(values, strip, z):
    lane = iota((values.shape[0], LANES), 1)
    rolled = turn(strip, -(z * GROUP + GROUP // 2), 1)
    tiles = [values[:, k : k + LANES] for k in range(0, values.shape[1], LANES)]
    tiles[0] = jnp.where(lane < 2, rolled, tiles[0])
    tiles[-1] = jnp.where(lane >= LANES - 2, rolled, tiles[-1])
    return jnp.concatenate(tiles, axis=1)


def strip_columns(shape):
    lane = iota(shape, 1)
    return lane % GROUP, lane // GROUP


def strip_coefs(width_x, width_y):
    gx, gy = lax.axis_index("gx"), lax.axis_index("gy")
    total_x, total_y = width_x * lax.axis_size("gx"), width_y * lax.axis_size("gy")
    shape = (width_x + SUB, LANES)
    col, _ = strip_columns(shape)
    row = iota(shape, 0)
    row = jnp.where(row >= width_x + 4, row - shape[0], row)
    place = jnp.where(col < GROUP // 2, col + (width_y - GROUP // 2), col - GROUP // 2)
    place = jnp.where(col < 2, col - 2, place)
    place = jnp.where(col >= GROUP - 2, col + (width_y - GROUP + 2), place)
    rows = (row + gx * width_x).astype(F32)
    cols = (place + gy * width_y).astype(F32)
    return edge_coefs(rows, cols, total_x, total_y, within(rows, cols, total_x, total_y))


def design(
    e1_ref, e2_ref, xe1_ref, xe2_ref, sl_ref, xsl_ref, sum_ref, g_ref,
    l_ref, gs_ref, ss_ref, coef_ref,
):
    width_x, width_y = sl_ref.shape
    for k, values in enumerate(strip_coefs(width_x, width_y)):
        coef_ref[k] = values
    group = iota((SUB, LANES), 1) // GROUP
    for start in range(0, width_x, SUB):
        here = pl.ds(start, SUB)
        total = sum_ref[here]
        ss_ref[here] = jnp.where(group == ZLO, turn(ends(total), ZLO * GROUP + GROUP // 2, 1), 0.0)
        for c in range(3):
            strips = [jnp.zeros((SUB, LANES), F32) for _ in range(STEPS)]
            for p in range(PLANES):
                z = ZLO + p
                first = patch_rows(e1_ref[c, p, here], xe1_ref.at[c, p], start, width_x)
                second = patch_rows(e2_ref[c, z - LO, here], xe2_ref.at[c, z], start, width_x)
                weights = [g_ref[n, c, p, here] for n in range(STEPS)]
                total = total + weights[0] * first + weights[1] * second
                for n in range(STEPS):
                    rolled = turn(ends(weights[n]), z * GROUP + GROUP // 2, 1)
                    strips[n] = jnp.where(group == z, rolled, strips[n])
            for n in range(STEPS):
                gs_ref[n, c, here] = strips[n]
        slope = patch_rows(sl_ref[here], xsl_ref, start, width_x)
        l_ref[here] = (grad_scale * (eps_high - eps_low)) * slope * total


def strips_y(s_ref, t_ref, ya_ref, yb_ref, table, coef_ref):
    planes_z = LANES // GROUP
    size = coef_ref.shape[1]
    col, plane = strip_columns((size, LANES))
    from_low, from_high = neighbours("gy", ya_ref[...], yb_ref[...])

    def field(f):
        own = jnp.concatenate([s_ref[f], t_ref[f]], axis=0)
        own = jnp.where(col < 2, turn(from_low, -2 * f, 1), own)
        return jnp.where(col >= GROUP - 2, turn(from_high, GROUP - 2 - 2 * f, 1), own)

    damping, coef_h, inverse = coef_ref[0], coef_ref[1], coef_ref[2]
    source = field(6)
    half = GROUP // 2

    def next_col(v):
        jump = (col == 1) | (col == half - 1)
        return jnp.where(jump, turn(v, 1 - half, 1), turn(v, -1, 1))

    def prev_col(v):
        jump = (col == half) | (col == GROUP - 2)
        return jnp.where(jump, turn(v, half - 1, 1), turn(v, 1, 1))

    filtered = turn(source, 1, 0) + 2.0 * source + turn(source, size - 1, 0)
    filtered = (prev_col(filtered) + 2.0 * filtered + next_col(filtered)) / 16.0
    design, slope = design_terms(filtered)
    choices = table_inverse(table, size, LANES)
    layer = (plane >= ZLO) & (plane < ZLO + PLANES)
    coef_e = jnp.where(layer, design, pick(source, choices)) * inverse
    e = [field(c) for c in range(3)]
    h = [field(3 + c) for c in range(3)]
    top = plane == planes_z - 1
    bottom = plane == 0

    def dxf(v):
        return turn(v, size - 1, 0) - v

    def dyf(v):
        return next_col(v) - v

    def dzf(v):
        return jnp.where(top, 0.0, turn(v, LANES - GROUP, 1)) - v

    def dxb(v):
        return v - turn(v, 1, 0)

    def dyb(v):
        return v - prev_col(v)

    def dzb(v):
        return v - jnp.where(bottom, 0.0, turn(v, GROUP, 1))

    steps = []
    for _ in range(STEPS):
        curl = (dyf(e[2]) - dzf(e[1]), dzf(e[0]) - dxf(e[2]), dxf(e[1]) - dyf(e[0]))
        h = [damping * v - coef_h * c for v, c in zip(h, curl)]
        curl = (dyb(h[2]) - dzb(h[1]), dzb(h[0]) - dxb(h[2]), dxb(h[1]) - dyb(h[0]))
        e = [damping * v + coef_e * c for v, c in zip(e, curl)]
        steps.append(e)
    return steps, h, slope


def slot_of(param, rows_mine):
    gx, gy = lax.axis_index("gx"), lax.axis_index("gy")
    count_gx, count_gy = lax.axis_size("gx"), lax.axis_size("gy")
    owner = lax.div(param, jnp.int32(rows_mine))
    row = param - owner * rows_mine
    ox = lax.div(owner, jnp.int32(count_gy))
    oy = owner - ox * count_gy
    core = (oy ^ gy) & 1
    near = ((ox & 1) + 2 * (oy >> 1)) ^ ((gx & 1) + 2 * (gy >> 1))
    far = (ox >> 1) ^ (gx >> 1)
    return ((core * count_gy + near) * (count_gx // 2) + far) * rows_mine + row


def gradient(
    s_ref, t_ref, yb_ref, ya_ref, xa_ref, xb_ref, table, own_ref, l_ref, gs_ref, ss_ref, coef_ref,
    buf_ref, ye_ref, yh_ref, lpad, vpad, gpad,
):
    width_x, width_y = l_ref.shape
    tiles_x, tiles_y = width_x // TILE, width_y // TILE

    def scalar(row, lane):
        here = iota(row.shape, 1) == lane
        return jnp.max(jnp.where(here, row, 0.0)).astype(jnp.int32)

    id_x, id_y, own = {}, {}, {}
    for tx in range(tiles_x):
        for t in range(tiles_y):
            u = t * TILE // LANES * LANES
            row = own_ref[pl.ds(tx * SUB, 1), pl.ds(u, LANES)]
            own[tx, t] = scalar(row, t * TILE - u) - 1
    for k, tile in enumerate(neighbours("gx", xa_ref[TILES - 1], xb_ref[TILES - 1])):
        for t in range(tiles_y):
            u = t * TILE // LANES * LANES
            id_x[k, t] = scalar(tile[1:2, u : u + LANES], t * TILE - u)
    for row in [tx * TILE for tx in range(tiles_x)] + [width_x, width_x + SUB - 1]:
        first = row // SUB * SUB
        here = pl.ds(first, SUB)
        for k, tile in enumerate(neighbours("gy", ya_ref[here], yb_ref[here])):
            id_y[k, row] = scalar(tile[row - first : row - first + 1], GROUP - 1 - k)
    steps, h, slope_y = strips_y(s_ref, t_ref, ya_ref, yb_ref, table, coef_ref)
    for c in range(3):
        ye_ref[c] = steps[-1][c]
        yh_ref[c] = h[c]
    pad = 2 * SUB
    lpad[pl.ds(0, pad)] = jnp.zeros((pad, width_y), F32)
    lpad[pl.ds(pad + width_x, pad)] = jnp.zeros((pad, width_y), F32)
    buf_ref[...] = jnp.zeros(buf_ref.shape, F32)
    for start in range(0, width_x, SUB):
        here, rows = pl.ds(start, SUB), slice(start, start + SUB)
        total = ss_ref[here]
        for c in range(3):
            for n in range(STEPS):
                total = total + gs_ref[n, c, here] * steps[n][c][rows]
        total = sum((turn(total, -p * GROUP, 1) for p in range(1, PLANES)), total)
        total = (grad_scale * (eps_high - eps_low)) * slope_y[rows] * total
        lpad[pl.ds(pad + start, SUB)] = patch_cols(l_ref[here], total, ZLO)
    lane = iota((SUB, width_y), 1)
    for start in range(SUB, pad + width_x + SUB, SUB):
        v = lpad[pl.ds(start - 1, SUB)] + 2.0 * lpad[pl.ds(start, SUB)] + lpad[pl.ds(start + 1, SUB)]
        v = v / 16.0
        left = jnp.where(lane == 0, 0.0, turn(v, 1, 1))
        right = jnp.where(lane == width_y - 1, 0.0, turn(v, width_y - 1, 1))
        g = left + 2.0 * v + right
        for u in range(width_y // LANES):
            vpad[u, pl.ds(start, SUB)] = v[:, u * LANES : (u + 1) * LANES]
            gpad[u, pl.ds(start, SUB)] = g[:, u * LANES : (u + 1) * LANES]

    half = LANES // 2
    lines = TILE // 2
    devices = lax.axis_size("gx") * lax.axis_size("gy")
    rows_mine = buf_ref.shape[0] // devices
    lane = iota((lines, LANES), 1)
    lane8 = iota((SUB, LANES), 1)
    sub8 = iota((SUB, LANES), 0)

    def add_tile(param, values):
        slot = slot_of(param, rows_mine)
        buf_ref[slot] = buf_ref[slot] + values

    def add_rows(ident, start, values):
        slot = slot_of(jnp.maximum(ident - 1, 0), rows_mine)
        rows = pl.ds(start, SUB)
        buf_ref[slot, rows] = buf_ref[slot, rows] + jnp.where(ident > 0, values, 0.0)

    for tx in range(tiles_x):
        for u in range(width_y // LANES):
            even = gpad[u, pl.ds(pad + tx * TILE, lines, stride=2)]
            odd = gpad[u, pl.ds(pad + tx * TILE + 1, lines, stride=2)]
            add_tile(own[tx, 2 * u], jnp.where(lane < half, even, turn(odd, half, 1)))
            add_tile(own[tx, 2 * u + 1], jnp.where(lane < half, turn(even, half, 1), odd))
    before, after = pl.ds(pad - SUB, SUB), pl.ds(pad + width_x, SUB)
    for t in range(tiles_y):
        u, odd = divmod(t, 2)
        top, low = gpad[u, before], gpad[u, after]
        top = top if odd else turn(top, half, 1)
        low = turn(low, half, 1) if odd else low
        keep = (sub8 == SUB - 1) & (lane8 >= half)
        add_rows(id_x[0, t], lines - SUB, jnp.where(keep, top, 0.0))
        keep = (sub8 == 0) & (lane8 < half)
        add_rows(id_x[1, t], 0, jnp.where(keep, low, 0.0))
    end = width_y // LANES - 1
    for tx in range(tiles_x):
        even, odd = (pl.ds(pad + tx * TILE + k, lines, stride=2) for k in (0, 1))
        left = jnp.where(lane == half - 1, turn(vpad[0, even], half - 1, 1), 0.0)
        left = jnp.where(lane == LANES - 1, turn(vpad[0, odd], LANES - 1, 1), left)
        right = jnp.where(lane == 0, turn(vpad[end, even], 1, 1), 0.0)
        right = jnp.where(lane == half, turn(vpad[end, odd], half + 1, 1), right)
        for ahead, values in ((False, left), (True, right)):
            owner = id_y[ahead, tx * TILE]
            add_tile(jnp.maximum(owner - 1, 0), jnp.where(owner > 0, values, 0.0))
    tail = width_x + SUB - 1
    corners = (
        (SUB - 1, False, tail, before, lines - SUB, LANES - 1),
        (SUB - 1, True, tail, before, lines - SUB, half),
        (0, False, width_x, after, 0, half - 1),
        (0, True, width_x, after, 0, 0),
    )
    for sub, ahead, row, rows, start, target in corners:
        keep = (sub8 == sub) & (lane8 == target)
        values = vpad[end, rows] if ahead else vpad[0, rows]
        values = turn(values, target - (LANES - 1 if ahead else 0), 1)
        add_rows(id_y[ahead, row], start, jnp.where(keep, values, 0.0))


def merge(e_ref, h_ref, em, hm, xe_ref, xh_ref, ye_ref, yh_ref, eo_ref, ho_ref, out, sems):
    _, planes_z, width_x, _ = e_ref.shape
    parts = (
        (e_ref, em, xe_ref, ye_ref, eo_ref, LO + 2, HI - 1),
        (h_ref, hm, xh_ref, yh_ref, ho_ref, LO + 1, HI - 1),
    )
    half = planes_z // 2

    def send(n, c, k):
        rows = pl.ds(k * half, half)
        return pltpu.make_async_copy(out.at[n, c, rows], parts[n][4].at[c, rows], sems.at[n, c, k])

    def body(c, _):
        for n, (rest, mid, xs, ys, _, low, high) in enumerate(parts):
            for z in range(planes_z):
                src = mid.at[c, z - LO] if low <= z < high else rest.at[c, z]
                for start in range(0, width_x, SUB):
                    here = pl.ds(start, SUB)
                    values = patch_rows(src[here], xs.at[c, z], start, width_x)
                    out[n, c, z, here] = patch_cols(values, ys[c, here], z)
                if z % half == half - 1:
                    send(n, c, z // half).start()
        return 0

    lax.fori_loop(0, 3, body, 0)
    for n in range(2):
        for c in range(3):
            for k in range(2):
                send(n, c, k).wait()


def first_sum(parts, buf_ref, got_ref, *outs):
    size = outs[0].shape[0]
    for k in range(parts):
        rows = pl.ds(k * size, size)
        outs[k][...] = buf_ref[rows] + got_ref[rows]


def rounds(count):
    if count == 4:
        return [(0, 1, 2, 3), (1, 3, 0, 2), (3, 2, 1, 0), (2, 0, 3, 1)]
    return [tuple(k ^ n for k in range(count)) for n in range(count)]


def second_sum(parts, rows_mine, *refs):
    ins, outs = refs[:parts], refs[parts + 1 :]
    here = lax.axis_index("gx") >> 1
    for out, targets in zip(outs, rounds(len(outs))):
        slot = sum(jnp.where(here == k, k ^ to, 0) for k, to in enumerate(targets))
        rows = pl.ds(slot * rows_mine, rows_mine)
        out[...] = sum(ref[rows] for ref in ins[1:]) + ins[0][rows]


def pair(block, partner, spare=None):
    count_gx, count_gy = lax.axis_size("gx"), lax.axis_size("gy")
    route = []
    for i in range(count_gx):
        for j in range(count_gy):
            a, b = partner(i, j)
            if not (0 <= a < count_gx and 0 <= b < count_gy):
                a, b = spare(i, j)
            route.append((i * count_gy + j, a * count_gy + b))
    return lax.ppermute(block, ("gx", "gy"), route)


def after(k):
    return ((k + 1) ^ 1) - 1


def on_device(e_adj, h_adj, density, material, eps_table, dft_adj, dft_fwd, tile_map):
    planes_z, width_x, width_y = material.shape
    count_gx, count_gy = lax.axis_size("gx"), lax.axis_size("gy")
    assert planes_z == SUB
    face = struct(TILES, SUB, width_y)
    xa, xb, own_ids, table = pl.pallas_call(
        pack_x,
        out_shape=(
            pltpu.VMEM(face.shape, F32),
            pltpu.VMEM(face.shape, F32),
            pltpu.VMEM((width_x // TILE * SUB, width_y), F32),
            pltpu.VMEM((eps_table.shape[0] * SUB, LANES), F32),
        ),
        in_specs=[HBM] * 6,
        out_specs=(VMEM,) * 4,
        scratch_shapes=[
            pltpu.VMEM((width_y // LANES, 3 * planes_z * 2 * SUB, LANES), F32),
            pltpu.VMEM((width_y // LANES, 3 * planes_z * 2 * SUB, LANES), F32),
            pltpu.VMEM((width_y // LANES, planes_z * 2 * SUB, LANES), jnp.int32),
            pltpu.VMEM((2 * SUB, width_y), F32),
            pltpu.SMEM(tile_map.shape, jnp.int32),
            pltpu.SMEM(eps_table.shape, F32),
            pltpu.SemaphoreType.DMA((6 * width_y // LANES + 4,)),
        ],
        compiler_params=params(),
        name="pack_x",
    )(
        *(
            pltpu.with_memory_space_constraint(x, pltpu.HBM)
            for x in (e_adj, h_adj, material, density, tile_map, eps_table)
        )
    )
    xa = pair(xa, lambda i, j: (i ^ 1, j))
    xb = pair(xb, lambda i, j: (after(i), j), lambda i, j: (i, j ^ 1))
    strip = pl.pallas_call(
        build_strips,
        out_shape=struct(8, width_x, LANES),
        in_specs=[VMEM] * 5,
        out_specs=VMEM,
        compiler_params=params(),
        cost_estimate=cost(1, 1),
        name="build_strips",
    )(e_adj, h_adj, material, density, own_ids)

    base, weight = pl.pallas_call(
        transform,
        out_shape=(
            struct(width_x, width_y),
            struct(STEPS, 3, PLANES, width_x, width_y),
        ),
        in_specs=[VMEM] * 2,
        out_specs=(VMEM,) * 2,
        compiler_params=params(),
        cost_estimate=cost(1, 1),
        name="transform",
    )(dft_adj, dft_fwd)
    plane = struct(width_x, width_y)
    middle = struct(3, HI - LO, width_x, width_y)
    full = struct(3, planes_z, width_x, width_y)
    em, hm, e1, slope, damp, ch, ce = pl.pallas_call(
        interior_first,
        out_shape=(middle, middle, struct(3, PLANES, width_x, width_y))
        + (plane,) * 3
        + (struct(HI - LO, width_x, width_y),),
        in_specs=[VMEM] * 5,
        out_specs=(VMEM,) * 7,
        compiler_params=params(),
        cost_estimate=cost(1, 1),
        name="interior_first",
    )(e_adj, h_adj, material, density, table)
    e2, h2, done = pl.pallas_call(
        interior_rest,
        out_shape=(full, full, struct(SUB, LANES)),
        in_specs=[VMEM] * 9,
        out_specs=(VMEM,) * 3,
        scratch_shapes=[pltpu.VMEM((planes_z, width_x, width_y), F32)],
        compiler_params=params(),
        cost_estimate=cost(1, 1),
        name="interior_rest",
    )(e_adj, h_adj, material, table, em, hm, damp, ch, ce)

    tails, ya, yb = pl.pallas_call(
        pack_y,
        out_shape=(struct(8, SUB, LANES),) + (struct(width_x + SUB, LANES),) * 2,
        in_specs=[VMEM] * 3 + [ANY],
        out_specs=(VMEM,) * 3,
        compiler_params=params(),
        name="pack_y",
    )(strip, xa, xb, slope)
    yb = pair(yb, lambda i, j: (i, after(j)), lambda i, j: (i ^ 1, j))
    ya = pair(ya, lambda i, j: (i, j ^ 1))
    xe2, xh2, xe1, xslope = pl.pallas_call(
        strips_x,
        out_shape=(
            struct(3, planes_z, 2, SUB, width_y),
            struct(3, planes_z, 2, SUB, width_y),
            struct(3, PLANES, 2, SUB, width_y),
            struct(2, SUB, width_y),
        ),
        in_specs=[VMEM] * 7,
        out_specs=(VMEM,) * 4,
        scratch_shapes=[
            pltpu.VMEM((2, 3, planes_z + 1, SUB, width_y), F32),
            pltpu.VMEM((2, 3, planes_z + 1, SUB, width_y), F32),
            pltpu.VMEM((2, planes_z, SUB, width_y), F32),
        ],
        compiler_params=params(),
        cost_estimate=cost(1, 1),
        name="strips_x",
    )(e_adj, h_adj, material, density, table, xa, xb)

    devices = count_gx * count_gy
    rows_mine = (width_x // TILE) * (width_y // TILE) // REPEAT
    lines = TILE // 2
    padded = width_x + 4 * SUB
    local, weight_y, base_y, coef_y = pl.pallas_call(
        design,
        out_shape=(
            plane,
            struct(STEPS, 3, width_x, LANES),
            struct(width_x, LANES),
            struct(3, width_x + SUB, LANES),
        ),
        in_specs=[VMEM] * 8,
        out_specs=(VMEM,) * 4,
        compiler_params=params(),
        cost_estimate=cost(1, 1),
        name="design",
    )(e1, em, xe1, xe2, slope, xslope, base, weight)
    buf, ye2, yh2 = pl.pallas_call(
        gradient,
        out_shape=(struct(devices * rows_mine, lines, LANES),)
        + (struct(3, width_x + SUB, LANES),) * 2,
        in_specs=[VMEM] * 12,
        out_specs=(VMEM,) * 3,
        scratch_shapes=[
            pltpu.VMEM((padded, width_y), F32),
            pltpu.VMEM((width_y // LANES, padded, LANES), F32),
            pltpu.VMEM((width_y // LANES, padded, LANES), F32),
        ],
        compiler_params=params(),
        cost_estimate=cost(1, 1),
        name="gradient",
    )(strip, tails, yb, ya, xa, xb, table, own_ids, local, weight_y, base_y, coef_y)

    half = devices * rows_mine // 2
    far = count_gx // 2
    got = pair(buf[half:], lambda i, j: (i, j ^ 1))
    parts = pl.pallas_call(
        lambda *refs: first_sum(count_gy, *refs),
        out_shape=(struct(far * rows_mine, lines, LANES),) * count_gy,
        in_specs=[VMEM] * 2,
        out_specs=(VMEM,) * count_gy,
        compiler_params=params(),
        name="first_sum",
    )(buf, got)
    parts = [parts[0]] + [
        pair(parts[k], lambda i, j: (i ^ (k & 1), j ^ (k >> 1 << 1))) for k in range(count_gy - 1, 0, -1)
    ]
    e_out, h_out = pl.pallas_call(
        merge,
        out_shape=(full,) * 2,
        in_specs=[VMEM] * 8,
        out_specs=(HBM,) * 2,
        scratch_shapes=[
            pltpu.VMEM((2, 3, planes_z, width_x, width_y), F32),
            pltpu.SemaphoreType.DMA((2, 3, 2)),
        ],
        compiler_params=params(),
        cost_estimate=cost(1, 1),
        name="merge",
    )(e2, h2, em, hm, xe2, xh2, ye2, yh2)
    parts = pl.pallas_call(
        lambda *refs: second_sum(count_gy, rows_mine, *refs),
        out_shape=(struct(rows_mine, lines, LANES),) * far,
        in_specs=[VMEM] * count_gy + [ANY],
        out_specs=(VMEM,) * far,
        compiler_params=params(),
        name="second_sum",
    )(*parts, done)
    parts = [parts[0]] + [
        pair(part, lambda i, j: (2 * targets[i >> 1] + i % 2, j))
        for part, targets in zip(parts[1:], rounds(far)[1:])
    ]
    param_grad = sum(parts[1:], parts[0]).reshape(rows_mine, TILE * TILE)

    return e_out, h_out, param_grad


def solution(mesh):
    in_specs = (
        P(None, None, "gx", "gy"),
        P(None, None, "gx", "gy"),
        P("gx", "gy"),
        P(None, "gx", "gy"),
        P(),
        P(None, None, None, None, "gx", "gy"),
        P(None, None, None, None, "gx", "gy"),
        P("gx", "gy"),
    )
    out_specs = (P(None, None, "gx", "gy"), P(None, None, "gx", "gy"), P(("gx", "gy"), None))
    return jax.shard_map(
        on_device, mesh=mesh, in_specs=in_specs, out_specs=out_specs, check_vma=False
    )
```

```python
import math

import jax
import jax.numpy as jnp
from jax import lax
from jax.experimental import pallas as pl
from jax.experimental.pallas import tpu as pltpu
from jax.sharding import PartitionSpec as P

PLANES = 2
ZLO = 3
STEPS = 2
FREQ = 4
PML = 12
TILE = 64
REPEAT = 4

courant = 0.5
sigma_peak = 0.8
dft_weight = 0.5
sharpness = 4.0
threshold = 0.5
eps_low = 2.1
eps_high = 12.1
grad_scale = 0.01

F32 = jnp.float32
LANES = 128
SUB = 8
GROUP = 16
ANY = pl.BlockSpec(memory_space=pl.ANY)
HBM = pl.BlockSpec(memory_space=pltpu.HBM)
VMEM = pl.BlockSpec(memory_space=pltpu.VMEM)
SMEM = pl.BlockSpec(memory_space=pltpu.SMEM)


def params(size=40 * 2**20):
    return pltpu.CompilerParams(vmem_limit_bytes=size)


def struct(*shape, dtype=F32):
    return jax.ShapeDtypeStruct(shape, dtype)


def cost(flops, moved):
    return pl.CostEstimate(flops=int(flops), bytes_accessed=int(moved), transcendentals=0)


def iota(shape, dim):
    return lax.broadcasted_iota(jnp.int32, shape, dim)


def in_design(z):
    return ZLO <= z < ZLO + PLANES


def turn(values, shift, axis):
    size = values.shape[axis]
    shift %= size
    return values if shift == 0 else pltpu.roll(values, shift, axis)


def depth_cubed(places, total):
    depth = jnp.maximum(jnp.maximum(PML - places, places - (total - 1 - PML)), 0.0) / PML
    return depth * depth * depth


def edge_coefs(rows, cols, total_x, total_y, inside=None):
    sigma = sigma_peak * (depth_cubed(rows, total_x) + depth_cubed(cols, total_y))
    inverse = 1.0 / (1.0 + 0.5 * sigma)
    if inside is not None:
        inverse = jnp.where(inside, inverse, 0.0)
    return (1.0 - 0.5 * sigma) * inverse, courant * inverse, inverse


def within(rows, cols, total_x, total_y):
    return (rows >= 0) & (rows < total_x) & (cols >= 0) & (cols < total_y)


def table_inverse(table, rows, cols):
    tiles = [table[k * SUB : (k + 1) * SUB] for k in range(table.shape[0] // SUB)]
    return [jnp.tile(tile, (rows // SUB, cols // LANES)) for tile in tiles]


def pick(index, choices):
    out = jnp.zeros_like(choices[0])
    for k, choice in enumerate(choices):
        out = jnp.where(index == k, choice, out)
    return out


def design_terms(filtered):
    high = math.tanh(sharpness * threshold)
    norm = high + math.tanh(sharpness * (1.0 - threshold))
    bend = jnp.tanh(sharpness * (filtered - threshold))
    eps = eps_low + (eps_high - eps_low) * ((high + bend) / norm)
    return courant / eps, sharpness * (1.0 - bend * bend) / norm


def blur(values):
    rows, cols = values.shape
    summed = turn(values, 1, 0) + 2.0 * values + turn(values, rows - 1, 0)
    return (turn(summed, 1, 1) + 2.0 * summed + turn(summed, cols - 1, 1)) / 16.0


def id_row(tile_map, tx, shape):
    lane = iota(shape, len(shape) - 1)
    out = jnp.zeros(shape, F32)
    for t in range(tile_map.shape[1]):
        out = jnp.where(lane // TILE == t, (tile_map[tx, t] + 1).astype(F32), out)
    return out


TILES = 10
BEHIND = (0, 1, 2, 4, 5)


def pack_x(
    e_in, h_in, m_in, d_in, map_in, table_in,
    a_ref, b_ref, id_ref, inverse_ref, eb, hb, mb, db, map_ref, table_ref, sems,
):
    planes_z, size, width_y = m_in.shape
    span = 2 * SUB
    tiles = width_y // LANES
    views = [
        (e_in, eb.reshape(tiles, 3, planes_z, span, LANES)),
        (h_in, hb.reshape(tiles, 3, planes_z, span, LANES)),
        (m_in, mb.reshape(tiles, planes_z, span, LANES)),
    ]
    copies = [], [], []
    count = 0

    def fetch(n, source, target):
        nonlocal count
        copies[n].append(pltpu.make_async_copy(source, target, sems.at[count]))
        copies[n][-1].start()
        count += 1

    for n, (src, dst) in enumerate(views):
        for k, start in enumerate((0, size - SUB)):
            here, there = pl.ds(start, SUB), pl.ds(k * SUB, SUB)
            for u in range(tiles):
                lanes = pl.ds(u * LANES, LANES)
                if n == 2:
                    fetch(n, src.at[:, here, lanes], dst.at[u, :, there])
                    continue
                for c in range(3):
                    fetch(n, src.at[c, :, here, lanes], dst.at[u, c, :, there])
            if n == 2:
                fetch(n, d_in.at[here], db.at[there])
    fetch(2, map_in, map_ref)
    fetch(2, table_in, table_ref)
    gx, gy = lax.axis_index("gx"), lax.axis_index("gy")
    total_x, total_y = size * lax.axis_size("gx"), width_y * lax.axis_size("gy")
    shape = (SUB, width_y)
    sub = iota(shape, 0)
    rows = jnp.full(shape, (gx + 1) * size - 2, jnp.int32).astype(F32)
    cols = (iota(shape, 1) + gy * width_y).astype(F32)
    damping, coef_h, _ = edge_coefs(rows, cols, total_x, total_y)
    layer = (sub >= ZLO) & (sub < ZLO + PLANES)

    def wait(n):
        for copy in copies[n]:
            copy.wait()

    def row(ref, c, r):
        rows = pl.ds(c * planes_z * span + r, planes_z, stride=span)
        return jnp.concatenate([ref[u, rows] for u in range(tiles)], axis=1)

    near, far = span - 1, span - 2
    wait(0)
    ex, ey, ez = (row(eb, c, far) for c in range(3))
    up = jnp.where(sub == SUB - 1, 0.0, turn(ex, SUB - 1, 0))
    curl_y = (up - ex) - (row(eb, 2, near) - ez)
    curl_z = (row(eb, 1, near) - ey) - (turn(ex, width_y - 1, 1) - ex)
    high = [row(eb, c, near) for c in range(3)]
    low = [row(eb, c, 0) for c in range(3)]
    beyond = [row(eb, 1, 1), row(eb, 2, 1)]
    strips = [row_to_strip(v) for v in (ex, ey, ez)]
    wait(1)
    mag = [row(hb, c, far) for c in (1, 2)]
    strips += [row_to_strip(v) for v in mag]
    high += [row(hb, c, near) for c in range(3)]
    high += [damping * h - coef_h * curl for h, curl in zip(mag, (curl_y, curl_z))]
    low += [row(hb, c, 0) for c in range(3)] + beyond
    wait(2)
    for side, edge, further, tx in ((low, 0, 1, 0), (high, near, far, map_ref.shape[0] - 1)):
        density = jnp.broadcast_to(db[edge : edge + 1], shape)
        side.append(jnp.where(layer, density, row(mb, 0, edge).astype(F32)))
        misc = jnp.broadcast_to(db[further : further + 1], shape)
        side.append(jnp.where(sub == 1, id_row(map_ref, tx, shape), misc))
    strips.append(strips[-1])
    for k in range(3):
        pair_of = jnp.concatenate([strips[2 * k], strips[2 * k + 1]], axis=1)
        high[-1] = jnp.where(sub == 2 + k, jnp.broadcast_to(pair_of, shape), high[-1])
    even = gx % 2 == 0
    for k in range(TILES):
        a_ref[k] = jnp.where(even, high[k], low[k])
        b_ref[k] = jnp.where(even, low[k], high[k])
    for tx in range(map_ref.shape[0]):
        id_ref[pl.ds(tx * SUB, SUB)] = id_row(map_ref, tx, shape)
    for k in range(table_ref.shape[0]):
        inverse_ref[pl.ds(k * SUB, SUB)] = courant / jnp.full((SUB, LANES), table_ref[k], F32)


def neighbours(axis, from_a, from_b):
    here = lax.axis_index(axis)
    even = here % 2 == 0
    before = jnp.where(here > 0, jnp.where(even, from_b, from_a), 0.0)
    after = jnp.where(here < lax.axis_size(axis) - 1, jnp.where(even, from_a, from_b), 0.0)
    return before, after


def x_halos(xa_ref, xb_ref):
    both = [neighbours("gx", xa_ref[k], xb_ref[k]) for k in range(TILES)]
    return [t[0] for t in both], [t[1] for t in both]


def ends(values):
    lane = iota((values.shape[0], LANES), 1)
    return jnp.where(lane < LANES // 2, values[:, :LANES], values[:, -LANES:])


def row_to_strip(values):
    shape = (SUB, LANES)
    rolled = pltpu.roll(ends(values), GROUP // 2, 1, stride=GROUP, stride_axis=0)
    rolled = jnp.where(iota(shape, 1) // GROUP == iota(shape, 0), rolled, 0.0)
    return jnp.sum(rolled, axis=0, keepdims=True)


def build_strips(e_ref, h_ref, m_ref, d_ref, id_ref, s_ref):
    planes_z, width_x, width_y = m_ref.shape
    group = iota((SUB, LANES), 1) // GROUP

    def gather(get, here):
        acc = jnp.zeros((SUB, LANES), F32)
        for z in range(planes_z):
            acc = jnp.where(group == z, turn(ends(get(z, here)), z * GROUP + GROUP // 2, 1), acc)
        return acc

    def body(c, _):
        for base, ref in ((0, e_ref), (3, h_ref)):
            for start in range(0, width_x, SUB):
                here = pl.ds(start, SUB)
                s_ref[base + c, here] = gather(lambda z, here: ref[c, z, here], here)
        return 0

    lax.fori_loop(0, 3, body, 0)

    def source(z, here):
        return d_ref[here] if in_design(z) else m_ref[z, here].astype(F32)

    for start in range(0, width_x, SUB):
        here = pl.ds(start, SUB)
        s_ref[6, here] = gather(source, here)
        row = id_ref[pl.ds(start // TILE * SUB, SUB)]
        s_ref[7, here] = turn(ends(row), GROUP // 2, 1)


def pack_y(s_ref, xa_ref, xb_ref, _after, t_ref, a_ref, b_ref):
    width_x = s_ref.shape[1]
    even_y = lax.axis_index("gy") % 2 == 0
    below, above = x_halos(xa_ref, xb_ref)
    shape = (SUB, LANES)
    sub = iota(shape, 0)

    def row(tile, k):
        return jnp.broadcast_to(tile[k : k + 1], tile.shape)

    def wide(values):
        return jnp.broadcast_to(values, shape)

    zero = jnp.zeros(shape, F32)
    tails = []
    for f in range(8):
        if f < 7:
            k = 8 if f == 6 else f
            after_1, before_1 = (wide(row_to_strip(side[k])) for side in (above, below))
        else:
            after_1, before_1 = (wide(row_to_strip(row(side[9], 1))) for side in (above, below))
        after_2, before_2 = zero, zero
        if f in (1, 2):
            after_2 = wide(row_to_strip(above[5 + f]))
        if f in BEHIND:
            k = BEHIND.index(f)
            lanes = (k % 2) * LANES
            before_2 = wide(below[9][2 + k // 2 : 3 + k // 2, lanes : lanes + LANES])
        if f == 6:
            after_2, before_2 = (wide(row_to_strip(row(side[9], 0))) for side in (above, below))
        tail = jnp.where(sub == 0, after_1, jnp.where(sub == 1, after_2, 0.0))
        tail = jnp.where(sub == 6, before_2, jnp.where(sub == 7, before_1, tail))
        t_ref[f] = tail
        tails.append(tail)
    lane = iota(shape, 1) % GROUP
    for start in range(0, width_x + SUB, SUB):
        low = zero
        high = zero
        for f in range(8):
            values = tails[f] if start == width_x else s_ref[f, pl.ds(start, SUB)]
            mask = lane // 2 == f
            low = jnp.where(mask, turn(values, 2 * f - GROUP // 2, 1), low)
            high = jnp.where(mask, turn(values, 2 * f - (GROUP // 2 - 2), 1), high)
        a_ref[pl.ds(start, SUB)] = jnp.where(even_y, high, low)
        b_ref[pl.ds(start, SUB)] = jnp.where(even_y, low, high)


def transform(adj_ref, fwd_ref, s_ref, g_ref):
    rows = 2 * SUB

    def body(k, _):
        here = pl.ds(pl.multiple_of(k * rows, rows), rows)
        total = None
        for c in range(3):
            for p in range(PLANES):
                parts = [None] * STEPS
                for f in range(FREQ):
                    real = fwd_ref[f, 0, c, p, here].astype(F32)
                    imag = fwd_ref[f, 1, c, p, here].astype(F32)
                    term = real * adj_ref[f, 0, c, p, here] - imag * adj_ref[f, 1, c, p, here]
                    total = term if total is None else total + term
                    for n in range(STEPS):
                        angle = (0.21 + 0.06 * f) * (n + 1)
                        term = (dft_weight * math.cos(angle)) * real + (
                            dft_weight * math.sin(angle)
                        ) * imag
                        parts[n] = term if parts[n] is None else parts[n] + term
                for n in range(STEPS):
                    g_ref[n, c, p, here] = parts[n]
        s_ref[here] = total
        return 0

    lax.fori_loop(0, s_ref.shape[0] // rows, body, 0)


LO = ZLO - STEPS
HI = ZLO + PLANES + STEPS - 1


def update_mag(e, e_up, h, out, damp, ch):
    width_x, width_y = damp.shape
    for start in range(0, width_x, SUB):
        here = pl.ds(start, SUB)

        def ahead(c, tile):
            if start + SUB < width_x:
                return e(c)[pl.ds(start + 1, SUB)]
            return turn(tile, SUB - 1, 0)

        ex, ey, ez = (e(c)[here] for c in range(3))
        up_x = e_up(0)[here] - ex if e_up else -ex
        up_y = e_up(1)[here] - ey if e_up else -ey
        cx = (turn(ez, width_y - 1, 1) - ez) - up_y
        cy = up_x - (ahead(2, ez) - ez)
        cz = (ahead(1, ey) - ey) - (turn(ex, width_y - 1, 1) - ex)
        dm, cf = damp[here], ch[here]
        for c, curl in enumerate((cx, cy, cz)):
            out(c)[here] = dm * h(c)[here] - cf * curl


def update_elec(h, h_down, e, out, damp, ce):
    width_x, width_y = damp.shape
    for start in range(0, width_x, SUB):
        here = pl.ds(start, SUB)

        def behind(c, tile):
            return h(c)[pl.ds(start - 1, SUB)] if start else turn(tile, 1, 0)

        hx, hy, hz = (h(c)[here] for c in range(3))
        up_x = hx - h_down(0)[here] if h_down else hx
        up_y = hy - h_down(1)[here] if h_down else hy
        cx = (hz - turn(hz, 1, 1)) - up_y
        cy = up_x - (hz - behind(2, hz))
        cz = (hy - behind(1, hy)) - (hx - turn(hx, 1, 1))
        dm, cf = damp[here], ce[here]
        for c, curl in enumerate((cx, cy, cz)):
            out(c)[here] = dm * e(c)[here] + cf * curl


def at(ref, z):
    return lambda c: ref.at[c, z]


def fill_ce(ce, k, z, m_ref, choices, ch):
    for start in range(0, ch.shape[0], SUB):
        here = pl.ds(start, SUB)
        ce[k, here] = pick(m_ref[z, here], choices) * (ch[here] * (1.0 / courant))


def interior_first(e_ref, h_ref, m_ref, d_ref, table, em, hm, e1_ref, sl_ref, damp, ch, ce):
    planes_z, width_x, width_y = m_ref.shape
    gx, gy = lax.axis_index("gx"), lax.axis_index("gy")
    total_x, total_y = width_x * lax.axis_size("gx"), width_y * lax.axis_size("gy")
    shape = (width_x, width_y)
    rows = (iota(shape, 0) + gx * width_x).astype(F32)
    cols = (iota(shape, 1) + gy * width_y).astype(F32)
    damping, coef_h, inverse = edge_coefs(rows, cols, total_x, total_y)
    damp[...] = damping
    ch[...] = coef_h
    design, slope = design_terms(blur(d_ref[...]))
    sl_ref[...] = slope
    choices = table_inverse(table, SUB, width_y)
    for z in range(LO, HI):
        if in_design(z):
            ce[z - LO] = design * inverse
        elif z > LO:
            fill_ce(ce, z - LO, z, m_ref, choices, ch)

    def e(z):
        return at(em, z - LO)

    def h(z):
        return at(hm, z - LO)

    for z in range(LO, HI):
        update_mag(at(e_ref, z), at(e_ref, z + 1), at(h_ref, z), h(z), damp, ch)
    for z in range(LO + 1, HI):
        update_elec(h(z), h(z - 1), at(e_ref, z), e(z), damp, ce.at[z - LO])
    for c in range(3):
        for p in range(PLANES):
            e1_ref[c, p] = em[c, ZLO + p - LO]
    for z in range(LO + 1, HI - 1):
        update_mag(e(z), e(z + 1), h(z), h(z), damp, ch)
    for z in range(LO + 2, HI - 1):
        update_elec(h(z), h(z - 1), e(z), e(z), damp, ce.at[z - LO])


def interior_rest(e_ref, h_ref, m_ref, table, em, hm, damp, ch, ce, e2, h2, done, ce2):
    planes_z, width_x, width_y = m_ref.shape
    choices = table_inverse(table, SUB, width_y)
    done[...] = jnp.zeros(done.shape, F32)
    rest = [z for z in range(planes_z) if not LO < z < HI]
    for z in rest:
        fill_ce(ce2, z, z, m_ref, choices, ch)

    def coef(z):
        return ce.at[z - LO] if LO < z < HI else ce2.at[z]

    def e1(z):
        return at(em, z - LO) if LO < z < HI else at(e2, z)

    def h1(z):
        return at(hm, z - LO) if LO <= z < HI else at(h2, z)

    def h_last(z):
        return at(hm, z - LO) if LO < z < HI - 1 else at(h2, z)

    for z in range(planes_z):
        if not LO <= z < HI:
            up = at(e_ref, z + 1) if z + 1 < planes_z else None
            update_mag(at(e_ref, z), up, at(h_ref, z), at(h2, z), damp, ch)
    for z in rest:
        update_elec(h1(z), h1(z - 1) if z else None, at(e_ref, z), at(e2, z), damp, coef(z))
    for z in range(planes_z):
        if not LO < z < HI - 1:
            up = e1(z + 1) if z + 1 < planes_z else None
            update_mag(e1(z), up, h1(z), at(h2, z), damp, ch)
    for z in range(planes_z):
        if not in_design(z):
            down = h_last(z - 1) if z else None
            update_elec(h_last(z), down, e1(z), at(e2, z), damp, coef(z))


def strips_x(
    e_ref, h_ref, m_ref, d_ref, table, xa_ref, xb_ref,
    e2_ref, h2_ref, e1_ref, sl_ref, xe, xh, ce,
):
    planes_z, width_x, width_y = m_ref.shape
    gx, gy = lax.axis_index("gx"), lax.axis_index("gy")
    total_x, total_y = width_x * lax.axis_size("gx"), width_y * lax.axis_size("gy")
    shape = (SUB, width_y)
    sub = iota(shape, 0)
    cols = (iota(shape, 1) + gy * width_y).astype(F32)
    choices = table_inverse(table, SUB, width_y)
    zero = jnp.zeros(shape, F32)
    damps, chs = [], []

    below, above = x_halos(xa_ref, xb_ref)
    edges = pl.ds(0, SUB), pl.ds(width_x - SUB, SUB)

    def place(values, tile, z, at_sub):
        return jnp.where(sub == at_sub, turn(tile, at_sub - z, 0), values)

    def strip(side, own, near, far, z):
        out = turn(own, 2 if side == 0 else 6, 0)
        out = place(out, near, z, 1 if side == 0 else 6)
        if far is None:
            return jnp.where(sub == (0 if side == 0 else 7), 0.0, out)
        return place(out, far[0], far[1], 0 if side == 0 else 7)

    def source(side, z):
        own = d_ref[edges[side]] if in_design(z) else m_ref[z, edges[side]].astype(F32)
        halo = (below, above)[side]
        return strip(side, own, halo[8], (halo[9], 0), z)

    for side in range(2):
        rows = (sub + gx * width_x + (-2 if side == 0 else width_x - 6)).astype(F32)
        inside = within(rows, cols, total_x, total_y)
        damping, coef_h, inverse = edge_coefs(rows, cols, total_x, total_y, inside)
        damps.append(damping)
        chs.append(coef_h)
        for z in range(planes_z):
            for c in range(3):
                halo = (below, above)[side]
                far = (above[5 + c], z) if side and c else None
                xe[side, c, z] = strip(side, e_ref[c, z, edges[side]], halo[c], far, z)
                xh[side, c, z + 1] = strip(side, h_ref[c, z, edges[side]], halo[3 + c], None, z)
        for c in range(3):
            xe[side, c, planes_z] = zero
            xh[side, c, 0] = zero
        design, slope = design_terms(blur(source(side, ZLO)))
        sl_ref[side] = turn(slope, 6 if side == 0 else 2, 0)
        for z in range(planes_z):
            if in_design(z):
                ce[side, z] = design * inverse
            else:
                ce[side, z] = pick(source(side, z), choices) * inverse

    def mag(z):
        for side in range(2):
            ex, ey, ez = (xe[side, c, z] for c in range(3))
            cx = (turn(ez, width_y - 1, 1) - ez) - (xe[side, 1, z + 1] - ey)
            cy = (xe[side, 0, z + 1] - ex) - (turn(ez, SUB - 1, 0) - ez)
            cz = (turn(ey, SUB - 1, 0) - ey) - (turn(ex, width_y - 1, 1) - ex)
            for c, curl in enumerate((cx, cy, cz)):
                xh[side, c, z + 1] = damps[side] * xh[side, c, z + 1] - chs[side] * curl

    def elec(z):
        for side in range(2):
            hx, hy, hz = (xh[side, c, z + 1] for c in range(3))
            cx = (hz - turn(hz, 1, 1)) - (hy - xh[side, 1, z])
            cy = (hx - xh[side, 0, z]) - (hz - turn(hz, 1, 0))
            cz = (hy - turn(hy, 1, 0)) - (hx - turn(hx, 1, 1))
            for c, curl in enumerate((cx, cy, cz)):
                xe[side, c, z] = damps[side] * xe[side, c, z] + ce[side, z] * curl

    def loop(f):
        for z in range(planes_z):
            f(z)

    back = (6, 2)
    for n in range(STEPS):
        loop(mag)
        if n == 0:
            for z in range(planes_z):
                for c in (1, 2):
                    xh[0, c, z + 1] = place(xh[0, c, z + 1], below[5 + c], z, 0)
        loop(elec)
        if n == 0:
            for side in range(2):
                for c in range(3):
                    for p in range(PLANES):
                        e1_ref[c, p, side] = turn(xe[side, c, ZLO + p], back[side], 0)

    def finish(z):
        for side in range(2):
            for c in range(3):
                e2_ref[c, z, side] = turn(xe[side, c, z], back[side], 0)
                h2_ref[c, z, side] = turn(xh[side, c, z + 1], back[side], 0)

    loop(finish)


def patch_rows(values, strip, start, width_x):
    sub = iota(values.shape, 0)
    if start == 0:
        values = jnp.where(sub < 2, strip[0], values)
    if start == width_x - SUB:
        values = jnp.where(sub >= 6, strip[1], values)
    return values


def patch_cols(values, strip, z):
    lane = iota((values.shape[0], LANES), 1)
    rolled = turn(strip, -(z * GROUP + GROUP // 2), 1)
    tiles = [values[:, k : k + LANES] for k in range(0, values.shape[1], LANES)]
    tiles[0] = jnp.where(lane < 2, rolled, tiles[0])
    tiles[-1] = jnp.where(lane >= LANES - 2, rolled, tiles[-1])
    return jnp.concatenate(tiles, axis=1)


def strip_columns(shape):
    lane = iota(shape, 1)
    return lane % GROUP, lane // GROUP


def strip_coefs(width_x, width_y):
    gx, gy = lax.axis_index("gx"), lax.axis_index("gy")
    total_x, total_y = width_x * lax.axis_size("gx"), width_y * lax.axis_size("gy")
    shape = (width_x + SUB, LANES)
    col, _ = strip_columns(shape)
    row = iota(shape, 0)
    row = jnp.where(row >= width_x + 4, row - shape[0], row)
    place = jnp.where(col < GROUP // 2, col + (width_y - GROUP // 2), col - GROUP // 2)
    place = jnp.where(col < 2, col - 2, place)
    place = jnp.where(col >= GROUP - 2, col + (width_y - GROUP + 2), place)
    rows = (row + gx * width_x).astype(F32)
    cols = (place + gy * width_y).astype(F32)
    return edge_coefs(rows, cols, total_x, total_y, within(rows, cols, total_x, total_y))


def design(
    e1_ref, e2_ref, xe1_ref, xe2_ref, sl_ref, xsl_ref, sum_ref, g_ref,
    l_ref, gs_ref, ss_ref, coef_ref,
):
    width_x, width_y = sl_ref.shape
    for k, values in enumerate(strip_coefs(width_x, width_y)):
        coef_ref[k] = values
    group = iota((SUB, LANES), 1) // GROUP
    for start in range(0, width_x, SUB):
        here = pl.ds(start, SUB)
        total = sum_ref[here]
        ss_ref[here] = jnp.where(group == ZLO, turn(ends(total), ZLO * GROUP + GROUP // 2, 1), 0.0)
        for c in range(3):
            strips = [jnp.zeros((SUB, LANES), F32) for _ in range(STEPS)]
            for p in range(PLANES):
                z = ZLO + p
                first = patch_rows(e1_ref[c, p, here], xe1_ref.at[c, p], start, width_x)
                second = patch_rows(e2_ref[c, z - LO, here], xe2_ref.at[c, z], start, width_x)
                weights = [g_ref[n, c, p, here] for n in range(STEPS)]
                total = total + weights[0] * first + weights[1] * second
                for n in range(STEPS):
                    rolled = turn(ends(weights[n]), z * GROUP + GROUP // 2, 1)
                    strips[n] = jnp.where(group == z, rolled, strips[n])
            for n in range(STEPS):
                gs_ref[n, c, here] = strips[n]
        slope = patch_rows(sl_ref[here], xsl_ref, start, width_x)
        l_ref[here] = (grad_scale * (eps_high - eps_low)) * slope * total


def strips_y(s_ref, t_ref, ya_ref, yb_ref, table, coef_ref):
    planes_z = LANES // GROUP
    size = coef_ref.shape[1]
    col, plane = strip_columns((size, LANES))
    from_low, from_high = neighbours("gy", ya_ref[...], yb_ref[...])

    def field(f):
        own = jnp.concatenate([s_ref[f], t_ref[f]], axis=0)
        own = jnp.where(col < 2, turn(from_low, -2 * f, 1), own)
        return jnp.where(col >= GROUP - 2, turn(from_high, GROUP - 2 - 2 * f, 1), own)

    damping, coef_h, inverse = coef_ref[0], coef_ref[1], coef_ref[2]
    source = field(6)
    half = GROUP // 2

    def next_col(v):
        jump = (col == 1) | (col == half - 1)
        return jnp.where(jump, turn(v, 1 - half, 1), turn(v, -1, 1))

    def prev_col(v):
        jump = (col == half) | (col == GROUP - 2)
        return jnp.where(jump, turn(v, half - 1, 1), turn(v, 1, 1))

    filtered = turn(source, 1, 0) + 2.0 * source + turn(source, size - 1, 0)
    filtered = (prev_col(filtered) + 2.0 * filtered + next_col(filtered)) / 16.0
    design, slope = design_terms(filtered)
    choices = table_inverse(table, size, LANES)
    layer = (plane >= ZLO) & (plane < ZLO + PLANES)
    coef_e = jnp.where(layer, design, pick(source, choices)) * inverse
    e = [field(c) for c in range(3)]
    h = [field(3 + c) for c in range(3)]
    top = plane == planes_z - 1
    bottom = plane == 0

    def dxf(v):
        return turn(v, size - 1, 0) - v

    def dyf(v):
        return next_col(v) - v

    def dzf(v):
        return jnp.where(top, 0.0, turn(v, LANES - GROUP, 1)) - v

    def dxb(v):
        return v - turn(v, 1, 0)

    def dyb(v):
        return v - prev_col(v)

    def dzb(v):
        return v - jnp.where(bottom, 0.0, turn(v, GROUP, 1))

    steps = []
    for _ in range(STEPS):
        curl = (dyf(e[2]) - dzf(e[1]), dzf(e[0]) - dxf(e[2]), dxf(e[1]) - dyf(e[0]))
        h = [damping * v - coef_h * c for v, c in zip(h, curl)]
        curl = (dyb(h[2]) - dzb(h[1]), dzb(h[0]) - dxb(h[2]), dxb(h[1]) - dyb(h[0]))
        e = [damping * v + coef_e * c for v, c in zip(e, curl)]
        steps.append(e)
    return steps, h, slope


def slot_of(param, rows_mine):
    gx, gy = lax.axis_index("gx"), lax.axis_index("gy")
    count_gx, count_gy = lax.axis_size("gx"), lax.axis_size("gy")
    owner = lax.div(param, jnp.int32(rows_mine))
    row = param - owner * rows_mine
    ox = lax.div(owner, jnp.int32(count_gy))
    oy = owner - ox * count_gy
    core = (oy ^ gy) & 1
    near = ((ox & 1) + 2 * (oy >> 1)) ^ ((gx & 1) + 2 * (gy >> 1))
    far = (ox >> 1) ^ (gx >> 1)
    return ((core * count_gy + near) * (count_gx // 2) + far) * rows_mine + row


def gradient(
    s_ref, t_ref, yb_ref, ya_ref, xa_ref, xb_ref, table, own_ref, l_ref, gs_ref, ss_ref, coef_ref,
    buf_ref, ye_ref, yh_ref, lpad, vpad, gpad,
):
    width_x, width_y = l_ref.shape
    tiles_x, tiles_y = width_x // TILE, width_y // TILE

    def scalar(row, lane):
        here = iota(row.shape, 1) == lane
        return jnp.max(jnp.where(here, row, 0.0)).astype(jnp.int32)

    id_x, id_y, own = {}, {}, {}
    for tx in range(tiles_x):
        for t in range(tiles_y):
            u = t * TILE // LANES * LANES
            row = own_ref[pl.ds(tx * SUB, 1), pl.ds(u, LANES)]
            own[tx, t] = scalar(row, t * TILE - u) - 1
    for k, tile in enumerate(neighbours("gx", xa_ref[TILES - 1], xb_ref[TILES - 1])):
        for t in range(tiles_y):
            u = t * TILE // LANES * LANES
            id_x[k, t] = scalar(tile[1:2, u : u + LANES], t * TILE - u)
    for row in [tx * TILE for tx in range(tiles_x)] + [width_x, width_x + SUB - 1]:
        first = row // SUB * SUB
        here = pl.ds(first, SUB)
        for k, tile in enumerate(neighbours("gy", ya_ref[here], yb_ref[here])):
            id_y[k, row] = scalar(tile[row - first : row - first + 1], GROUP - 1 - k)
    steps, h, slope_y = strips_y(s_ref, t_ref, ya_ref, yb_ref, table, coef_ref)
    for c in range(3):
        ye_ref[c] = steps[-1][c]
        yh_ref[c] = h[c]
    pad = 2 * SUB
    lpad[pl.ds(0, pad)] = jnp.zeros((pad, width_y), F32)
    lpad[pl.ds(pad + width_x, pad)] = jnp.zeros((pad, width_y), F32)
    buf_ref[...] = jnp.zeros(buf_ref.shape, F32)
    for start in range(0, width_x, SUB):
        here, rows = pl.ds(start, SUB), slice(start, start + SUB)
        total = ss_ref[here]
        for c in range(3):
            for n in range(STEPS):
                total = total + gs_ref[n, c, here] * steps[n][c][rows]
        total = sum((turn(total, -p * GROUP, 1) for p in range(1, PLANES)), total)
        total = (grad_scale * (eps_high - eps_low)) * slope_y[rows] * total
        lpad[pl.ds(pad + start, SUB)] = patch_cols(l_ref[here], total, ZLO)
    lane = iota((SUB, width_y), 1)
    for start in range(SUB, pad + width_x + SUB, SUB):
        v = lpad[pl.ds(start - 1, SUB)] + 2.0 * lpad[pl.ds(start, SUB)] + lpad[pl.ds(start + 1, SUB)]
        v = v / 16.0
        left = jnp.where(lane == 0, 0.0, turn(v, 1, 1))
        right = jnp.where(lane == width_y - 1, 0.0, turn(v, width_y - 1, 1))
        g = left + 2.0 * v + right
        for u in range(width_y // LANES):
            vpad[u, pl.ds(start, SUB)] = v[:, u * LANES : (u + 1) * LANES]
            gpad[u, pl.ds(start, SUB)] = g[:, u * LANES : (u + 1) * LANES]

    half = LANES // 2
    lines = TILE // 2
    devices = lax.axis_size("gx") * lax.axis_size("gy")
    rows_mine = buf_ref.shape[0] // devices
    lane = iota((lines, LANES), 1)
    lane8 = iota((SUB, LANES), 1)
    sub8 = iota((SUB, LANES), 0)

    def add_tile(param, values):
        slot = slot_of(param, rows_mine)
        buf_ref[slot] = buf_ref[slot] + values

    def add_rows(ident, start, values):
        slot = slot_of(jnp.maximum(ident - 1, 0), rows_mine)
        rows = pl.ds(start, SUB)
        buf_ref[slot, rows] = buf_ref[slot, rows] + jnp.where(ident > 0, values, 0.0)

    for tx in range(tiles_x):
        for u in range(width_y // LANES):
            even = gpad[u, pl.ds(pad + tx * TILE, lines, stride=2)]
            odd = gpad[u, pl.ds(pad + tx * TILE + 1, lines, stride=2)]
            add_tile(own[tx, 2 * u], jnp.where(lane < half, even, turn(odd, half, 1)))
            add_tile(own[tx, 2 * u + 1], jnp.where(lane < half, turn(even, half, 1), odd))
    before, after = pl.ds(pad - SUB, SUB), pl.ds(pad + width_x, SUB)
    for t in range(tiles_y):
        u, odd = divmod(t, 2)
        top, low = gpad[u, before], gpad[u, after]
        top = top if odd else turn(top, half, 1)
        low = turn(low, half, 1) if odd else low
        keep = (sub8 == SUB - 1) & (lane8 >= half)
        add_rows(id_x[0, t], lines - SUB, jnp.where(keep, top, 0.0))
        keep = (sub8 == 0) & (lane8 < half)
        add_rows(id_x[1, t], 0, jnp.where(keep, low, 0.0))
    end = width_y // LANES - 1
    for tx in range(tiles_x):
        even, odd = (pl.ds(pad + tx * TILE + k, lines, stride=2) for k in (0, 1))
        left = jnp.where(lane == half - 1, turn(vpad[0, even], half - 1, 1), 0.0)
        left = jnp.where(lane == LANES - 1, turn(vpad[0, odd], LANES - 1, 1), left)
        right = jnp.where(lane == 0, turn(vpad[end, even], 1, 1), 0.0)
        right = jnp.where(lane == half, turn(vpad[end, odd], half + 1, 1), right)
        for ahead, values in ((False, left), (True, right)):
            owner = id_y[ahead, tx * TILE]
            add_tile(jnp.maximum(owner - 1, 0), jnp.where(owner > 0, values, 0.0))
    tail = width_x + SUB - 1
    corners = (
        (SUB - 1, False, tail, before, lines - SUB, LANES - 1),
        (SUB - 1, True, tail, before, lines - SUB, half),
        (0, False, width_x, after, 0, half - 1),
        (0, True, width_x, after, 0, 0),
    )
    for sub, ahead, row, rows, start, target in corners:
        keep = (sub8 == sub) & (lane8 == target)
        values = vpad[end, rows] if ahead else vpad[0, rows]
        values = turn(values, target - (LANES - 1 if ahead else 0), 1)
        add_rows(id_y[ahead, row], start, jnp.where(keep, values, 0.0))


def merge(e_ref, h_ref, em, hm, xe_ref, xh_ref, ye_ref, yh_ref, eo_ref, ho_ref, out, sems):
    _, planes_z, width_x, _ = e_ref.shape
    parts = (
        (e_ref, em, xe_ref, ye_ref, eo_ref, LO + 2, HI - 1),
        (h_ref, hm, xh_ref, yh_ref, ho_ref, LO + 1, HI - 1),
    )
    half = planes_z // 2

    def send(n, c, k):
        rows = pl.ds(k * half, half)
        return pltpu.make_async_copy(out.at[n, c, rows], parts[n][4].at[c, rows], sems.at[n, c, k])

    def body(c, _):
        for n, (rest, mid, xs, ys, _, low, high) in enumerate(parts):
            for z in range(planes_z):
                src = mid.at[c, z - LO] if low <= z < high else rest.at[c, z]
                for start in range(0, width_x, SUB):
                    here = pl.ds(start, SUB)
                    values = patch_rows(src[here], xs.at[c, z], start, width_x)
                    out[n, c, z, here] = patch_cols(values, ys[c, here], z)
                if z % half == half - 1:
                    send(n, c, z // half).start()
        return 0

    lax.fori_loop(0, 3, body, 0)
    for n in range(2):
        for c in range(3):
            for k in range(2):
                send(n, c, k).wait()


def first_sum(parts, buf_ref, got_ref, *outs):
    size = outs[0].shape[0]
    for k in range(parts):
        rows = pl.ds(k * size, size)
        outs[k][...] = buf_ref[rows] + got_ref[rows]


def rounds(count):
    if count == 4:
        return [(0, 1, 2, 3), (1, 3, 0, 2), (3, 2, 1, 0), (2, 0, 3, 1)]
    return [tuple(k ^ n for k in range(count)) for n in range(count)]


def second_sum(parts, rows_mine, *refs):
    ins, outs = refs[:parts], refs[parts + 1 :]
    here = lax.axis_index("gx") >> 1
    for out, targets in zip(outs, rounds(len(outs))):
        slot = sum(jnp.where(here == k, k ^ to, 0) for k, to in enumerate(targets))
        rows = pl.ds(slot * rows_mine, rows_mine)
        out[...] = sum(ref[rows] for ref in ins[1:]) + ins[0][rows]


def pair(block, partner, spare=None):
    count_gx, count_gy = lax.axis_size("gx"), lax.axis_size("gy")
    route = []
    for i in range(count_gx):
        for j in range(count_gy):
            a, b = partner(i, j)
            if not (0 <= a < count_gx and 0 <= b < count_gy):
                a, b = spare(i, j)
            route.append((i * count_gy + j, a * count_gy + b))
    return lax.ppermute(block, ("gx", "gy"), route)


def after(k):
    return ((k + 1) ^ 1) - 1


def on_device(e_adj, h_adj, density, material, eps_table, dft_adj, dft_fwd, tile_map):
    planes_z, width_x, width_y = material.shape
    count_gx, count_gy = lax.axis_size("gx"), lax.axis_size("gy")
    assert planes_z == SUB
    face = struct(TILES, SUB, width_y)
    xa, xb, own_ids, table = pl.pallas_call(
        pack_x,
        out_shape=(
            pltpu.VMEM(face.shape, F32),
            pltpu.VMEM(face.shape, F32),
            pltpu.VMEM((width_x // TILE * SUB, width_y), F32),
            pltpu.VMEM((eps_table.shape[0] * SUB, LANES), F32),
        ),
        in_specs=[HBM] * 6,
        out_specs=(VMEM,) * 4,
        scratch_shapes=[
            pltpu.VMEM((width_y // LANES, 3 * planes_z * 2 * SUB, LANES), F32),
            pltpu.VMEM((width_y // LANES, 3 * planes_z * 2 * SUB, LANES), F32),
            pltpu.VMEM((width_y // LANES, planes_z * 2 * SUB, LANES), jnp.int32),
            pltpu.VMEM((2 * SUB, width_y), F32),
            pltpu.SMEM(tile_map.shape, jnp.int32),
            pltpu.SMEM(eps_table.shape, F32),
            pltpu.SemaphoreType.DMA((14 * width_y // LANES + 4,)),
        ],
        compiler_params=params(),
        name="pack_x",
    )(
        *(
            pltpu.with_memory_space_constraint(x, pltpu.HBM)
            for x in (e_adj, h_adj, material, density, tile_map, eps_table)
        )
    )
    xa = pair(xa, lambda i, j: (i ^ 1, j))
    xb = pair(xb, lambda i, j: (after(i), j), lambda i, j: (i, j ^ 1))
    strip = pl.pallas_call(
        build_strips,
        out_shape=struct(8, width_x, LANES),
        in_specs=[VMEM] * 5,
        out_specs=VMEM,
        compiler_params=params(),
        cost_estimate=cost(1, 1),
        name="build_strips",
    )(e_adj, h_adj, material, density, own_ids)

    base, weight = pl.pallas_call(
        transform,
        out_shape=(
            struct(width_x, width_y),
            struct(STEPS, 3, PLANES, width_x, width_y),
        ),
        in_specs=[VMEM] * 2,
        out_specs=(VMEM,) * 2,
        compiler_params=params(),
        cost_estimate=cost(1, 1),
        name="transform",
    )(dft_adj, dft_fwd)
    plane = struct(width_x, width_y)
    middle = struct(3, HI - LO, width_x, width_y)
    full = struct(3, planes_z, width_x, width_y)
    em, hm, e1, slope, damp, ch, ce = pl.pallas_call(
        interior_first,
        out_shape=(middle, middle, struct(3, PLANES, width_x, width_y))
        + (plane,) * 3
        + (struct(HI - LO, width_x, width_y),),
        in_specs=[VMEM] * 5,
        out_specs=(VMEM,) * 7,
        compiler_params=params(),
        cost_estimate=cost(1, 1),
        name="interior_first",
    )(e_adj, h_adj, material, density, table)
    e2, h2, done = pl.pallas_call(
        interior_rest,
        out_shape=(full, full, struct(SUB, LANES)),
        in_specs=[VMEM] * 9,
        out_specs=(VMEM,) * 3,
        scratch_shapes=[pltpu.VMEM((planes_z, width_x, width_y), F32)],
        compiler_params=params(),
        cost_estimate=cost(1, 1),
        name="interior_rest",
    )(e_adj, h_adj, material, table, em, hm, damp, ch, ce)

    tails, ya, yb = pl.pallas_call(
        pack_y,
        out_shape=(struct(8, SUB, LANES),) + (struct(width_x + SUB, LANES),) * 2,
        in_specs=[VMEM] * 3 + [ANY],
        out_specs=(VMEM,) * 3,
        compiler_params=params(),
        name="pack_y",
    )(strip, xa, xb, slope)
    yb = pair(yb, lambda i, j: (i, after(j)), lambda i, j: (i ^ 1, j))
    ya = pair(ya, lambda i, j: (i, j ^ 1))
    xe2, xh2, xe1, xslope = pl.pallas_call(
        strips_x,
        out_shape=(
            struct(3, planes_z, 2, SUB, width_y),
            struct(3, planes_z, 2, SUB, width_y),
            struct(3, PLANES, 2, SUB, width_y),
            struct(2, SUB, width_y),
        ),
        in_specs=[VMEM] * 7,
        out_specs=(VMEM,) * 4,
        scratch_shapes=[
            pltpu.VMEM((2, 3, planes_z + 1, SUB, width_y), F32),
            pltpu.VMEM((2, 3, planes_z + 1, SUB, width_y), F32),
            pltpu.VMEM((2, planes_z, SUB, width_y), F32),
        ],
        compiler_params=params(),
        cost_estimate=cost(1, 1),
        name="strips_x",
    )(e_adj, h_adj, material, density, table, xa, xb)

    devices = count_gx * count_gy
    rows_mine = (width_x // TILE) * (width_y // TILE) // REPEAT
    lines = TILE // 2
    padded = width_x + 4 * SUB
    local, weight_y, base_y, coef_y = pl.pallas_call(
        design,
        out_shape=(
            plane,
            struct(STEPS, 3, width_x, LANES),
            struct(width_x, LANES),
            struct(3, width_x + SUB, LANES),
        ),
        in_specs=[VMEM] * 8,
        out_specs=(VMEM,) * 4,
        compiler_params=params(),
        cost_estimate=cost(1, 1),
        name="design",
    )(e1, em, xe1, xe2, slope, xslope, base, weight)
    buf, ye2, yh2 = pl.pallas_call(
        gradient,
        out_shape=(struct(devices * rows_mine, lines, LANES),)
        + (struct(3, width_x + SUB, LANES),) * 2,
        in_specs=[VMEM] * 12,
        out_specs=(VMEM,) * 3,
        scratch_shapes=[
            pltpu.VMEM((padded, width_y), F32),
            pltpu.VMEM((width_y // LANES, padded, LANES), F32),
            pltpu.VMEM((width_y // LANES, padded, LANES), F32),
        ],
        compiler_params=params(),
        cost_estimate=cost(1, 1),
        name="gradient",
    )(strip, tails, yb, ya, xa, xb, table, own_ids, local, weight_y, base_y, coef_y)

    half = devices * rows_mine // 2
    far = count_gx // 2
    got = pair(buf[half:], lambda i, j: (i, j ^ 1))
    parts = pl.pallas_call(
        lambda *refs: first_sum(count_gy, *refs),
        out_shape=(struct(far * rows_mine, lines, LANES),) * count_gy,
        in_specs=[VMEM] * 2,
        out_specs=(VMEM,) * count_gy,
        compiler_params=params(),
        name="first_sum",
    )(buf, got)
    parts = [parts[0]] + [
        pair(parts[k], lambda i, j: (i ^ (k & 1), j ^ (k >> 1 << 1))) for k in range(count_gy - 1, 0, -1)
    ]
    e_out, h_out = pl.pallas_call(
        merge,
        out_shape=(full,) * 2,
        in_specs=[VMEM] * 8,
        out_specs=(HBM,) * 2,
        scratch_shapes=[
            pltpu.VMEM((2, 3, planes_z, width_x, width_y), F32),
            pltpu.SemaphoreType.DMA((2, 3, 2)),
        ],
        compiler_params=params(),
        cost_estimate=cost(1, 1),
        name="merge",
    )(e2, h2, em, hm, xe2, xh2, ye2, yh2)
    parts = pl.pallas_call(
        lambda *refs: second_sum(count_gy, rows_mine, *refs),
        out_shape=(struct(rows_mine, lines, LANES),) * far,
        in_specs=[VMEM] * count_gy + [ANY],
        out_specs=(VMEM,) * far,
        compiler_params=params(),
        name="second_sum",
    )(*parts, done)
    parts = [parts[0]] + [
        pair(part, lambda i, j: (2 * targets[i >> 1] + i % 2, j))
        for part, targets in zip(parts[1:], rounds(far)[1:])
    ]
    param_grad = sum(parts[1:], parts[0]).reshape(rows_mine, TILE * TILE)

    return e_out, h_out, param_grad


def solution(mesh):
    in_specs = (
        P(None, None, "gx", "gy"),
        P(None, None, "gx", "gy"),
        P("gx", "gy"),
        P(None, "gx", "gy"),
        P(),
        P(None, None, None, None, "gx", "gy"),
        P(None, None, None, None, "gx", "gy"),
        P("gx", "gy"),
    )
    out_specs = (P(None, None, "gx", "gy"), P(None, None, "gx", "gy"), P(("gx", "gy"), None))
    return jax.shard_map(
        on_device, mesh=mesh, in_specs=in_specs, out_specs=out_specs, check_vma=False
    )
```
